32 devices in a mesh: dp: 32 (over z, y, x, core).
Axes of the slice: x: 2, y: 2, z: 4, core: 2. Of those that a mesh axis runs over, the one named last changes fastest.
Arguments:
- tokens: bfloat16 [256, 128, 768], P('dp'), may hold values from -6 to 6
- segment_ids: int32 [256, 128], P('dp'), may hold values from 0 to 3, never falling along the last dimension, each value on 1 to 64 neighbouring positions
- time_embed: bfloat16 [256, 768], P('dp'), may hold values from -4 to 4
- norm1_gain: bfloat16 [768], P('dp'), may hold values from 0.25 to 1.75
- norm1_shift: bfloat16 [768], P('dp'), may hold values from -2 to 2
- w_qkv: bfloat16 [768, 2304], P('dp'), may hold values from -0.21875 to 0.21875
- b_query: bfloat16 [768], P('dp'), may hold values from -2 to 2
- b_value: bfloat16 [768], P('dp'), may hold values from -2 to 2
- w_proj: bfloat16 [768, 768], P('dp'), may hold values from -1.25 to 1.25
- b_proj: bfloat16 [768], P('dp'), may hold values from -2 to 2
- norm2_gain: bfloat16 [768], P('dp'), may hold values from 0.25 to 1.75
- norm2_shift: bfloat16 [768], P('dp'), may hold values from -2 to 2
- w_fc: bfloat16 [768, 3072], P('dp'), may hold values from -0.21875 to 0.21875
- b_fc: bfloat16 [3072], P('dp'), may hold values from -2 to 2
- w_out: bfloat16 [3072, 768], P('dp'), may hold values from -0.109375 to 0.109375
- b_out: bfloat16 [768], P('dp'), may hold values from -2 to 2
- cotangent: bfloat16 [256, 128, 768], P('dp'), may hold values from -6 to 6
Outputs:
- layer_out: bfloat16 [256, 128, 768], P('dp')
- d_tokens: float32 [256, 128, 768], P('dp')
- d_time: float32 [256, 768], P('dp')
- d_norm1_gain: float32 [768], P('dp')
- d_norm1_shift: float32 [768], P('dp')
- d_w_qkv: float32 [768, 2304], P('dp')
- d_b_query: float32 [768], P('dp')
- d_b_value: float32 [768], P('dp')
- d_w_proj: float32 [768, 768], P('dp')
- d_b_proj: float32 [768], P('dp')
- d_norm2_gain: float32 [768], P('dp')
- d_norm2_shift: float32 [768], P('dp')
- d_w_fc: float32 [768, 3072], P('dp')
- d_b_fc: float32 [3072], P('dp')
- d_w_out: float32 [3072, 768], P('dp')
- d_b_out: float32 [768], P('dp')
The draws below stay inside these ranges and needn't reach their ends.
Inputs may be any that keep to these rules, and one draw needn't show every extreme that they name: `segment_ids`: within a row the ids never fall, and each id covers at most 64 consecutive tokens.
All inputs are finite; a program needn't handle non-finite values.
Results may differ from the reference program's by a relative error of at most 0.012.
Values may be sent and summed in bfloat16 or wider, within the bound.
No kernel may reach another device: no remote copies, remote signals or barrier semaphores. Data moves between devices by JAX's collectives and lax.ppermute only.
A program may use at most 192 MiB of HBM per device.

```python
import math
import jax
import jax.numpy as jnp
import numpy as np
from jax import lax

D = 768
HD = 64
FF = 3072
SEQ = 128
ROWS = 256


def strengthened(array, key, source, target, parts, factor):
    def block_of(axis_at):
        return (jnp.arange(array.shape[axis_at]) // (array.shape[axis_at] // parts)).reshape((-1,) + (1,) * (array.ndim - 1 - axis_at))

    one_side = jax.random.permutation(key, parts)[block_of(target)]
    second = (block_of(target) + parts // 2) % parts
    return jnp.where((block_of(source) == one_side) | (block_of(source) == second), factor * array, array)


def block_levels(rng, shape, pieces, low, largest):
    gain, own = 1.0, jax.random.fold_in(rng, 6)
    for position, blocks in pieces:
        steps = jnp.exp(jax.random.uniform(jax.random.fold_in(own, position), (blocks,), jnp.float32, low / len(pieces), largest / len(pieces)))
        gain = gain * jnp.repeat(steps, shape[position] // blocks).reshape([-1 if axis == position else 1 for axis in range(len(shape))])
    return gain


def split_up(count, total, most, skew):
    weights = [(1 << 20) // math.isqrt(standing ** skew) + 1 for standing in range(2, count + 1)]
    spare, given = total - most - (count - 1), [1] * (count - 1)
    while spare > 0:
        movable = [i for i in range(count - 1) if given[i] < most]
        whole, remaining = sum([weights[i] for i in movable]), spare
        for i in movable:
            addition = min(most - given[i], max(1, remaining * weights[i] // whole), spare)
            given[i] = given[i] + addition
            spare = spare - addition
    return np.array([most] + given)


def uneven_parts(stream_key, number_of, total, bound, lean):
    if number_of == 2:
        one = jax.random.randint(stream_key, (), max(1, total - bound), min(bound, total - 1) + 1)
        return jnp.stack([one, total - one])
    lengths = jnp.asarray(split_up(number_of, total, bound, lean), jnp.int32)
    pairs = (number_of - 1) // 2
    donor, receiver = lengths[1:1 + 2 * pairs:2], lengths[2:2 + 2 * pairs:2]
    slack = jnp.minimum(donor - 1, bound - receiver)
    shifted = jax.random.randint(jax.random.fold_in(stream_key, 1), (pairs,), 0, 1 << 20) % (slack + 1)
    lengths = lengths.at[1:1 + 2 * pairs:2].set(donor - shifted).at[2:2 + 2 * pairs:2].set(receiver + shifted)
    return lengths[jax.random.permutation(jax.random.fold_in(stream_key, 2), number_of)]


def scatter_about(key, shape, scale, limit, shards=(), held_as=jnp.bfloat16):
    drawn = scale * jax.random.normal(key, shape, jnp.float32)
    if shards:
        drawn = drawn * block_levels(key, shape, shards, -0.22, 0.18)
    return jnp.clip(drawn, -limit, limit).astype(held_as)


def gaussian_with(own_key, shape, deviation, bound, shards, heavy, kind=jnp.bfloat16):
    drawn = deviation * jax.random.normal(own_key, shape, jnp.float32)
    if shards:
        drawn = drawn * block_levels(own_key, shape, shards, -0.22, 0.18)
    return jnp.clip(strengthened(drawn, jax.random.fold_in(own_key, 3), *heavy), -bound, bound).astype(kind)


def setup_inputs(seed: int = 0) -> dict:
    key_list = jax.random.split(jax.random.key(seed), 18)
    tokens = scatter_about(key_list[0], (ROWS, SEQ, D), 1.0, 6.0, ((0, 32),))
    segment_ids = jax.vmap(lambda own: jnp.searchsorted(jnp.cumsum(uneven_parts(own, max(SEQ // 32, 4), SEQ, SEQ // 2, 1)), jnp.arange(SEQ), side="right"))(jax.random.split(key_list[1], ROWS)).reshape((ROWS, SEQ)).astype(jnp.int32)
    time_embed = scatter_about(key_list[2], (ROWS, D), 0.5, 4.0, ((0, 32),))
    norm1_gain = jnp.clip(1.0 + 0.15 * jax.random.normal(key_list[3], (D,), jnp.float32), 0.25, 1.75).astype(jnp.bfloat16)
    norm1_shift = scatter_about(key_list[4], (D,), 0.3, 2.0, ((0, 32),))
    w_qkv = scatter_about(key_list[5], (D, 3 * D), D ** -0.5, 0.21875, ((0, 32),))
    b_query = scatter_about(key_list[6], (D,), 0.3, 2.0, ((0, 32),))
    b_value = scatter_about(key_list[7], (D,), 0.3, 2.0, ((0, 32),))
    w_proj = scatter_about(key_list[8], (D, D), (D // 32) ** -0.5, 1.25, ((0, 32),))
    b_proj = scatter_about(key_list[9], (D,), 0.3, 2.0, ((0, 32),))
    norm2_gain = jnp.clip(1.0 + 0.15 * jax.random.normal(key_list[10], (D,), jnp.float32), 0.25, 1.75).astype(jnp.bfloat16)
    norm2_shift = scatter_about(key_list[11], (D,), 0.3, 2.0, ((0, 32),))
    w_fc = scatter_about(key_list[12], (D, FF), D ** -0.5, 0.21875, ((0, 32),))
    b_fc = scatter_about(key_list[13], (FF,), 0.3, 2.0, ((0, 32),))
    w_out = scatter_about(key_list[14], (FF, D), FF ** -0.5, 0.109375, ((0, 32),))
    b_out = scatter_about(key_list[15], (D,), 0.3, 2.0, ((0, 32),))
    cotangent = gaussian_with(key_list[16], (ROWS, SEQ, D), 1.0, 6.0, ((0, 32),), (0, 2, 32, 2.75))
    return {"tokens": tokens, "segment_ids": segment_ids, "time_embed": time_embed, "norm1_gain": norm1_gain, "norm1_shift": norm1_shift, "w_qkv": w_qkv, "b_query": b_query, "b_value": b_value, "w_proj": w_proj, "b_proj": b_proj, "norm2_gain": norm2_gain, "norm2_shift": norm2_shift, "w_fc": w_fc, "b_fc": b_fc, "w_out": w_out, "b_out": b_out, "cotangent": cotangent}


@jax.custom_vjp
def low(v):
    return lax.optimization_barrier(v.astype(jnp.bfloat16)).astype(jnp.float32)

@jax.custom_vjp
def low_back(v):
    return v

def low_keep(v):
    return (low(v), None)

def low_pass(kept, grad):
    return (grad,)

def back_keep(v):
    return (v, None)

def back_low(kept, grad):
    return (low(grad),)
low.defvjp(low_keep, low_pass)
low_back.defvjp(back_keep, back_low)
highest = lax.Precision.HIGHEST
norm_eps = 1e-05
masked_fill = -1e+30

def layer_norm(values, gain_vec, shift_vec):
    center_mean = lax.optimization_barrier(jnp.mean(values, axis=-1, keepdims=True))
    centered = values - center_mean
    spread = lax.optimization_barrier(jnp.mean(centered * centered, axis=-1, keepdims=True))
    return centered * lax.rsqrt(spread + norm_eps) * gain_vec + shift_vec

def forward_layer(params, inputs, times, segments):
    attn_gain, attn_shift, qkv_w, query_bias, value_bias, proj_w, proj_bias, mlp_gain, mlp_shift, fc_w, fc_bias, out_w, out_bias = params
    group_rows, row_len, feat_width = inputs.shape
    head_count = feat_width // HD
    hidden_in = inputs + times[:, None, :]
    normed1 = low(layer_norm(hidden_in, attn_gain, attn_shift))
    qkv_bias = jnp.concatenate([query_bias, jnp.zeros_like(query_bias), value_bias])
    qkv_all = jnp.einsum('rsd,de->rse', normed1, qkv_w, precision=highest) + qkv_bias
    qkv_all = low(low_back(qkv_all)).reshape(group_rows, row_len, 3, head_count, HD)
    queries = qkv_all[:, :, 0]
    key_heads = qkv_all[:, :, 1]
    value_heads = qkv_all[:, :, 2]
    scores = jnp.einsum('rqhe,rkhe->rhqk', queries, key_heads, precision=highest) * HD ** (-0.5)
    scores = low_back(scores)
    same_doc = segments[:, :, None] == segments[:, None, :]
    scores = jnp.where(same_doc[:, None, :, :], scores, masked_fill)
    weights = low(jax.nn.softmax(scores, axis=-1))
    attended = jnp.einsum('rhqk,rkhe->rqhe', weights, value_heads, precision=highest)
    attended = low(low_back(attended.reshape(group_rows, row_len, feat_width)))
    branch = low_back(jnp.einsum('rsd,de->rse', attended, proj_w, precision=highest) + proj_bias)
    hidden = hidden_in + branch
    normed2 = low(layer_norm(hidden, mlp_gain, mlp_shift))
    pre_act = low_back(jnp.einsum('rsd,df->rsf', normed2, fc_w, precision=highest) + fc_bias)
    activated = low(jax.nn.gelu(pre_act, approximate=False))
    return hidden + jnp.einsum('rsf,fd->rsd', activated, out_w, precision=highest) + out_bias

def reference(tokens, segment_ids, time_embed, norm1_gain, norm1_shift, w_qkv, b_query, b_value, w_proj, b_proj, norm2_gain, norm2_shift, w_fc, b_fc, w_out, b_out, cotangent):
    params = tuple((member.astype(jnp.float32) for member in (norm1_gain, norm1_shift, w_qkv, b_query, b_value, w_proj, b_proj, norm2_gain, norm2_shift, w_fc, b_fc, w_out, b_out)))
    row_total, row_len, feat_width = tokens.shape
    group_rows = math.gcd(row_total, 32)
    group_count = row_total // group_rows
    inputs = tokens.astype(jnp.float32).reshape(group_count, group_rows, row_len, feat_width)
    times = time_embed.astype(jnp.float32).reshape(group_count, group_rows, feat_width)
    segments = segment_ids.reshape(group_count, group_rows, row_len)
    cotangents = cotangent.astype(jnp.float32).reshape(group_count, group_rows, row_len, feat_width)

    def group_step(totals, group_data):
        group_in, group_time, group_seg, group_cot = group_data

        def apply_layer(layer_params, layer_in, layer_time):
            return forward_layer(layer_params, layer_in, layer_time, group_seg)
        group_out, pull_back = jax.vjp(apply_layer, params, group_in, group_time)
        param_grads, input_grads, time_grads = pull_back(group_cot)
        totals = tuple((running + addend for running, addend in zip(totals, param_grads)))
        return (totals, (group_out.astype(jnp.bfloat16), input_grads, time_grads))
    zero_sums = tuple((jnp.zeros(member.shape, jnp.float32) for member in params))
    totals, (outputs, input_grads, time_grads) = lax.scan(group_step, zero_sums, (inputs, times, segments, cotangents))
    grad_scale = 1.0 / math.sqrt(row_total * row_len)
    scaled = tuple((member * grad_scale for member in totals))
    return (outputs.reshape(row_total, row_len, feat_width), input_grads.reshape(row_total, row_len, feat_width), time_grads.reshape(row_total, feat_width), scaled[0], scaled[1], scaled[2], scaled[3], scaled[4], scaled[5], scaled[6], scaled[7], scaled[8], scaled[9], scaled[10], scaled[11], scaled[12])
```

```python
import functools
import math

import jax
import jax.numpy as jnp
from jax import lax
from jax.experimental import pallas as pl
from jax.experimental.pallas import tpu as pltpu
from jax.sharding import PartitionSpec as P

HD = 64
EPS = 1e-05
MASKED = -1e30
F32 = jnp.float32
BF16 = jnp.bfloat16
VMEM_LIMIT = 48 * 1024 * 1024


def dot(a, b, a_dim, b_dim):
    return lax.dot_general(a, b, (((a_dim,), (b_dim,)), ((), ())), preferred_element_type=F32)


def normalise(values):
    centered = values - jnp.mean(values, axis=-1, keepdims=True)
    spread = jnp.mean(centered * centered, axis=-1, keepdims=True)
    inv = lax.rsqrt(spread + EPS)
    return centered * inv, inv


def head_pair(block):
    lane = lax.broadcasted_iota(jnp.int32, block.shape, 1)
    zero = jnp.zeros_like(block)
    return jnp.concatenate([jnp.where(lane < HD, block, zero), jnp.where(lane >= HD, block, zero)], axis=0)


def own_lanes(stacked):
    half = stacked.shape[0] // 2
    lane = lax.broadcasted_iota(jnp.int32, (half, stacked.shape[1]), 1)
    return jnp.where(lane < HD, stacked[:half], stacked[half:])


def row_mask(seg_row):
    size = seg_row.shape[1]
    across = jnp.broadcast_to(seg_row.astype(F32), (size, size))
    return jnp.where(across == across.T, 0.0, MASKED)


def colsum(v):
    return jnp.sum(v, axis=0, keepdims=True)


Z, Y, X, CORES = 4, 2, 2, 2
PIECES = Z * Y * X * CORES


def merge_rows(blocks):
    count, rows, width = blocks.shape
    return blocks.astype(F32).reshape(count * rows, width).astype(BF16)


def slots(place, z, y, x):
    ys, xs = y ^ place[1], x ^ place[2]
    first = jnp.where(place[3] == 0, ys, xs)
    second = jnp.where(place[3] == 0, xs, ys)
    return first, second, (place[0] - z + Z) % Z


def put_blocks(place, z, y, x, even, odd, keep, send, tail=()):
    first, second, deep = slots(place, z, y, x)
    mine = place[3] == 0
    keep[(first, second, deep) + tail] = jnp.where(mine, even, odd)
    send[(second, first, deep) + tail] = jnp.where(mine, odd, even)


def attn_forward_body(
    place, tok, time, seg, mine0, mine1, other0, other1, n1, qkv, probs, att, hid, n2, weights, vec, *, rows
):
    size = tok.shape[0] // rows
    width = tok.shape[1]

    @pl.when(pl.program_id(0) == 0)
    def _():
        even = place[3] == 0
        for z in range(Z):
            for y in range(Y):
                for x in range(X):
                    first, second, deep = slots(place, z, y, x)
                    mine = jnp.where(first == 0, mine0[second, deep], mine1[second, deep])
                    other = jnp.where(second == 0, other0[first, deep], other1[first, deep])
                    both = [jnp.where(even, mine, other), jnp.where(even, other, mine)]
                    chip = (z * Y + y) * X + x
                    both = jnp.concatenate([b.astype(F32) for b in both], axis=0)
                    step = both.shape[0]
                    weights[chip * step : (chip + 1) * step, :] = both.astype(BF16)
        vec[...] = weights[:, 4 * width :].astype(F32).T[:16]

    x = tok[...].astype(F32)
    x = jnp.concatenate(
        [x[r * size : (r + 1) * size] + time[r].astype(F32) for r in range(rows)], axis=0
    )
    nhat, _ = normalise(x)
    normed = (nhat * vec[0:1, :] + vec[1:2, :]).astype(BF16)
    n1[...] = normed
    for part in range(3):
        cols = slice(part * width, (part + 1) * width)
        block = dot(normed, weights[:, cols], 1, 0)
        if part == 0:
            block = block + vec[2:3, :]
        if part == 2:
            block = block + vec[3:4, :]
        qkv[:, cols] = block.astype(BF16)
    pairs = width // (2 * HD)
    for r in range(rows):
        sl = slice(r * size, (r + 1) * size)
        mask = row_mask(seg[r])
        for p in range(pairs):
            c = 2 * HD * p
            q = qkv[sl, c : c + 2 * HD] * jnp.asarray(HD**-0.5, BF16)
            k = head_pair(qkv[sl, width + c : width + c + 2 * HD])
            v = head_pair(qkv[sl, 2 * width + c : 2 * width + c + 2 * HD])
            s = dot(q, k, 1, 1)
            halves = []
            for h in range(2):
                sh = s[:, h * size : (h + 1) * size] + mask
                e = jnp.exp(sh - jnp.max(sh, axis=-1, keepdims=True))
                halves.append((e / jnp.sum(e, axis=-1, keepdims=True)).astype(BF16))
            pr = jnp.concatenate(halves, axis=1)
            probs[r, p] = pr
            att[sl, c : c + 2 * HD] = dot(pr, v, 1, 0).astype(BF16)
    hidden = x + dot(att[...], weights[:, 3 * width : 4 * width], 1, 0) + vec[4:5, :]
    hid[...] = hidden
    nhat2, _ = normalise(hidden)
    n2[...] = (nhat2 * vec[5:6, :] + vec[6:7, :]).astype(BF16)


def attn_forward(place, tok, time, seg, gathered, rows=2):
    row_count = seg.shape[0]
    toks, width = tok.shape
    size = toks // row_count
    tm = rows * size
    pairs = width // (2 * HD)
    wide = gathered[0].shape[-1]
    full = lambda s: pl.BlockSpec(s, lambda i: (0,) * len(s))
    tile = lambda cols: pl.BlockSpec((tm, cols), lambda i: (i, 0))
    return pl.pallas_call(
        functools.partial(attn_forward_body, rows=rows),
        grid=(row_count // rows,),
        in_specs=[
            pl.BlockSpec(memory_space=pltpu.SMEM),
            tile(width),
            pl.BlockSpec((rows, 1, width), lambda i: (i, 0, 0)),
            pl.BlockSpec((rows, 1, size), lambda i: (i, 0, 0)),
        ]
        + [full(g.shape) for g in gathered],
        out_specs=[
            tile(width),
            tile(3 * width),
            pl.BlockSpec((rows, pairs, size, 2 * size), lambda i: (i, 0, 0, 0)),
            tile(width),
            tile(width),
            tile(width),
            full((width, wide)),
            full((16, width)),
        ],
        out_shape=[
            jax.ShapeDtypeStruct((toks, width), BF16),
            jax.ShapeDtypeStruct((toks, 3 * width), BF16),
            jax.ShapeDtypeStruct((row_count, pairs, size, 2 * size), BF16),
            jax.ShapeDtypeStruct((toks, width), BF16),
            jax.ShapeDtypeStruct((toks, width), F32),
            jax.ShapeDtypeStruct((toks, width), BF16),
            jax.ShapeDtypeStruct((width, wide), BF16),
            jax.ShapeDtypeStruct((16, width), F32),
        ],
        compiler_params=pltpu.CompilerParams(vmem_limit_bytes=VMEM_LIMIT),
        cost_estimate=pl.CostEstimate(flops=16 * 10**9, bytes_accessed=20 * 10**6, transcendentals=2 * 10**6),
        name="attn_forward",
    )(place, tok, time, seg, *gathered)


def ffn_body(
    place, n2, cot, fc, out, bfc, acc_out, acc_dn2, dbfc, keep, send, fc_s, out_s, act_s, dpre_s, *, tm, sub
):
    step = pl.program_id(0)
    width = n2.shape[1]

    @pl.when(step == 0)
    def _():
        acc_out[...] = jnp.zeros_like(acc_out)
        acc_dn2[...] = jnp.zeros_like(acc_dn2)

    fc_s[...] = merge_rows(fc[:, 0])
    out_s[...] = merge_rows(out[...].reshape((-1,) + out.shape[2:]))
    chunk = fc_s.shape[1]
    for part in range(chunk // sub):
        cols = slice(part * sub, (part + 1) * sub)
        bias = bfc[:, cols]
        db = jnp.zeros_like(bias)
        for m in range(n2.shape[0] // tm):
            sl = slice(m * tm, (m + 1) * tm)
            pre = dot(n2[sl, :], fc_s[:, cols], 1, 0) + bias
            d_act = dot(cot[sl, :], out_s[cols, :], 1, 1)
            cdf = 0.5 * lax.erf(pre * math.sqrt(0.5)) + 0.5
            density = jnp.exp(pre * pre * -0.5) * (1.0 / math.sqrt(2.0 * math.pi))
            act = (pre * cdf).astype(BF16)
            d_pre = (d_act * (cdf + pre * density)).astype(BF16)
            act_s[sl, cols] = act
            dpre_s[sl, cols] = d_pre
            db = db + jnp.sum(d_pre.astype(F32), axis=0, keepdims=True)
            acc_out[sl, :] += dot(act, out_s[cols, :], 1, 0)
            acc_dn2[sl, :] += dot(d_pre, fc_s[:, cols], 1, 1)
        dbfc[:, cols] = db
    grad = dot(act_s[...], cot[...], 0, 0)
    rows = out.shape[2]
    blocks = out.shape[1]
    for y in range(Y):
        for x in range(X):
            for b in range(blocks):
                at = ((y * X + x) * CORES * blocks + b) * rows
                even = grad[at : at + rows].astype(BF16)
                odd = grad[at + blocks * rows : at + (blocks + 1) * rows].astype(BF16)
                put_blocks(place, step, y, x, even, odd, keep, send, (blocks + b,))
    grad = dot(n2[...], dpre_s[...], 0, 0)
    for z in range(Z):
        for y in range(Y):
            for x in range(X):
                at = ((z * Y + y) * X + x) * CORES * rows
                even = grad[at : at + rows].astype(BF16)
                odd = grad[at + rows : at + 2 * rows].astype(BF16)
                put_blocks(place, z, y, x, even, odd, keep, send, (step,))


def ffn(place, n2, cot, gathered, bfc, tm=512, sub=256):
    toks, width = n2.shape
    pieces, count, rows, _ = gathered.shape
    blocks = count // 2
    hidden = width * blocks
    chunk = hidden // Z
    full = lambda s: pl.BlockSpec(s, lambda j: (0,) * len(s))
    parted = (Y, X, Z, count, rows, width)
    return pl.pallas_call(
        functools.partial(ffn_body, tm=tm, sub=sub),
        grid=(Z,),
        in_specs=[
            pl.BlockSpec(memory_space=pltpu.SMEM),
            full((toks, width)),
            full((toks, width)),
            pl.BlockSpec((pieces, 1, rows, width), lambda j: (0, j, 0, 0)),
            pl.BlockSpec((pieces // Z, blocks, rows, width), lambda j: (j, 1, 0, 0)),
            pl.BlockSpec((1, chunk), lambda j: (0, j)),
        ],
        out_specs=[
            full((toks, width)),
            full((toks, width)),
            pl.BlockSpec((1, chunk), lambda j: (0, j)),
            full(parted),
            full(parted),
        ],
        out_shape=[
            jax.ShapeDtypeStruct((toks, width), F32),
            jax.ShapeDtypeStruct((toks, width), F32),
            jax.ShapeDtypeStruct((1, hidden), F32),
            jax.ShapeDtypeStruct(parted, BF16),
            jax.ShapeDtypeStruct(parted, BF16),
        ],
        scratch_shapes=[
            pltpu.VMEM((width, chunk), BF16),
            pltpu.VMEM((chunk, width), BF16),
            pltpu.VMEM((toks, chunk), BF16),
            pltpu.VMEM((toks, chunk), BF16),
        ],
        compiler_params=pltpu.CompilerParams(vmem_limit_bytes=VMEM_LIMIT),
        cost_estimate=pl.CostEstimate(flops=30 * 10**9, bytes_accessed=30 * 10**6, transcendentals=6 * 10**6),
        name="ffn",
    )(place, n2, cot, gathered, gathered, bfc)


def attn_backward_body(
    hid, acc_out, acc_dn2, cot, qkv, probs, wproj, vec, layer_out, dhid, dbr, dqkv, sums, *, rows
):
    width = hid.shape[1]
    size = hid.shape[0] // rows

    @pl.when(pl.program_id(0) == 0)
    def _():
        sums[...] = jnp.zeros_like(sums)

    hidden = hid[...]
    layer_out[...] = (hidden + acc_out[...] + vec[7:8, :]).astype(BF16)
    nhat, inv = normalise(hidden)
    dn2 = acc_dn2[...]
    cotangent = cot[...].astype(F32)
    q = dn2 * vec[5:6, :]
    mean_q = jnp.mean(q, axis=-1, keepdims=True)
    mean_qn = jnp.mean(q * nhat, axis=-1, keepdims=True)
    d_hidden = cotangent + (q - mean_q - nhat * mean_qn) * inv
    dhid[...] = d_hidden
    branch = d_hidden.astype(BF16)
    dbr[...] = branch
    sums[0:1, :] += colsum(dn2 * nhat)
    sums[1:2, :] += colsum(dn2)
    sums[2:3, :] += colsum(branch.astype(F32))
    sums[3:4, :] += colsum(cotangent)
    d_mixed = dot(branch, wproj[...], 1, 1).astype(BF16)
    pairs = width // (2 * HD)
    for r in range(rows):
        sl = slice(r * size, (r + 1) * size)
        for p in range(pairs):
            c = 2 * HD * p
            qb = qkv[sl, c : c + 2 * HD] * jnp.asarray(HD**-0.5, BF16)
            k = head_pair(qkv[sl, width + c : width + c + 2 * HD])
            v = head_pair(qkv[sl, 2 * width + c : 2 * width + c + 2 * HD])
            dm = d_mixed[sl, c : c + 2 * HD]
            pr = probs[r, p]
            dp = dot(dm, v, 1, 1)
            pf = pr.astype(F32)
            prod = dp * pf
            ds = jnp.concatenate(
                [
                    prod[:, h * size : (h + 1) * size]
                    - pf[:, h * size : (h + 1) * size]
                    * jnp.sum(prod[:, h * size : (h + 1) * size], axis=-1, keepdims=True)
                    for h in range(2)
                ],
                axis=1,
            ).astype(BF16)
            dv = own_lanes(dot(pr, dm, 0, 0))
            dk = own_lanes(dot(ds, qb, 0, 0))
            dq = dot(ds, k, 1, 0) * HD**-0.5
            dqkv[sl, c : c + 2 * HD] = dq.astype(BF16)
            dqkv[sl, width + c : width + c + 2 * HD] = dk.astype(BF16)
            dqkv[sl, 2 * width + c : 2 * width + c + 2 * HD] = dv.astype(BF16)
    sums[4:5, :] += colsum(dqkv[:, :width].astype(F32))
    sums[5:6, :] += colsum(dqkv[:, 2 * width :].astype(F32))


def attn_backward(hid, acc_out, acc_dn2, cot, qkv, probs, wproj, vec, rows=2):
    row_count, pairs, size, _ = probs.shape
    toks, width = hid.shape
    tm = rows * size
    full = lambda s: pl.BlockSpec(s, lambda i: (0,) * len(s))
    tile = lambda cols: pl.BlockSpec((tm, cols), lambda i: (i, 0))
    return pl.pallas_call(
        functools.partial(attn_backward_body, rows=rows),
        grid=(row_count // rows,),
        in_specs=[
            tile(width),
            tile(width),
            tile(width),
            tile(width),
            tile(3 * width),
            pl.BlockSpec((rows, pairs, size, 2 * size), lambda i: (i, 0, 0, 0)),
            pl.BlockSpec((width, width), lambda i: (0, 3)),
            full(vec.shape),
        ],
        out_specs=[tile(width), tile(width), tile(width), tile(3 * width), full((8, width))],
        out_shape=[
            jax.ShapeDtypeStruct((toks, width), BF16),
            jax.ShapeDtypeStruct((toks, width), F32),
            jax.ShapeDtypeStruct((toks, width), BF16),
            jax.ShapeDtypeStruct((toks, 3 * width), BF16),
            jax.ShapeDtypeStruct((8, width), F32),
        ],
        compiler_params=pltpu.CompilerParams(vmem_limit_bytes=VMEM_LIMIT),
        cost_estimate=pl.CostEstimate(flops=20 * 10**9, bytes_accessed=30 * 10**6, transcendentals=0),
        name="attn_backward",
    )(hid, acc_out, acc_dn2, cot, qkv, probs, wproj, vec)


def weight_grad_body(place, n1, dqkv, att, dbr, keep, send):
    rows = keep.shape[3]

    def emit(grad):
        for z in range(Z):
            for y in range(Y):
                for x in range(X):
                    at = ((z * Y + y) * X + x) * CORES * rows
                    even = grad[at : at + rows].astype(BF16)
                    odd = grad[at + rows : at + 2 * rows].astype(BF16)
                    put_blocks(place, z, y, x, even, odd, keep, send)

    @pl.when(pl.program_id(0) == 0)
    def _():
        emit(dot(att[...], dbr[...], 0, 0))

    @pl.when(pl.program_id(0) > 0)
    def _():
        emit(dot(n1[...], dqkv[...], 0, 0))


def weight_grad(place, n1, dqkv, att, dbr):
    toks, width = n1.shape
    rows = width // PIECES
    full = pl.BlockSpec((toks, width), lambda j: (0, 0))
    parted = pl.BlockSpec((Y, X, Z, rows, width), lambda j: (0, 0, 0, 0, (j + 3) % 4))
    shape = jax.ShapeDtypeStruct((Y, X, Z, rows, 4 * width), BF16)
    return pl.pallas_call(
        weight_grad_body,
        grid=(4,),
        in_specs=[
            pl.BlockSpec(memory_space=pltpu.SMEM),
            full,
            pl.BlockSpec((toks, width), lambda j: (0, jnp.maximum(j - 1, 0))),
            full,
            full,
        ],
        out_specs=[parted, parted],
        out_shape=[shape, shape],
        compiler_params=pltpu.CompilerParams(vmem_limit_bytes=VMEM_LIMIT),
        cost_estimate=pl.CostEstimate(flops=5 * 10**9, bytes_accessed=15 * 10**6, transcendentals=0),
        name="weight_grad",
    )(place, n1, dqkv, att, dbr)


def input_grad_body(tok, time, dhid, dqkv, wqkv, vec, dtok, dtime, sums, *, rows):
    width = tok.shape[1]
    size = tok.shape[0] // rows

    @pl.when(pl.program_id(0) == 0)
    def _():
        sums[...] = jnp.zeros_like(sums)

    x = tok[...].astype(F32)
    x = jnp.concatenate(
        [x[r * size : (r + 1) * size] + time[r].astype(F32) for r in range(rows)], axis=0
    )
    nhat, inv = normalise(x)
    dn1 = dot(dqkv[...], wqkv[...], 1, 1)
    sums[0:1, :] += colsum(dn1 * nhat)
    sums[1:2, :] += colsum(dn1)
    q = dn1 * vec[0:1, :]
    mean_q = jnp.mean(q, axis=-1, keepdims=True)
    mean_qn = jnp.mean(q * nhat, axis=-1, keepdims=True)
    d_tok = dhid[...] + (q - mean_q - nhat * mean_qn) * inv
    dtok[...] = d_tok
    for r in range(rows):
        dtime[r] = colsum(d_tok[r * size : (r + 1) * size])


def input_grad(tok, time, dhid, dqkv, wqkv, vec, rows=2):
    row_count = time.shape[0]
    toks, width = tok.shape
    tm = toks // row_count * rows
    full = lambda s: pl.BlockSpec(s, lambda i: (0,) * len(s))
    tile = lambda cols: pl.BlockSpec((tm, cols), lambda i: (i, 0))
    per_row = pl.BlockSpec((rows, 1, width), lambda i: (i, 0, 0))
    return pl.pallas_call(
        functools.partial(input_grad_body, rows=rows),
        grid=(row_count // rows,),
        in_specs=[
            tile(width),
            per_row,
            tile(width),
            tile(3 * width),
            pl.BlockSpec((width, 3 * width), lambda i: (0, 0)),
            full(vec.shape),
        ],
        out_specs=[tile(width), per_row, full((8, width))],
        out_shape=[
            jax.ShapeDtypeStruct((toks, width), F32),
            jax.ShapeDtypeStruct((row_count, 1, width), F32),
            jax.ShapeDtypeStruct((8, width), F32),
        ],
        compiler_params=pltpu.CompilerParams(vmem_limit_bytes=VMEM_LIMIT),
        cost_estimate=pl.CostEstimate(flops=8 * 10**9, bytes_accessed=18 * 10**6, transcendentals=0),
        name="input_grad",
    )(tok, time, dhid, dqkv, wqkv, vec)


def flip(position):
    return lambda i: i ^ position


def exchange(array, partner):
    return lax.ppermute(array, "dp", [(i, partner(i)) for i in range(PIECES)])


def plane_partner(stage):
    def partner(i):
        along_y = (i % 2 == 0) == (stage == "first")
        return i ^ (4 if along_y else 2)

    return partner


def gather_cube(block):
    ring = [block] + [exchange(block, lambda i, k=k: (i + 8 * k) % PIECES) for k in range(1, Z)]
    line = jnp.stack(ring)
    half = jnp.stack([line, exchange(line, plane_partner("second"))])
    rest = exchange(half, plane_partner("first"))
    return half, rest, exchange(half, flip(1)), exchange(rest, flip(1))


def sum_cube(keep, send):
    came = exchange(send, flip(1))
    wide = lambda v: v.astype(F32)
    away = (wide(keep[1]) + wide(came[1])).astype(BF16)
    first = exchange(away, plane_partner("first"))
    away = (wide(keep[0, 1]) + wide(came[0, 1]) + wide(first[1])).astype(BF16)
    second = exchange(away, plane_partner("second"))
    here = lambda k: wide(keep[0, 0, k]) + wide(came[0, 0, k]) + wide(first[0, k]) + wide(second[k])
    total = here(0)
    for k in range(1, Z):
        total = total + wide(exchange(here(k).astype(BF16), lambda i, k=k: (i - 8 * k) % PIECES))
    return total


def sum_everywhere(values):
    for bit in (1, 2, 4, 8, 16):
        values = values + exchange(values, flip(bit))
    return values


def gather_any(block):
    every = lax.all_gather(block, "dp", axis=0, tiled=True)
    every = every.reshape((Z, Y, X, CORES, every.shape[0] // PIECES) + every.shape[1:])
    deep = [0, 3, 2, 1]
    even = jnp.transpose(every[:, :, :, 0], (1, 2, 0, 3, 4))[:, :, jnp.array(deep)]
    odd = jnp.transpose(every[:, :, :, 1], (2, 1, 0, 3, 4))[:, :, jnp.array(deep)]
    return even[0], even[1], odd[0], odd[1]


def natural_blocks(keep, send):
    deep = jnp.array([0, 3, 2, 1])
    rest = tuple(range(3, keep.ndim))
    even = jnp.transpose(keep[:, :, deep], (2, 0, 1) + rest)
    odd = jnp.transpose(send[:, :, deep], (2, 1, 0) + rest)
    both = jnp.stack([even, odd], axis=3)
    return both.reshape((PIECES,) + both.shape[4:])


def on_device(
    tokens,
    segment_ids,
    time_embed,
    norm1_gain,
    norm1_shift,
    w_qkv,
    b_query,
    b_value,
    w_proj,
    b_proj,
    norm2_gain,
    norm2_shift,
    w_fc,
    b_fc,
    w_out,
    b_out,
    cotangent,
):
    row_count, row_len, width = tokens.shape
    toks = row_count * row_len
    devices = lax.axis_size("dp")
    cube = devices == PIECES
    rank = lax.axis_index("dp")
    grad_scale = 1.0 / math.sqrt(toks * devices)
    own = w_proj.shape[0]
    ratio = b_fc.shape[0] // own
    if cube:
        place = jnp.stack([rank // 8, (rank // 4) % 2, (rank // 2) % 2, rank % 2]).astype(jnp.int32)
    else:
        place = jnp.zeros((4,), jnp.int32)

    small = jnp.stack(
        [norm1_gain, norm1_shift, b_query, b_value, b_proj, norm2_gain, norm2_shift, b_out], axis=1
    )
    small = jnp.concatenate([small, b_fc.reshape(ratio, own).T], axis=1)
    small = jnp.pad(small, ((0, 0), (0, 128 - small.shape[1])))
    attn_block = jnp.concatenate([w_qkv, w_proj, small], axis=1)
    ffn_block = jnp.concatenate(
        [w_fc.reshape(own, ratio, width).transpose(1, 0, 2), w_out.reshape(ratio, own, width)], axis=0
    )
    if cube:
        ffn_full = lax.all_gather(ffn_block, "dp", axis=0)
        attn_full = gather_cube(attn_block)
    else:
        fc_full = lax.all_gather(w_fc, "dp", axis=0, tiled=True)
        out_full = lax.all_gather(w_out, "dp", axis=0, tiled=True)
        cut = width // PIECES
        ffn_full = jnp.concatenate(
            [
                fc_full.reshape(PIECES, cut, ratio, width).transpose(0, 2, 1, 3),
                out_full.reshape(PIECES, ratio, cut, width),
            ],
            axis=1,
        )
        attn_full = gather_any(attn_block)

    flat = tokens.reshape(toks, width)
    times = time_embed.reshape(row_count, 1, width)
    segments = segment_ids.reshape(row_count, 1, row_len)
    cot = cotangent.reshape(toks, width)
    n1, qkv, probs, att, hid, n2, attn_w, vec = attn_forward(place, flat, times, segments, attn_full)
    bfc = vec[8 : 8 + ratio].reshape(ratio, devices, own).transpose(1, 0, 2).reshape(1, ratio * width)
    acc_out, acc_dn2, dbfc, ffn_keep, ffn_send = ffn(place, n2, cot, ffn_full, bfc)
    layer_out, dhid, dbr, dqkv, sums = attn_backward(hid, acc_out, acc_dn2, cot, qkv, probs, attn_w, vec)
    attn_keep, attn_send = weight_grad(place, n1, dqkv, att, dbr)
    d_tokens, d_time, sums1 = input_grad(flat, times, dhid, dqkv, attn_w, vec)

    vectors = jnp.concatenate([sums[:6], sums1[:2], dbfc.reshape(ratio, width)], axis=0)
    if cube:
        vectors = sum_everywhere(vectors)
        own_ffn = sum_cube(ffn_keep, ffn_send)
        own_attn = sum_cube(attn_keep, attn_send)
        own_out = own_ffn[ratio:].reshape(ratio * own, width)
        own_fc = own_ffn[:ratio].transpose(1, 0, 2).reshape(own, ratio * width)
    else:
        vectors = lax.psum(vectors, "dp")
        grads = natural_blocks(attn_keep, attn_send).astype(F32)
        own_attn = lax.psum_scatter(grads.reshape(width, -1), "dp", scatter_dimension=0, tiled=True)
        grads = natural_blocks(ffn_keep, ffn_send).astype(F32)
        fc_grad = grads[:, :ratio].transpose(0, 2, 1, 3).reshape(width, ratio * width)
        own_fc = lax.psum_scatter(fc_grad, "dp", scatter_dimension=0, tiled=True)
        out_grad = grads[:, ratio:].reshape(ratio * width, width)
        own_out = lax.psum_scatter(out_grad, "dp", scatter_dimension=0, tiled=True)
    vectors = vectors * grad_scale
    mine = lax.dynamic_slice(vectors[:8], (0, rank * own), (8, own))
    own_bfc = lax.dynamic_slice(vectors[8:].reshape(-1), (rank * own * ratio,), (own * ratio,))
    own_attn = own_attn * grad_scale
    return (
        layer_out.reshape(tokens.shape),
        d_tokens.reshape(tokens.shape),
        d_time.reshape(time_embed.shape),
        mine[6],
        mine[7],
        own_attn[:, : 3 * width],
        mine[4],
        mine[5],
        own_attn[:, 3 * width :],
        mine[2],
        mine[0],
        mine[1],
        own_fc * grad_scale,
        own_bfc,
        own_out * grad_scale,
        mine[3],
    )


def solution(mesh):
    in_specs = (
        P("dp", None, None),
        P("dp", None),
        P("dp", None),
        P("dp"),
        P("dp"),
        P("dp", None),
        P("dp"),
        P("dp"),
        P("dp", None),
        P("dp"),
        P("dp"),
        P("dp"),
        P("dp", None),
        P("dp"),
        P("dp", None),
        P("dp"),
        P("dp", None, None),
    )
    out_specs = (
        P("dp", None, None),
        P("dp", None, None),
        P("dp", None),
        P("dp"),
        P("dp"),
        P("dp", None),
        P("dp"),
        P("dp"),
        P("dp", None),
        P("dp"),
        P("dp"),
        P("dp"),
        P("dp", None),
        P("dp"),
        P("dp", None),
        P("dp"),
    )
    return jax.shard_map(
        on_device, mesh=mesh, in_specs=in_specs, out_specs=out_specs, check_vma=False
    )
```

```python
import functools
import math

import jax
import jax.numpy as jnp
from jax import lax
from jax.experimental import pallas as pl
from jax.experimental.pallas import tpu as pltpu
from jax.sharding import PartitionSpec as P

HD = 64
EPS = 1e-05
MASKED = -1e30
F32 = jnp.float32
BF16 = jnp.bfloat16
VMEM_LIMIT = 48 * 1024 * 1024


def dot(a, b, a_dim, b_dim):
    return lax.dot_general(a, b, (((a_dim,), (b_dim,)), ((), ())), preferred_element_type=F32)


def normalise(values):
    centered = values - jnp.mean(values, axis=-1, keepdims=True)
    spread = jnp.mean(centered * centered, axis=-1, keepdims=True)
    inv = lax.rsqrt(spread + EPS)
    return centered * inv, inv


def head_pair(block):
    lane = lax.broadcasted_iota(jnp.int32, block.shape, 1)
    zero = jnp.zeros_like(block)
    return jnp.concatenate([jnp.where(lane < HD, block, zero), jnp.where(lane >= HD, block, zero)], axis=0)


def own_lanes(stacked):
    half = stacked.shape[0] // 2
    lane = lax.broadcasted_iota(jnp.int32, (half, stacked.shape[1]), 1)
    return jnp.where(lane < HD, stacked[:half], stacked[half:])


def row_mask(seg_row):
    size = seg_row.shape[1]
    across = jnp.broadcast_to(seg_row.astype(F32), (size, size))
    return jnp.where(across == across.T, 0.0, MASKED)


def colsum(v):
    return jnp.sum(v, axis=0, keepdims=True)


Z, Y, X, CORES = 4, 2, 2, 2
PIECES = Z * Y * X * CORES


def merge_rows(blocks):
    count, rows, width = blocks.shape
    return blocks.astype(F32).reshape(count * rows, width).astype(BF16)


def slots(place, z, y, x):
    ys, xs = y ^ place[1], x ^ place[2]
    first = jnp.where(place[3] == 0, ys, xs)
    second = jnp.where(place[3] == 0, xs, ys)
    return first, second, (place[0] - z + Z) % Z


def put_blocks(place, z, y, x, even, odd, keep, send, tail=()):
    first, second, deep = slots(place, z, y, x)
    mine = place[3] == 0
    keep[(first, second, deep) + tail] = jnp.where(mine, even, odd)
    send[(second, first, deep) + tail] = jnp.where(mine, odd, even)


def pick(place, parts, z, y, x):
    mine0, mine1, other0, other1 = parts
    first, second, deep = slots(place, z, y, x)
    mine = jnp.where(first == 0, mine0[second, deep], mine1[second, deep])
    other = jnp.where(second == 0, other0[first, deep], other1[first, deep])
    even = place[3] == 0
    return jnp.where(even, mine, other), jnp.where(even, other, mine)


def spread(small, cut, row, stride, start, length):
    lane = lax.broadcasted_iota(jnp.int32, (8, 128), 1)
    tiles = [jnp.zeros((8, 128), F32) for _ in range(length // 128)]
    for i in range(PIECES):
        at = start + i * stride
        tile, shift = at // 128, at % 128
        block = small[i * cut + row : i * cut + row + 8]
        if shift:
            block = pltpu.roll(block, shift, 1)
        if shift + cut <= 128:
            tiles[tile] = tiles[tile] + block
        else:
            tiles[tile] = tiles[tile] + jnp.where(lane >= shift, block, 0.0)
            tiles[tile + 1] = tiles[tile + 1] + jnp.where(lane < shift, block, 0.0)
    return jnp.concatenate(tiles, axis=1)


def attn_forward_body(
    place, tok, time, seg, mine0, mine1, other0, other1, n1, qkv, probs, att, hid, n2, weights, vec, bfc, *, rows
):
    size = tok.shape[0] // rows
    width = tok.shape[1]

    @pl.when(pl.program_id(0) == 0)
    def _():
        for z in range(Z):
            for y in range(Y):
                for x in range(X):
                    both = pick(place, (mine0, mine1, other0, other1), z, y, x)
                    both = jnp.concatenate([b.astype(F32) for b in both], axis=0)
                    step = both.shape[0]
                    at = ((z * Y + y) * X + x) * step
                    weights[at : at + step, :] = both.astype(BF16)
        small = weights[:, 4 * width :].astype(F32)
        cut = width // PIECES
        vec[...] = spread(small, cut, 0, cut, 0, width)
        early = spread(small, cut, 8, 2 * cut, 0, bfc.shape[1])
        late = spread(small, cut, 8, 2 * cut, cut, bfc.shape[1])
        bfc[...] = early[0:2] + late[2:4]

    x = tok[...].astype(F32)
    x = jnp.concatenate(
        [x[r * size : (r + 1) * size] + time[r].astype(F32) for r in range(rows)], axis=0
    )
    nhat, _ = normalise(x)
    normed = (nhat * vec[0:1, :] + vec[1:2, :]).astype(BF16)
    n1[...] = normed
    for part in range(3):
        cols = slice(part * width, (part + 1) * width)
        block = dot(normed, weights[:, cols], 1, 0)
        if part == 0:
            block = block + vec[2:3, :]
        if part == 2:
            block = block + vec[3:4, :]
        qkv[:, cols] = block.astype(BF16)
    pairs = width // (2 * HD)
    for r in range(rows):
        sl = slice(r * size, (r + 1) * size)
        mask = row_mask(seg[r])
        for p in range(pairs):
            c = 2 * HD * p
            q = qkv[sl, c : c + 2 * HD] * jnp.asarray(HD**-0.5, BF16)
            k = head_pair(qkv[sl, width + c : width + c + 2 * HD])
            v = head_pair(qkv[sl, 2 * width + c : 2 * width + c + 2 * HD])
            s = dot(q, k, 1, 1)
            halves = []
            for h in range(2):
                sh = s[:, h * size : (h + 1) * size] + mask
                e = jnp.exp(sh - jnp.max(sh, axis=-1, keepdims=True))
                halves.append((e / jnp.sum(e, axis=-1, keepdims=True)).astype(BF16))
            pr = jnp.concatenate(halves, axis=1)
            probs[r, p] = pr
            att[sl, c : c + 2 * HD] = dot(pr, v, 1, 0).astype(BF16)
    hidden = x + dot(att[...], weights[:, 3 * width : 4 * width], 1, 0) + vec[4:5, :]
    hid[...] = hidden
    nhat2, _ = normalise(hidden)
    n2[...] = (nhat2 * vec[5:6, :] + vec[6:7, :]).astype(BF16)


def attn_forward(place, tok, time, seg, gathered, rows=2):
    row_count = seg.shape[0]
    toks, width = tok.shape
    size = toks // row_count
    tm = rows * size
    pairs = width // (2 * HD)
    wide = gathered[0].shape[-1]
    full = lambda s: pl.BlockSpec(s, lambda i: (0,) * len(s))
    tile = lambda cols: pl.BlockSpec((tm, cols), lambda i: (i, 0))
    return pl.pallas_call(
        functools.partial(attn_forward_body, rows=rows),
        grid=(row_count // rows,),
        in_specs=[
            pl.BlockSpec(memory_space=pltpu.SMEM),
            tile(width),
            pl.BlockSpec((rows, 1, width), lambda i: (i, 0, 0)),
            pl.BlockSpec((rows, 1, size), lambda i: (i, 0, 0)),
        ]
        + [full(g.shape) for g in gathered],
        out_specs=[
            tile(width),
            tile(3 * width),
            pl.BlockSpec((rows, pairs, size, 2 * size), lambda i: (i, 0, 0, 0)),
            tile(width),
            tile(width),
            tile(width),
            full((width, wide)),
            full((8, width)),
            full((2, 2 * width)),
        ],
        out_shape=[
            jax.ShapeDtypeStruct((toks, width), BF16),
            jax.ShapeDtypeStruct((toks, 3 * width), BF16),
            jax.ShapeDtypeStruct((row_count, pairs, size, 2 * size), BF16),
            jax.ShapeDtypeStruct((toks, width), BF16),
            jax.ShapeDtypeStruct((toks, width), F32),
            jax.ShapeDtypeStruct((toks, width), BF16),
            jax.ShapeDtypeStruct((width, wide), BF16),
            jax.ShapeDtypeStruct((8, width), F32),
            jax.ShapeDtypeStruct((2, 2 * width), F32),
        ],
        compiler_params=pltpu.CompilerParams(vmem_limit_bytes=VMEM_LIMIT),
        cost_estimate=pl.CostEstimate(flops=16 * 10**9, bytes_accessed=20 * 10**6, transcendentals=2 * 10**6),
        name="attn_forward",
    )(place, tok, time, seg, *gathered)


def ffn_body(place, n2, cot, fc, out, bfc, acc_out, acc_dn2, dbfc, keep, send, fc_s, out_s, act_s, dpre_s, *, tm, sub, half):
    step = pl.program_id(0)

    @pl.when(step == 0)
    def _():
        acc_out[...] = jnp.zeros_like(acc_out)
        acc_dn2[...] = jnp.zeros_like(acc_dn2)

    fc_s[...] = merge_rows(fc[:, 0])
    out_s[...] = merge_rows(out[...].reshape((-1,) + out.shape[2:]))
    chunk = fc_s.shape[1]
    for part in range(chunk // sub):
        cols = slice(part * sub, (part + 1) * sub)
        bias = bfc[half : half + 1, cols]
        db = jnp.zeros_like(bias)
        for m in range(n2.shape[0] // tm):
            sl = slice(m * tm, (m + 1) * tm)
            pre = dot(n2[sl, :], fc_s[:, cols], 1, 0) + bias
            d_act = dot(cot[sl, :], out_s[cols, :], 1, 1)
            cdf = 0.5 * lax.erf(pre * math.sqrt(0.5)) + 0.5
            density = jnp.exp(pre * pre * -0.5) * (1.0 / math.sqrt(2.0 * math.pi))
            act = (pre * cdf).astype(BF16)
            d_pre = (d_act * (cdf + pre * density)).astype(BF16)
            act_s[sl, cols] = act
            dpre_s[sl, cols] = d_pre
            db = db + jnp.sum(d_pre.astype(F32), axis=0, keepdims=True)
            acc_out[sl, :] += dot(act, out_s[cols, :], 1, 0)
            acc_dn2[sl, :] += dot(d_pre, fc_s[:, cols], 1, 1)
        dbfc[:, cols] = db
    grad = dot(act_s[...], cot[...], 0, 0)
    blocks, rows = out.shape[1:3]
    planes = out.shape[0] // (Y * X * CORES)
    for z in range(planes):
        for y in range(Y):
            for x in range(X):
                for b in range(blocks):
                    at = (((z * Y + y) * X + x) * CORES * blocks + b) * rows
                    even = grad[at : at + rows].astype(BF16)
                    odd = grad[at + blocks * rows : at + (blocks + 1) * rows].astype(BF16)
                    put_blocks(place, step * planes + z, y, x, even, odd, keep, send, (blocks + b,))
    grad = dot(n2[...], dpre_s[...], 0, 0)
    for z in range(Z):
        for y in range(Y):
            for x in range(X):
                at = ((z * Y + y) * X + x) * CORES * rows
                even = grad[at : at + rows].astype(BF16)
                odd = grad[at + rows : at + 2 * rows].astype(BF16)
                put_blocks(place, z, y, x, even, odd, keep, send, (step,))


def ffn(place, n2, cot, gathered, bfc, half, tm=512, sub=256):
    toks, width = n2.shape
    pieces, _, rows, _ = gathered.shape
    blocks = 2
    count = 2 * blocks
    once = pl.Buffered(buffer_count=1)
    full = lambda s: pl.BlockSpec(s, lambda j: (0,) * len(s), pipeline_mode=once)
    whole = lambda s: pl.BlockSpec(s, lambda j: (0,) * len(s))
    parted = (Y, X, Z, count, rows, width)
    return pl.pallas_call(
        functools.partial(ffn_body, tm=tm, sub=sub, half=half),
        grid=(blocks,),
        in_specs=[
            pl.BlockSpec(memory_space=pltpu.SMEM),
            full((toks, width)),
            full((toks, width)),
            pl.BlockSpec((pieces, 1, rows, width), lambda j: (0, count * half + j, 0, 0)),
            pl.BlockSpec((pieces // blocks, blocks, rows, width), lambda j: (j, 2 * half + 1, 0, 0)),
            pl.BlockSpec((2, width), lambda j: (0, j)),
        ],
        out_specs=[
            whole((toks, width)),
            whole((toks, width)),
            pl.BlockSpec((1, width), lambda j: (0, j)),
            whole(parted),
            whole(parted),
        ],
        out_shape=[
            jax.ShapeDtypeStruct((toks, width), F32),
            jax.ShapeDtypeStruct((toks, width), F32),
            jax.ShapeDtypeStruct((1, blocks * width), F32),
            jax.ShapeDtypeStruct(parted, BF16),
            jax.ShapeDtypeStruct(parted, BF16),
        ],
        scratch_shapes=[
            pltpu.VMEM((width, width), BF16),
            pltpu.VMEM((width, width), BF16),
            pltpu.VMEM((toks, width), BF16),
            pltpu.VMEM((toks, width), BF16),
        ],
        compiler_params=pltpu.CompilerParams(vmem_limit_bytes=VMEM_LIMIT),
        cost_estimate=pl.CostEstimate(flops=15 * 10**9, bytes_accessed=20 * 10**6, transcendentals=3 * 10**6),
        name="ffn",
    )(place, n2, cot, gathered, gathered, bfc)


def attn_backward_body(
    tok, time, hid, out0, out1, dn20, dn21, cot, qkv, probs, weights, vec, *refs, rows
):
    layer_out, dtok, dtime, dbr, dqkv, sums = refs[-6:]
    width = hid.shape[1]
    size = hid.shape[0] // rows

    @pl.when(pl.program_id(0) == 0)
    def _():
        sums[...] = jnp.zeros_like(sums)

    hidden = hid[...]
    layer_out[...] = (hidden + (out0[...] + out1[...]) + vec[7:8, :]).astype(BF16)
    nhat, inv = normalise(hidden)
    dn2 = dn20[...] + dn21[...]
    cotangent = cot[...].astype(F32)
    q = dn2 * vec[5:6, :]
    mean_q = jnp.mean(q, axis=-1, keepdims=True)
    mean_qn = jnp.mean(q * nhat, axis=-1, keepdims=True)
    d_hidden = cotangent + (q - mean_q - nhat * mean_qn) * inv
    dtok[...] = d_hidden
    branch = d_hidden.astype(BF16)
    dbr[...] = branch
    sums[0:1, :] += colsum(dn2 * nhat)
    sums[1:2, :] += colsum(dn2)
    sums[2:3, :] += colsum(branch.astype(F32))
    sums[3:4, :] += colsum(cotangent)
    d_mixed = dot(branch, weights[:, 3 * width : 4 * width], 1, 1).astype(BF16)
    pairs = width // (2 * HD)
    for r in range(rows):
        sl = slice(r * size, (r + 1) * size)
        for p in range(pairs):
            c = 2 * HD * p
            qb = qkv[sl, c : c + 2 * HD] * jnp.asarray(HD**-0.5, BF16)
            k = head_pair(qkv[sl, width + c : width + c + 2 * HD])
            v = head_pair(qkv[sl, 2 * width + c : 2 * width + c + 2 * HD])
            dm = d_mixed[sl, c : c + 2 * HD]
            pr = probs[r, p]
            dp = dot(dm, v, 1, 1)
            pf = pr.astype(F32)
            prod = dp * pf
            ds = jnp.concatenate(
                [
                    prod[:, h * size : (h + 1) * size]
                    - pf[:, h * size : (h + 1) * size]
                    * jnp.sum(prod[:, h * size : (h + 1) * size], axis=-1, keepdims=True)
                    for h in range(2)
                ],
                axis=1,
            ).astype(BF16)
            dv = own_lanes(dot(pr, dm, 0, 0))
            dk = own_lanes(dot(ds, qb, 0, 0))
            dq = dot(ds, k, 1, 0) * HD**-0.5
            dqkv[sl, c : c + 2 * HD] = dq.astype(BF16)
            dqkv[sl, width + c : width + c + 2 * HD] = dk.astype(BF16)
            dqkv[sl, 2 * width + c : 2 * width + c + 2 * HD] = dv.astype(BF16)
    sums[4:5, :] += colsum(dqkv[:, :width].astype(F32))
    sums[5:6, :] += colsum(dqkv[:, 2 * width :].astype(F32))

    x = tok[...].astype(F32)
    x = jnp.concatenate(
        [x[r * size : (r + 1) * size] + time[r].astype(F32) for r in range(rows)], axis=0
    )
    nhat, inv = normalise(x)
    dn1 = dot(dqkv[...], weights[:, : 3 * width], 1, 1)
    sums[6:7, :] += colsum(dn1 * nhat)
    sums[7:8, :] += colsum(dn1)
    q = dn1 * vec[0:1, :]
    mean_q = jnp.mean(q, axis=-1, keepdims=True)
    mean_qn = jnp.mean(q * nhat, axis=-1, keepdims=True)
    d_tok = dtok[...] + (q - mean_q - nhat * mean_qn) * inv
    dtok[...] = d_tok
    for r in range(rows):
        dtime[r] = colsum(d_tok[r * size : (r + 1) * size])


def attn_backward(tok, time, hid, outs, dn2s, cot, qkv, probs, weights, vec, base, steps, before=(), rows=2):
    row_count, pairs, size, _ = probs.shape
    width = hid.shape[1]
    tm = rows * size
    toks = row_count * size
    once = pl.Buffered(buffer_count=1)
    full = lambda s: pl.BlockSpec(s, lambda i: (0,) * len(s), pipeline_mode=once)
    tile = lambda cols: pl.BlockSpec((tm, cols), lambda i: (i + base, 0))
    per_row = pl.BlockSpec((rows, 1, width), lambda i: (i + base, 0, 0))
    return pl.pallas_call(
        functools.partial(attn_backward_body, rows=rows),
        grid=(steps,),
        in_specs=[tile(width), per_row]
        + [tile(width)] * 6
        + [
            tile(3 * width),
            pl.BlockSpec((rows, pairs, size, 2 * size), lambda i: (i + base, 0, 0, 0)),
            full(weights.shape),
            full(vec.shape),
        ]
        + [pl.BlockSpec(memory_space=pl.ANY)] * len(before),
        out_specs=[
            tile(width),
            tile(width),
            per_row,
            tile(width),
            tile(3 * width),
            pl.BlockSpec((8, width), lambda i: (0, 0)),
        ],
        input_output_aliases={12 + k: k for k in range(len(before))},
        out_shape=[
            jax.ShapeDtypeStruct((toks, width), BF16),
            jax.ShapeDtypeStruct((toks, width), F32),
            jax.ShapeDtypeStruct((row_count, 1, width), F32),
            jax.ShapeDtypeStruct((toks, width), BF16),
            jax.ShapeDtypeStruct((toks, 3 * width), BF16),
            jax.ShapeDtypeStruct((8, width), F32),
        ],
        compiler_params=pltpu.CompilerParams(vmem_limit_bytes=VMEM_LIMIT),
        cost_estimate=pl.CostEstimate(flops=6 * 10**9 * steps, bytes_accessed=10 * 10**6 * steps, transcendentals=0),
        name="attn_backward",
    )(tok, time, hid, *outs, *dn2s, cot, qkv, probs, weights, vec, *before)


def collect(vectors, cut, stride, start, piece):
    at = start + piece * stride
    tile, shift = at // 128, at % 128
    lane = lax.broadcasted_iota(jnp.int32, (vectors.shape[0], 128), 1)
    block = vectors[:, tile * 128 : (tile + 1) * 128]
    if shift + cut > 128:
        block = jnp.where(lane >= shift, block, vectors[:, (tile + 1) * 128 : (tile + 2) * 128])
    if shift:
        block = pltpu.roll(block, 128 - shift, 1)
    return jnp.where(lane < cut, block, 0.0)


def weight_grad_body(place, *refs, columns, with_vectors):
    keep, send = refs[-2:]
    rows = keep.shape[3]
    width = refs[0].shape[1]
    step = pl.program_id(0)

    def emit(grad, tail):
        for z in range(Z):
            for y in range(Y):
                for x in range(X):
                    at = ((z * Y + y) * X + x) * CORES * rows
                    even = grad[at : at + rows].astype(BF16)
                    odd = grad[at + rows : at + 2 * rows].astype(BF16)
                    put_blocks(place, z, y, x, even, odd, keep, send, tail)

    for k in range(columns):

        @pl.when(step == k)
        def _(k=k):
            emit(dot(refs[0][...], refs[1][...], 0, 0), (slice(None), slice(k * width, (k + 1) * width)))

    if with_vectors:

        @pl.when(step == columns)
        def _():
            att, dbr, sums0, sums1, dbfc0, dbfc1 = refs[2:8]
            emit(dot(att[...], dbr[...], 0, 0), (slice(None), slice(columns * width, (columns + 1) * width)))
            vectors = sums0[...] + sums1[...]
            pad = jnp.zeros((6, dbfc0.shape[1]), F32)
            hidden = jnp.concatenate([dbfc0[...], dbfc1[...], pad], axis=0)

            def block(piece):
                early = collect(hidden, rows, 2 * rows, 0, piece)
                late = collect(hidden, rows, 2 * rows, rows, piece)
                top = collect(vectors, rows, rows, 0, piece)
                rest = [early[:2], late[:2], jnp.zeros((rows - 12, 128), F32)]
                return jnp.concatenate([top] + rest, axis=0).astype(BF16)

            for z in range(Z):
                for y in range(Y):
                    for x in range(X):
                        piece = ((z * Y + y) * X + x) * CORES
                        tail = (slice(None), slice((columns + 1) * width, (columns + 1) * width + 128))
                        put_blocks(place, z, y, x, block(piece), block(piece + 1), keep, send, tail)


def weight_grad(place, n1, dqkv, first, columns, extra=()):
    toks, width = n1.shape
    rows = width // PIECES
    once = pl.Buffered(buffer_count=1)
    full = lambda a: pl.BlockSpec(a.shape, lambda j: (0, 0), pipeline_mode=once)
    parted = (Y, X, Z, rows, columns * width + (width + 128 if extra else 0))
    whole = pl.BlockSpec(parted, lambda j: (0,) * 5)
    shape = jax.ShapeDtypeStruct(parted, BF16)
    return pl.pallas_call(
        functools.partial(weight_grad_body, columns=columns, with_vectors=bool(extra)),
        grid=(columns + bool(extra),),
        in_specs=[
            pl.BlockSpec(memory_space=pltpu.SMEM),
            full(n1),
            pl.BlockSpec((toks, width), lambda j: (0, first + jnp.minimum(j, columns - 1))),
        ]
        + [full(e) for e in extra],
        out_specs=[whole, whole],
        out_shape=[shape, shape],
        compiler_params=pltpu.CompilerParams(vmem_limit_bytes=VMEM_LIMIT),
        cost_estimate=pl.CostEstimate(flops=25 * 10**8, bytes_accessed=8 * 10**6, transcendentals=0),
        name="weight_grad",
    )(place, n1, dqkv, *extra)


def flip(position):
    return lambda i: i ^ position


def exchange(array, partner):
    return lax.ppermute(array, "dp", [(i, partner(i)) for i in range(PIECES)])


def plane_partner(stage):
    def partner(i):
        along_y = (i % 2 == 0) == (stage == "first")
        return i ^ (4 if along_y else 2)

    return partner


class CubeGather:
    def __init__(self, block):
        self.ready, self.step, self.mine, self.parts = block, 0, None, None

    def send(self):
        if self.step == 0:
            ring = [exchange(self.ready, lambda i, k=k: (i + 8 * k) % PIECES) for k in range(1, Z)]
            self.ready = jnp.stack([self.ready] + ring)
        elif self.step == 1:
            self.ready = jnp.stack([self.ready, exchange(self.ready, plane_partner("second"))])
        elif self.step == 2:
            self.ready = (self.ready, exchange(self.ready, plane_partner("first")))
        else:
            self.parts = self.ready + tuple(exchange(half, flip(1)) for half in self.ready)
        self.step += 1


class CubeSum:
    def __init__(self, keep, send):
        self.grads, self.keep, self.ahead = (keep, send), keep, send
        self.came, self.first, self.second, self.rest = None, None, None, None

    def part(self, *at):
        total = self.keep[at].astype(F32) + self.came[at].astype(F32)
        if self.first is not None:
            total = total + self.first[at[1:]].astype(F32)
        if self.second is not None:
            total = total + self.second[at[2:]].astype(F32)
        return total

    def send(self):
        if self.came is None:
            self.came = exchange(self.ahead, flip(1))
        elif self.first is None:
            self.ahead = self.part(1).astype(BF16)
            self.first = exchange(self.ahead, plane_partner("first"))
        elif self.second is None:
            self.ahead = self.part(0, 1).astype(BF16)
            self.second = exchange(self.ahead, plane_partner("second"))
        else:
            self.ahead = [self.part(0, 0, k).astype(BF16) for k in range(1, Z)]
            self.rest = [
                exchange(block, lambda i, k=k: (i - 8 * k) % PIECES) for k, block in enumerate(self.ahead, 1)
            ]

    def total(self):
        return self.part(0, 0, 0) + sum(block.astype(F32) for block in self.rest)


def hold(first, *then):
    return tuple(lax.optimization_barrier((first, one))[1] for one in then)


def sum_over(values, *bits):
    for bit in bits:
        values = values + exchange(values, flip(bit))
    return values


def cut_any(every):
    every = every.reshape((Z, Y, X, CORES, every.shape[0] // PIECES) + every.shape[1:])
    deep = jnp.array([0, 3, 2, 1])
    even = jnp.transpose(every[:, :, :, 0], (1, 2, 0, 3, 4))[:, :, deep]
    odd = jnp.transpose(every[:, :, :, 1], (2, 1, 0, 3, 4))[:, :, deep]
    return even[0], even[1], odd[0], odd[1]


def natural_blocks(keep, send):
    deep = jnp.array([0, 3, 2, 1])
    rest = tuple(range(3, keep.ndim))
    even = jnp.transpose(keep[:, :, deep], (2, 0, 1) + rest)
    odd = jnp.transpose(send[:, :, deep], (2, 1, 0) + rest)
    both = jnp.stack([even, odd], axis=3)
    return both.reshape((PIECES,) + both.shape[4:])


def on_device(
    tokens,
    segment_ids,
    time_embed,
    norm1_gain,
    norm1_shift,
    w_qkv,
    b_query,
    b_value,
    w_proj,
    b_proj,
    norm2_gain,
    norm2_shift,
    w_fc,
    b_fc,
    w_out,
    b_out,
    cotangent,
):
    row_count, row_len, width = tokens.shape
    toks = row_count * row_len
    devices = lax.axis_size("dp")
    cube = devices == PIECES
    rank = lax.axis_index("dp")
    grad_scale = 1.0 / math.sqrt(toks * devices)
    own = w_proj.shape[0]
    ratio = b_fc.shape[0] // own
    if cube:
        place = jnp.stack([rank // 8, (rank // 4) % 2, (rank // 2) % 2, rank % 2]).astype(jnp.int32)
    else:
        place = jnp.zeros((4,), jnp.int32)

    small = jnp.concatenate(
        [norm1_gain, norm1_shift, b_query, b_value, b_proj, norm2_gain, norm2_shift, b_out, b_fc]
    ).reshape(8 + ratio, own)
    order = list(range(8)) + [8 + 2 * h + k for k in range(ratio // 2) for h in range(2)]
    small = jnp.concatenate([small[v : v + 1] for v in order], axis=0)
    cut = width // PIECES
    halves = 2
    blocks = ratio // halves
    ffn_fc = lambda w: w.reshape(-1, PIECES, halves, blocks * cut).transpose(2, 0, 1, 3).reshape(halves, -1, blocks, width)
    if cube:
        ffn_block = jnp.concatenate(
            [ffn_fc(w_fc).transpose(0, 2, 1, 3), w_out.reshape(halves, blocks, own, width)], axis=1
        )
        ffn_full = lax.all_gather(ffn_block.reshape(-1, own, width), "dp", axis=0)
        small = jnp.pad(small, ((0, own - small.shape[0]), (0, 128 - own)))
        attn_gather = CubeGather(jnp.concatenate([w_qkv, w_proj, small], axis=1))
        for _ in range(4):
            attn_gather.send()
        attn_full = attn_gather.parts
    else:
        whole = lambda w: lax.all_gather(w, "dp", axis=0, tiled=True)
        natural = whole(small.T.reshape(own, -1))
        vectors = natural[:, :8].T
        hidden_bias = whole(b_fc).reshape(PIECES, ratio, cut)
        small = jnp.concatenate(
            [vectors.reshape(8, PIECES, cut).transpose(1, 0, 2), hidden_bias[:, jnp.array([0, 2, 1, 3])]], axis=1
        )
        small = jnp.pad(small, ((0, 0), (0, cut - small.shape[1]), (0, 128 - cut))).reshape(width, 128)
        attn_full = cut_any(jnp.concatenate([whole(w_qkv), whole(w_proj), small], axis=1))
        fc_full = ffn_fc(whole(w_fc)).reshape(halves, PIECES, cut, blocks, width).transpose(1, 0, 3, 2, 4)
        out_full = whole(w_out).reshape(PIECES, halves, blocks, cut, width)
        ffn_full = jnp.concatenate([fc_full, out_full], axis=2).reshape(PIECES, -1, cut, width)

    flat = tokens.reshape(toks, width)
    times = time_embed.reshape(row_count, 1, width)
    segments = segment_ids.reshape(row_count, 1, row_len)
    cot = cotangent.reshape(toks, width)
    n1, qkv, probs, att, hid, n2, attn_w, vec, bfc = attn_forward(place, flat, times, segments, attn_full)

    out0, dn20, dbfc0, *grads0 = ffn(place, n2, cot, ffn_full, bfc, 0)
    sum0 = CubeSum(*grads0)
    if cube:
        sum0.send()
    bfc, out0 = lax.optimization_barrier((bfc, out0))
    out1, dn21, dbfc1, *grads1 = ffn(place, n2, cot, ffn_full, bfc, 1)
    sum1 = CubeSum(*grads1)
    backward = lambda hid, base, steps, before: attn_backward(
        flat, times, hid, (out0, out1), (dn20, dn21), cot, qkv, probs, attn_w, vec, base, steps, before
    )
    steps = row_count // 2
    if cube:
        sum0.send()
        sum1.send()
        (hid,) = hold(sum0.ahead, hid)
    *before, sums0 = backward(hid, 0, 1, ())
    if cube:
        sum1.send()
        sum0.send()
        (hid,) = hold(sum1.ahead, *hold(sum0.ahead, hid))
    layer_out, d_tokens, d_time, dbr, dqkv, sums1 = backward(hid, 1, steps - 1, before)
    if cube:
        sum0.send()
        sum1.send()
        (dqkv,) = hold(sum1.ahead, *hold(sum0.ahead[0], dqkv))
    attn0 = CubeSum(*weight_grad(place, n1, dqkv, 0, 2))
    if cube:
        attn0.send()
        attn0.keep, dbr = lax.optimization_barrier((attn0.keep, dbr))
    attn1 = CubeSum(*weight_grad(place, n1, dqkv, 2, 1, (att, dbr, sums0, sums1, dbfc0, dbfc1)))
    if cube:
        attn0.send()
        attn1.send()
        attn1.send()
        sum1.second, *sum0.rest = hold(attn1.ahead, sum1.second, *sum0.rest)
        sum1.send()
        attn0.send()
        attn1.send()
        sum1.rest = hold(attn1.ahead, *sum1.rest)
        attn0.send()
        attn1.send()
        own_ffn = jnp.stack([sum0.total(), sum1.total()])
        (own_ffn,) = hold(attn1.ahead[0], own_ffn)
        own_attn = jnp.concatenate([attn0.total(), attn1.total()], axis=1)
        own_out = own_ffn[:, blocks:].reshape(ratio * own, width)
        own_fc = own_ffn[:, :blocks].transpose(2, 0, 1, 3).reshape(own, halves, PIECES, blocks * own)
        own_fc = own_fc.transpose(0, 2, 1, 3).reshape(own, ratio * width)
        vectors = own_attn[:, 4 * width :]
        mine = vectors[:8, :own]
        own_bfc = jnp.concatenate([vectors[8 + v, :own] for v in (0, 2, 1, 3)])
    else:
        scatter = lambda g: lax.psum_scatter(g, "dp", scatter_dimension=0, tiled=True)
        grads = jnp.concatenate([natural_blocks(*a.grads) for a in (attn0, attn1)], axis=-1).astype(F32)
        own_attn = scatter(grads[:, :, : 4 * width].reshape(width, -1))
        vectors = lax.psum(grads[:, :, 4 * width : 4 * width + cut], "dp")
        mine = lax.dynamic_slice(
            vectors[:, :8].transpose(1, 0, 2).reshape(8, width), (0, rank * own), (8, own)
        )
        hidden_grad = vectors[:, jnp.array([8, 10, 9, 11])].reshape(-1)
        own_bfc = lax.dynamic_slice(hidden_grad, (rank * own * ratio,), (own * ratio,))
        grads = jnp.stack([natural_blocks(*s.grads) for s in (sum0, sum1)], axis=1).astype(F32)
        out_grad = grads[:, :, blocks:].reshape(ratio * width, width)
        own_out = scatter(out_grad)
        fc_grad = grads[:, :, :blocks].transpose(0, 3, 1, 2, 4).reshape(width, halves, PIECES, blocks * cut)
        own_fc = scatter(fc_grad.transpose(0, 2, 1, 3).reshape(width, ratio * width))
    mine, own_bfc = mine * grad_scale, own_bfc * grad_scale
    own_attn = own_attn * grad_scale
    return (
        layer_out.reshape(tokens.shape),
        d_tokens.reshape(tokens.shape),
        d_time.reshape(time_embed.shape),
        mine[6],
        mine[7],
        own_attn[:, : 3 * width],
        mine[4],
        mine[5],
        own_attn[:, 3 * width : 4 * width],
        mine[2],
        mine[0],
        mine[1],
        own_fc * grad_scale,
        own_bfc,
        own_out * grad_scale,
        mine[3],
    )


def solution(mesh):
    in_specs = (
        P("dp", None, None),
        P("dp", None),
        P("dp", None),
        P("dp"),
        P("dp"),
        P("dp", None),
        P("dp"),
        P("dp"),
        P("dp", None),
        P("dp"),
        P("dp"),
        P("dp"),
        P("dp", None),
        P("dp"),
        P("dp", None),
        P("dp"),
        P("dp", None, None),
    )
    out_specs = (
        P("dp", None, None),
        P("dp", None, None),
        P("dp", None),
        P("dp"),
        P("dp"),
        P("dp", None),
        P("dp"),
        P("dp"),
        P("dp", None),
        P("dp"),
        P("dp"),
        P("dp"),
        P("dp", None),
        P("dp"),
        P("dp", None),
        P("dp"),
    )
    return jax.shard_map(
        on_device, mesh=mesh, in_specs=in_specs, out_specs=out_specs, check_vma=False
    )
```

```python
import functools
import math

import jax
import jax.numpy as jnp
from jax import lax
from jax.experimental import pallas as pl
from jax.experimental.pallas import tpu as pltpu
from jax.sharding import PartitionSpec as P

HD = 64
EPS = 1e-05
MASKED = -1e30
F32 = jnp.float32
BF16 = jnp.bfloat16
VMEM_LIMIT = 48 * 1024 * 1024


def dot(a, b, a_dim, b_dim):
    return lax.dot_general(a, b, (((a_dim,), (b_dim,)), ((), ())), preferred_element_type=F32)


def normalise(values):
    centered = values - jnp.mean(values, axis=-1, keepdims=True)
    spread = jnp.mean(centered * centered, axis=-1, keepdims=True)
    inv = lax.rsqrt(spread + EPS)
    return centered * inv, inv


def head_pair(block):
    lane = lax.broadcasted_iota(jnp.int32, block.shape, 1)
    zero = jnp.zeros_like(block)
    return jnp.concatenate([jnp.where(lane < HD, block, zero), jnp.where(lane >= HD, block, zero)], axis=0)


def own_lanes(stacked):
    half = stacked.shape[0] // 2
    lane = lax.broadcasted_iota(jnp.int32, (half, stacked.shape[1]), 1)
    return jnp.where(lane < HD, stacked[:half], stacked[half:])


def row_mask(seg_row):
    size = seg_row.shape[1]
    across = jnp.broadcast_to(seg_row.astype(F32), (size, size))
    return jnp.where(across == across.T, 0.0, MASKED)


def colsum(v):
    return jnp.sum(v, axis=0, keepdims=True)


Z, Y, X, CORES = 4, 2, 2, 2
PIECES = Z * Y * X * CORES


def merge_rows(blocks):
    count, rows, width = blocks.shape
    return blocks.astype(F32).reshape(count * rows, width).astype(BF16)


def slots(place, z, y, x):
    ys, xs = y ^ place[1], x ^ place[2]
    first = jnp.where(place[3] == 0, ys, xs)
    second = jnp.where(place[3] == 0, xs, ys)
    return first, second, (place[0] - z + Z) % Z


def put_blocks(place, z, y, x, even, odd, keep, send, tail=()):
    first, second, deep = slots(place, z, y, x)
    mine = place[3] == 0
    keep[(first, second, deep) + tail] = jnp.where(mine, even, odd)
    send[(second, first, deep) + tail] = jnp.where(mine, odd, even)


def pick(place, parts, z, y, x, tail=()):
    mine0, mine1, other0, other1 = parts
    first, second, deep = slots(place, z, y, x)
    mine = jnp.where(first == 0, mine0[(second, deep) + tail], mine1[(second, deep) + tail])
    other = jnp.where(second == 0, other0[(first, deep) + tail], other1[(first, deep) + tail])
    even = place[3] == 0
    return jnp.where(even, mine, other), jnp.where(even, other, mine)


def spread(small, cut, row, stride, start, length):
    lane = lax.broadcasted_iota(jnp.int32, (8, 128), 1)
    tiles = [jnp.zeros((8, 128), F32) for _ in range(length // 128)]
    for i in range(PIECES):
        at = start + i * stride
        tile, shift = at // 128, at % 128
        block = small[i * cut + row : i * cut + row + 8]
        if shift:
            block = pltpu.roll(block, shift, 1)
        if shift + cut <= 128:
            tiles[tile] = tiles[tile] + block
        else:
            tiles[tile] = tiles[tile] + jnp.where(lane >= shift, block, 0.0)
            tiles[tile + 1] = tiles[tile + 1] + jnp.where(lane < shift, block, 0.0)
    return jnp.concatenate(tiles, axis=1)


def attn_forward_body(
    place, tok, time, seg, mine0, mine1, other0, other1, n1, qkv, probs, att, hid, n2, weights, vec, bfc, *, rows
):
    size = tok.shape[0] // rows
    width = tok.shape[1]

    @pl.when(pl.program_id(0) == 0)
    def _():
        for z in range(Z):
            for y in range(Y):
                for x in range(X):
                    both = pick(place, (mine0, mine1, other0, other1), z, y, x)
                    both = jnp.concatenate([b.astype(F32) for b in both], axis=0)
                    step = both.shape[0]
                    at = ((z * Y + y) * X + x) * step
                    weights[at : at + step, :] = both.astype(BF16)
        small = weights[:, 4 * width :].astype(F32)
        cut = width // PIECES
        vec[...] = spread(small, cut, 0, cut, 0, width)
        early = spread(small, cut, 8, 2 * cut, 0, bfc.shape[1])
        late = spread(small, cut, 8, 2 * cut, cut, bfc.shape[1])
        bfc[...] = early[0:2] + late[2:4]

    x = tok[...].astype(F32)
    x = jnp.concatenate(
        [x[r * size : (r + 1) * size] + time[r].astype(F32) for r in range(rows)], axis=0
    )
    nhat, _ = normalise(x)
    normed = (nhat * vec[0:1, :] + vec[1:2, :]).astype(BF16)
    n1[...] = normed
    for part in range(3):
        cols = slice(part * width, (part + 1) * width)
        block = dot(normed, weights[:, cols], 1, 0)
        if part == 0:
            block = block + vec[2:3, :]
        if part == 2:
            block = block + vec[3:4, :]
        qkv[:, cols] = block.astype(BF16)
    pairs = width // (2 * HD)
    for r in range(rows):
        sl = slice(r * size, (r + 1) * size)
        mask = row_mask(seg[r])
        for p in range(pairs):
            c = 2 * HD * p
            q = qkv[sl, c : c + 2 * HD] * jnp.asarray(HD**-0.5, BF16)
            k = head_pair(qkv[sl, width + c : width + c + 2 * HD])
            v = head_pair(qkv[sl, 2 * width + c : 2 * width + c + 2 * HD])
            s = dot(k, q, 1, 1)
            halves = []
            for h in range(2):
                sh = s[h * size : (h + 1) * size] + mask
                e = jnp.exp(sh - jnp.max(sh, axis=0, keepdims=True))
                halves.append((e * (1.0 / jnp.sum(e, axis=0, keepdims=True))).astype(BF16))
            pr = jnp.concatenate(halves, axis=0)
            probs[r, p] = pr
            att[sl, c : c + 2 * HD] = dot(pr, v, 0, 0).astype(BF16)
    hidden = x + dot(att[...], weights[:, 3 * width : 4 * width], 1, 0) + vec[4:5, :]
    hid[...] = hidden
    nhat2, _ = normalise(hidden)
    n2[...] = (nhat2 * vec[5:6, :] + vec[6:7, :]).astype(BF16)


def attn_forward(place, tok, time, seg, gathered, rows=2):
    row_count = seg.shape[0]
    toks, width = tok.shape
    size = toks // row_count
    tm = rows * size
    pairs = width // (2 * HD)
    wide = gathered[0].shape[-1]
    full = lambda s: pl.BlockSpec(s, lambda i: (0,) * len(s))
    tile = lambda cols: pl.BlockSpec((tm, cols), lambda i: (i, 0))
    return pl.pallas_call(
        functools.partial(attn_forward_body, rows=rows),
        grid=(row_count // rows,),
        in_specs=[
            pl.BlockSpec(memory_space=pltpu.SMEM),
            tile(width),
            pl.BlockSpec((rows, 1, width), lambda i: (i, 0, 0)),
            pl.BlockSpec((rows, 1, size), lambda i: (i, 0, 0)),
        ]
        + [full(g.shape) for g in gathered],
        out_specs=[
            tile(width),
            tile(3 * width),
            pl.BlockSpec((rows, pairs, 2 * size, size), lambda i: (i, 0, 0, 0)),
            tile(width),
            tile(width),
            tile(width),
            full((width, wide)),
            full((8, width)),
            full((2, 2 * width)),
        ],
        out_shape=[
            jax.ShapeDtypeStruct((toks, width), BF16),
            jax.ShapeDtypeStruct((toks, 3 * width), BF16),
            jax.ShapeDtypeStruct((row_count, pairs, 2 * size, size), BF16),
            jax.ShapeDtypeStruct((toks, width), BF16),
            jax.ShapeDtypeStruct((toks, width), F32),
            jax.ShapeDtypeStruct((toks, width), BF16),
            jax.ShapeDtypeStruct((width, wide), BF16),
            jax.ShapeDtypeStruct((8, width), F32),
            jax.ShapeDtypeStruct((2, 2 * width), F32),
        ],
        compiler_params=pltpu.CompilerParams(vmem_limit_bytes=VMEM_LIMIT),
        cost_estimate=pl.CostEstimate(flops=16 * 10**9, bytes_accessed=20 * 10**6, transcendentals=2 * 10**6),
        name="attn_forward",
    )(place, tok, time, seg, *gathered)


def ffn_body(
    place, n2, cot, mine0, mine1, other0, other1, bfc, sum_out, sum_dn2, dbfc, keep, send, acc_out, acc_dn2, fc_s, out_s, act_s, dpre_s, *, tm, sub, half
):
    step = pl.program_id(0)

    @pl.when(step == 0)
    def _():
        acc_out[...] = jnp.zeros_like(acc_out)
        acc_dn2[...] = jnp.zeros_like(acc_dn2)

    gathered = (mine0, mine1, other0, other1)
    blocks, rows = 2, mine0.shape[-2]
    for z in range(Z):
        for y in range(Y):
            for x in range(X):
                both = pick(place, gathered, z, y, x, (step,))
                at = ((z * Y + y) * X + x) * CORES * rows
                fc_s[at : at + CORES * rows, :] = merge_rows(jnp.stack(both))
    for z in range(Z // blocks):
        for y in range(Y):
            for x in range(X):
                both = pick(place, gathered, step * (Z // blocks) + z, y, x, (slice(blocks, 2 * blocks),))
                at = ((z * Y + y) * X + x) * CORES * blocks * rows
                out_s[at : at + CORES * blocks * rows, :] = merge_rows(jnp.concatenate(both, axis=0))
    chunk = fc_s.shape[1]
    for part in range(chunk // sub):
        cols = slice(part * sub, (part + 1) * sub)
        bias = bfc[half : half + 1, cols]
        db = jnp.zeros_like(bias)
        for m in range(n2.shape[0] // tm):
            sl = slice(m * tm, (m + 1) * tm)
            pre = dot(n2[sl, :], fc_s[:, cols], 1, 0) + bias
            d_act = dot(cot[sl, :], out_s[cols, :], 1, 1)
            cdf = 0.5 * lax.erf(pre * math.sqrt(0.5)) + 0.5
            density = jnp.exp(pre * pre * -0.5) * (1.0 / math.sqrt(2.0 * math.pi))
            act = (pre * cdf).astype(BF16)
            d_pre = (d_act * (cdf + pre * density)).astype(BF16)
            act_s[sl, cols] = act
            dpre_s[sl, cols] = d_pre
            db = db + jnp.sum(d_pre.astype(F32), axis=0, keepdims=True)
            acc_out[sl, :] += dot(act, out_s[cols, :], 1, 0)
            acc_dn2[sl, :] += dot(d_pre, fc_s[:, cols], 1, 1)
        dbfc[:, cols] = db

    @pl.when(step == pl.num_programs(0) - 1)
    def _():
        sum_out[...] = acc_out[...].astype(BF16)
        sum_dn2[...] = acc_dn2[...].astype(BF16)

    grad = dot(act_s[...], cot[...], 0, 0)
    planes = Z // blocks
    for z in range(planes):
        for y in range(Y):
            for x in range(X):
                for b in range(blocks):
                    at = (((z * Y + y) * X + x) * CORES * blocks + b) * rows
                    even = grad[at : at + rows].astype(BF16)
                    odd = grad[at + blocks * rows : at + (blocks + 1) * rows].astype(BF16)
                    put_blocks(place, step * planes + z, y, x, even, odd, keep, send, (blocks + b,))
    grad = dot(n2[...], dpre_s[...], 0, 0)
    for z in range(Z):
        for y in range(Y):
            for x in range(X):
                at = ((z * Y + y) * X + x) * CORES * rows
                even = grad[at : at + rows].astype(BF16)
                odd = grad[at + rows : at + 2 * rows].astype(BF16)
                put_blocks(place, z, y, x, even, odd, keep, send, (step,))


def ffn(place, n2, cot, gathered, bfc, half, tm=512, sub=768):
    toks, width = n2.shape
    rows = width // PIECES
    blocks = 2
    count = 2 * blocks
    once = pl.Buffered(buffer_count=1)
    full = lambda s: pl.BlockSpec(s, lambda j: (0,) * len(s), pipeline_mode=once)
    whole = lambda s: pl.BlockSpec(s, lambda j: (0,) * len(s))
    parted = (Y, X, Z, count, rows, width)
    return pl.pallas_call(
        functools.partial(ffn_body, tm=tm, sub=sub, half=half),
        grid=(blocks,),
        in_specs=[
            pl.BlockSpec(memory_space=pltpu.SMEM),
            full((toks, width)),
            full((toks, width)),
        ]
        + [full(g.shape) for g in gathered]
        + [
            pl.BlockSpec((2, width), lambda j: (0, j)),
        ],
        out_specs=[
            whole((toks, width)),
            whole((toks, width)),
            pl.BlockSpec((1, width), lambda j: (0, j)),
            whole(parted),
            whole(parted),
        ],
        out_shape=[
            jax.ShapeDtypeStruct((toks, width), BF16),
            jax.ShapeDtypeStruct((toks, width), BF16),
            jax.ShapeDtypeStruct((1, blocks * width), F32),
            jax.ShapeDtypeStruct(parted, BF16),
            jax.ShapeDtypeStruct(parted, BF16),
        ],
        scratch_shapes=[
            pltpu.VMEM((toks, width), F32),
            pltpu.VMEM((toks, width), F32),
            pltpu.VMEM((width, width), BF16),
            pltpu.VMEM((width, width), BF16),
            pltpu.VMEM((toks, width), BF16),
            pltpu.VMEM((toks, width), BF16),
        ],
        compiler_params=pltpu.CompilerParams(vmem_limit_bytes=VMEM_LIMIT),
        cost_estimate=pl.CostEstimate(flops=15 * 10**9, bytes_accessed=20 * 10**6, transcendentals=3 * 10**6),
        name="ffn",
    )(place, n2, cot, *gathered, bfc)


def attn_backward_body(
    tok, time, hid, out0, out1, dn20, dn21, cot, qkv, probs, weights, vec, *refs, rows
):
    layer_out, dtok, dtime, dbr, dqkv, sums = refs[-6:]
    width = hid.shape[1]
    size = hid.shape[0] // rows

    @pl.when(pl.program_id(0) == 0)
    def _():
        sums[...] = jnp.zeros_like(sums)

    hidden = hid[...]
    layer_out[...] = (hidden + (out0[...].astype(F32) + out1[...].astype(F32)) + vec[7:8, :]).astype(BF16)
    nhat, inv = normalise(hidden)
    dn2 = dn20[...].astype(F32) + dn21[...].astype(F32)
    cotangent = cot[...].astype(F32)
    q = dn2 * vec[5:6, :]
    mean_q = jnp.mean(q, axis=-1, keepdims=True)
    mean_qn = jnp.mean(q * nhat, axis=-1, keepdims=True)
    d_hidden = cotangent + (q - mean_q - nhat * mean_qn) * inv
    dtok[...] = d_hidden
    branch = d_hidden.astype(BF16)
    dbr[...] = branch
    sums[0:1, :] += colsum(dn2 * nhat)
    sums[1:2, :] += colsum(dn2)
    sums[2:3, :] += colsum(branch.astype(F32))
    sums[3:4, :] += colsum(cotangent)
    d_mixed = dot(branch, weights[:, 3 * width : 4 * width], 1, 1).astype(BF16)
    pairs = width // (2 * HD)
    for r in range(rows):
        sl = slice(r * size, (r + 1) * size)
        for p in range(pairs):
            c = 2 * HD * p
            qb = qkv[sl, c : c + 2 * HD] * jnp.asarray(HD**-0.5, BF16)
            k = head_pair(qkv[sl, width + c : width + c + 2 * HD])
            v = head_pair(qkv[sl, 2 * width + c : 2 * width + c + 2 * HD])
            dm = d_mixed[sl, c : c + 2 * HD]
            pr = probs[r, p]
            dp = dot(v, dm, 1, 1)
            halves = []
            for h in range(2):
                pf = pr[h * size : (h + 1) * size].astype(F32)
                dph = dp[h * size : (h + 1) * size]
                halves.append((pf * (dph - jnp.sum(dph * pf, axis=0, keepdims=True))).astype(BF16))
            ds = jnp.concatenate(halves, axis=0)
            dv = own_lanes(dot(pr, dm, 1, 0))
            dk = own_lanes(dot(ds, qb, 1, 0))
            dq = dot(ds, k, 0, 0) * HD**-0.5
            dqkv[sl, c : c + 2 * HD] = dq.astype(BF16)
            dqkv[sl, width + c : width + c + 2 * HD] = dk.astype(BF16)
            dqkv[sl, 2 * width + c : 2 * width + c + 2 * HD] = dv.astype(BF16)
    sums[4:5, :] += colsum(dqkv[:, :width].astype(F32))
    sums[5:6, :] += colsum(dqkv[:, 2 * width :].astype(F32))

    x = tok[...].astype(F32)
    x = jnp.concatenate(
        [x[r * size : (r + 1) * size] + time[r].astype(F32) for r in range(rows)], axis=0
    )
    nhat, inv = normalise(x)
    dn1 = dot(dqkv[...], weights[:, : 3 * width], 1, 1)
    sums[6:7, :] += colsum(dn1 * nhat)
    sums[7:8, :] += colsum(dn1)
    q = dn1 * vec[0:1, :]
    mean_q = jnp.mean(q, axis=-1, keepdims=True)
    mean_qn = jnp.mean(q * nhat, axis=-1, keepdims=True)
    d_tok = dtok[...] + (q - mean_q - nhat * mean_qn) * inv
    dtok[...] = d_tok
    for r in range(rows):
        dtime[r] = colsum(d_tok[r * size : (r + 1) * size])


def attn_backward(tok, time, hid, outs, dn2s, cot, qkv, probs, weights, vec, base, steps, before=(), rows=2):
    row_count, pairs, _, size = probs.shape
    width = hid.shape[1]
    tm = rows * size
    toks = row_count * size
    once = pl.Buffered(buffer_count=1)
    full = lambda s: pl.BlockSpec(s, lambda i: (0,) * len(s), pipeline_mode=once)
    tile = lambda cols: pl.BlockSpec((tm, cols), lambda i: (i + base, 0))
    per_row = pl.BlockSpec((rows, 1, width), lambda i: (i + base, 0, 0))
    return pl.pallas_call(
        functools.partial(attn_backward_body, rows=rows),
        grid=(steps,),
        in_specs=[tile(width), per_row]
        + [tile(width)] * 6
        + [
            tile(3 * width),
            pl.BlockSpec((rows, pairs, 2 * size, size), lambda i: (i + base, 0, 0, 0)),
            full(weights.shape),
            full(vec.shape),
        ]
        + [pl.BlockSpec(memory_space=pl.ANY)] * len(before),
        out_specs=[
            tile(width),
            tile(width),
            per_row,
            tile(width),
            tile(3 * width),
            pl.BlockSpec((8, width), lambda i: (0, 0)),
        ],
        input_output_aliases={12 + k: k for k in range(len(before))},
        out_shape=[
            jax.ShapeDtypeStruct((toks, width), BF16),
            jax.ShapeDtypeStruct((toks, width), F32),
            jax.ShapeDtypeStruct((row_count, 1, width), F32),
            jax.ShapeDtypeStruct((toks, width), BF16),
            jax.ShapeDtypeStruct((toks, 3 * width), BF16),
            jax.ShapeDtypeStruct((8, width), F32),
        ],
        compiler_params=pltpu.CompilerParams(vmem_limit_bytes=VMEM_LIMIT),
        cost_estimate=pl.CostEstimate(flops=6 * 10**9 * steps, bytes_accessed=10 * 10**6 * steps, transcendentals=0),
        name="attn_backward",
    )(tok, time, hid, *outs, *dn2s, cot, qkv, probs, weights, vec, *before)


def collect(vectors, cut, stride, start, piece):
    at = start + piece * stride
    tile, shift = at // 128, at % 128
    lane = lax.broadcasted_iota(jnp.int32, (vectors.shape[0], 128), 1)
    block = vectors[:, tile * 128 : (tile + 1) * 128]
    if shift + cut > 128:
        block = jnp.where(lane >= shift, block, vectors[:, (tile + 1) * 128 : (tile + 2) * 128])
    if shift:
        block = pltpu.roll(block, 128 - shift, 1)
    return jnp.where(lane < cut, block, 0.0)


def weight_grad_body(place, n1, dqkv, att, dbr, sums0, sums1, dbfc0, dbfc1, keep0, send0, keep1, send1):
    rows = keep0.shape[3]
    width = n1.shape[1]
    step = pl.program_id(0)

    def emit(grad, keep, send, at_column):
        tail = (slice(None), slice(at_column, at_column + grad.shape[1]))
        for z in range(Z):
            for y in range(Y):
                for x in range(X):
                    at = ((z * Y + y) * X + x) * CORES * rows
                    even = grad[at : at + rows].astype(BF16)
                    odd = grad[at + rows : at + 2 * rows].astype(BF16)
                    put_blocks(place, z, y, x, even, odd, keep, send, tail)

    for k in range(2):

        @pl.when(step == k)
        def _(k=k):
            emit(dot(n1[...], dqkv[...], 0, 0), keep0, send0, k * width)

    @pl.when(step == 2)
    def _():
        emit(dot(n1[...], dqkv[...], 0, 0), keep1, send1, 0)

    @pl.when(step == 3)
    def _():
        emit(dot(att[...], dbr[...], 0, 0), keep1, send1, width)
        vectors = sums0[...] + sums1[...]
        pad = jnp.zeros((6, dbfc0.shape[1]), F32)
        hidden = jnp.concatenate([dbfc0[...], dbfc1[...], pad], axis=0)

        def block(piece):
            early = collect(hidden, rows, 2 * rows, 0, piece)
            late = collect(hidden, rows, 2 * rows, rows, piece)
            top = collect(vectors, rows, rows, 0, piece)
            rest = [early[:2], late[:2], jnp.zeros((rows - 12, 128), F32)]
            return jnp.concatenate([top] + rest, axis=0).astype(BF16)

        tail = (slice(None), slice(2 * width, 2 * width + 128))
        for z in range(Z):
            for y in range(Y):
                for x in range(X):
                    piece = ((z * Y + y) * X + x) * CORES
                    put_blocks(place, z, y, x, block(piece), block(piece + 1), keep1, send1, tail)


def weight_grad(place, n1, dqkv, att, dbr, sums0, sums1, dbfc0, dbfc1):
    toks, width = n1.shape
    rows = width // PIECES
    once = pl.Buffered(buffer_count=1)
    full = lambda a: pl.BlockSpec(a.shape, lambda j: (0, 0), pipeline_mode=once)
    shapes = [(Y, X, Z, rows, columns) for columns in (2 * width, 2 * width + 128) for _ in range(2)]
    return pl.pallas_call(
        weight_grad_body,
        grid=(4,),
        in_specs=[
            pl.BlockSpec(memory_space=pltpu.SMEM),
            full(n1),
            pl.BlockSpec((toks, width), lambda j: (0, jnp.minimum(j, 2))),
        ]
        + [full(e) for e in (att, dbr, sums0, sums1, dbfc0, dbfc1)],
        out_specs=[pl.BlockSpec(shape, lambda j: (0,) * 5) for shape in shapes],
        out_shape=[jax.ShapeDtypeStruct(shape, BF16) for shape in shapes],
        compiler_params=pltpu.CompilerParams(vmem_limit_bytes=VMEM_LIMIT),
        cost_estimate=pl.CostEstimate(flops=5 * 10**9, bytes_accessed=16 * 10**6, transcendentals=0),
        name="weight_grad",
    )(place, n1, dqkv, att, dbr, sums0, sums1, dbfc0, dbfc1)


def flip(position):
    return lambda i: i ^ position


def exchange(array, partner):
    return lax.ppermute(array, "dp", [(i, partner(i)) for i in range(PIECES)])


def plane_partner(stage):
    def partner(i):
        along_y = (i % 2 == 0) == (stage == "first")
        return i ^ (4 if along_y else 2)

    return partner


class CubeGather:
    def __init__(self, block):
        self.ready, self.came, self.step, self.parts = block, None, 0, None

    def send(self):
        if self.step == 0:
            self.came = [exchange(self.ready, lambda i, k=k: (i + 8 * k) % PIECES) for k in range(1, Z)]
        elif self.step == 1:
            self.came = [exchange(self.ready, plane_partner("second"))]
        elif self.step == 2:
            self.came = [exchange(self.ready, plane_partner("first"))]
        self.step += 1

    def take(self):
        if self.step < 3:
            self.ready = jnp.stack([self.ready] + list(self.came))
        else:
            self.parts = (self.ready, self.came[0])

    def share(self):
        self.parts = self.parts + tuple(exchange(half, flip(1)) for half in self.parts)


def meet(*things):
    return lax.optimization_barrier(things)


class CubeSum:
    def __init__(self, keep, send):
        self.grads, self.keep, self.ahead = (keep, send), keep, send
        self.came, self.first, self.second, self.rest = None, None, None, None

    def part(self, *at):
        total = self.keep[at].astype(F32) + self.came[at].astype(F32)
        if self.first is not None:
            total = total + self.first[at[1:]].astype(F32)
        if self.second is not None:
            total = total + self.second[at[2:]].astype(F32)
        return total

    def send(self):
        if self.came is None:
            self.came = exchange(self.ahead, flip(1))
        elif self.first is None:
            self.ahead = self.part(1).astype(BF16)
            self.first = exchange(self.ahead, plane_partner("first"))
        elif self.second is None:
            self.ahead = self.part(0, 1).astype(BF16)
            self.second = exchange(self.ahead, plane_partner("second"))
        else:
            self.ahead = [self.part(0, 0, k).astype(BF16) for k in range(1, Z)]
            self.rest = [
                exchange(block, lambda i, k=k: (i - 8 * k) % PIECES) for k, block in enumerate(self.ahead, 1)
            ]

    def total(self):
        return self.part(0, 0, 0) + sum(block.astype(F32) for block in self.rest)


def hold(first, *then):
    return tuple(lax.optimization_barrier((first, one))[1] for one in then)


def sum_over(values, *bits):
    for bit in bits:
        values = values + exchange(values, flip(bit))
    return values


def cut_any(blocks):
    every = blocks.reshape((Z, Y, X, CORES) + blocks.shape[1:])
    deep = jnp.array([0, 3, 2, 1])
    rest = tuple(range(3, every.ndim - 1))
    even = jnp.transpose(every[:, :, :, 0], (1, 2, 0) + rest)[:, :, deep]
    odd = jnp.transpose(every[:, :, :, 1], (2, 1, 0) + rest)[:, :, deep]
    return even[0], even[1], odd[0], odd[1]


def natural_blocks(keep, send):
    deep = jnp.array([0, 3, 2, 1])
    rest = tuple(range(3, keep.ndim))
    even = jnp.transpose(keep[:, :, deep], (2, 0, 1) + rest)
    odd = jnp.transpose(send[:, :, deep], (2, 1, 0) + rest)
    both = jnp.stack([even, odd], axis=3)
    return both.reshape((PIECES,) + both.shape[4:])


def on_device(
    tokens,
    segment_ids,
    time_embed,
    norm1_gain,
    norm1_shift,
    w_qkv,
    b_query,
    b_value,
    w_proj,
    b_proj,
    norm2_gain,
    norm2_shift,
    w_fc,
    b_fc,
    w_out,
    b_out,
    cotangent,
):
    row_count, row_len, width = tokens.shape
    toks = row_count * row_len
    devices = lax.axis_size("dp")
    cube = devices == PIECES
    rank = lax.axis_index("dp")
    grad_scale = 1.0 / math.sqrt(toks * devices)
    own = w_proj.shape[0]
    ratio = b_fc.shape[0] // own
    if cube:
        place = jnp.stack([rank // 8, (rank // 4) % 2, (rank // 2) % 2, rank % 2]).astype(jnp.int32)
    else:
        place = jnp.zeros((4,), jnp.int32)

    small = jnp.concatenate(
        [norm1_gain, norm1_shift, b_query, b_value, b_proj, norm2_gain, norm2_shift, b_out, b_fc]
    ).reshape(8 + ratio, own)
    order = list(range(8)) + [8 + 2 * h + k for k in range(ratio // 2) for h in range(2)]
    small = jnp.concatenate([small[v : v + 1] for v in order], axis=0)
    cut = width // PIECES
    halves = 2
    blocks = ratio // halves
    ffn_fc = lambda w: w.reshape(-1, PIECES, halves, blocks * cut).transpose(2, 0, 1, 3).reshape(halves, -1, blocks, width)
    if cube:
        ffn_block = jnp.concatenate(
            [ffn_fc(w_fc).transpose(0, 2, 1, 3), w_out.reshape(halves, blocks, own, width)], axis=1
        )
        small = jnp.pad(small, ((0, own - small.shape[0]), (0, 128 - own)))
        attn_gather = CubeGather(jnp.concatenate([w_qkv, w_proj, small], axis=1))
        early, late = CubeGather(ffn_block[0]), CubeGather(ffn_block[1])
        attn_gather.send()
        early.send()
        attn_gather.came, late.ready = meet(attn_gather.came, late.ready)
        attn_gather.take()
        attn_gather.send()
        late.send()
        attn_gather.came, early.came = meet(attn_gather.came, early.came)
        attn_gather.take()
        early.take()
        attn_gather.send()
        early.send()
        attn_gather.came, early.came, late.came = meet(attn_gather.came, early.came, late.came)
        attn_gather.take()
        attn_gather.share()
        early.take()
        late.take()
        early.send()
        late.send()
        attn_full = attn_gather.parts
    else:
        whole = lambda w: lax.all_gather(w, "dp", axis=0, tiled=True)
        natural = whole(small.T.reshape(own, -1))
        vectors = natural[:, :8].T
        hidden_bias = whole(b_fc).reshape(PIECES, ratio, cut)
        small = jnp.concatenate(
            [vectors.reshape(8, PIECES, cut).transpose(1, 0, 2), hidden_bias[:, jnp.array([0, 2, 1, 3])]], axis=1
        )
        small = jnp.pad(small, ((0, 0), (0, cut - small.shape[1]), (0, 128 - cut))).reshape(width, 128)
        attn_full = jnp.concatenate([whole(w_qkv), whole(w_proj), small], axis=1)
        attn_full = cut_any(attn_full.reshape(PIECES, cut, -1))
        fc_full = ffn_fc(whole(w_fc)).reshape(halves, PIECES, cut, blocks, width).transpose(1, 0, 3, 2, 4)
        out_full = whole(w_out).reshape(PIECES, halves, blocks, cut, width)
        ffn_full = jnp.concatenate([fc_full, out_full], axis=2)
        early, late = [cut_any(ffn_full[:, h].reshape(PIECES, -1, cut, width)) for h in range(halves)]

    flat = tokens.reshape(toks, width)
    times = time_embed.reshape(row_count, 1, width)
    segments = segment_ids.reshape(row_count, 1, row_len)
    cot = cotangent.reshape(toks, width)
    if cube:
        (segments,) = hold(late.ready, *hold(early.ready, segments))
    n1, qkv, probs, att, hid, n2, attn_w, vec, bfc = attn_forward(place, flat, times, segments, attn_full)
    if cube:
        n2, early.came, late.came = meet(n2, early.came, late.came)
        early.take()
        early.share()
        late.take()
        late.send()
        (n2,) = hold(late.ready, n2)
        early = early.parts
    out0, dn20, dbfc0, *grads0 = ffn(place, n2, cot, early, bfc, 0)
    sum0 = CubeSum(*grads0)
    if cube:
        out0, late.came, sum0.ahead = meet(out0, late.came, sum0.ahead)
        late.take()
        late.share()
        sum0.send()
        sum0.send()
        (n2,) = hold(sum0.ahead, n2)
        late = late.parts
    out1, dn21, dbfc1, *grads1 = ffn(place, n2, cot, late, bfc, 1)
    sum1 = CubeSum(*grads1)
    backward = lambda hid, base, steps, before: attn_backward(
        flat, times, hid, (out0, out1), (dn20, dn21), cot, qkv, probs, attn_w, vec, base, steps, before
    )
    steps = row_count // 2
    if cube:
        out1, sum1.ahead, sum0.first = meet(out1, sum1.ahead, sum0.first)
        sum1.send()
        sum0.send()
        (hid,) = hold(sum0.ahead, hid)
    *before, sums0 = backward(hid, 0, 1, ())
    if cube:
        sums0, sum0.second, sum1.came = meet(sums0, sum0.second, sum1.came)
        sum0.send()
        sum1.send()
        (hid,) = hold(sum1.ahead, *hold(sum0.ahead[0], hid))
    layer_out, d_tokens, d_time, dbr, dqkv, sums1 = backward(hid, 1, steps - 1, before)
    if cube:
        dqkv, sum0.rest, sum1.first = meet(dqkv, sum0.rest, sum1.first)
        sum1.send()
        (dqkv,) = hold(sum1.ahead, dqkv)
    grads = weight_grad(place, n1, dqkv, att, dbr, sums0, sums1, dbfc0, dbfc1)
    attn0, attn1 = CubeSum(*grads[:2]), CubeSum(*grads[2:])
    if cube:
        attn0.ahead, attn1.ahead, sum1.second = meet(attn0.ahead, attn1.ahead, sum1.second)
        attn0.send()
        attn1.send()
        attn0.send()
        attn1.send()
        (sum1.second,) = hold(attn1.ahead, sum1.second)
        sum1.send()
        attn0.send()
        attn1.send()
        attn0.send()
        attn1.send()
        sum1.rest = hold(attn1.ahead[0], *sum1.rest)
        attn0.rest = hold(attn1.ahead[0], *attn0.rest)
        own_ffn = jnp.stack([sum0.total(), sum1.total()])
        own_attn = jnp.concatenate([attn0.total(), attn1.total()], axis=1)
        own_out = own_ffn[:, blocks:].reshape(ratio * own, width)
        own_fc = own_ffn[:, :blocks].transpose(2, 0, 1, 3).reshape(own, halves, PIECES, blocks * own)
        own_fc = own_fc.transpose(0, 2, 1, 3).reshape(own, ratio * width)
        vectors = own_attn[:, 4 * width :]
        mine = vectors[:8, :own]
        own_bfc = jnp.concatenate([vectors[8 + v, :own] for v in (0, 2, 1, 3)])
    else:
        scatter = lambda g: lax.psum_scatter(g, "dp", scatter_dimension=0, tiled=True)
        grads = jnp.concatenate([natural_blocks(*a.grads) for a in (attn0, attn1)], axis=-1).astype(F32)
        own_attn = scatter(grads[:, :, : 4 * width].reshape(width, -1))
        vectors = lax.psum(grads[:, :, 4 * width : 4 * width + cut], "dp")
        mine = lax.dynamic_slice(
            vectors[:, :8].transpose(1, 0, 2).reshape(8, width), (0, rank * own), (8, own)
        )
        hidden_grad = vectors[:, jnp.array([8, 10, 9, 11])].reshape(-1)
        own_bfc = lax.dynamic_slice(hidden_grad, (rank * own * ratio,), (own * ratio,))
        grads = jnp.stack([natural_blocks(*s.grads) for s in (sum0, sum1)], axis=1).astype(F32)
        out_grad = grads[:, :, blocks:].reshape(ratio * width, width)
        own_out = scatter(out_grad)
        fc_grad = grads[:, :, :blocks].transpose(0, 3, 1, 2, 4).reshape(width, halves, PIECES, blocks * cut)
        own_fc = scatter(fc_grad.transpose(0, 2, 1, 3).reshape(width, ratio * width))
    mine, own_bfc = mine * grad_scale, own_bfc * grad_scale
    own_attn = own_attn * grad_scale
    return (
        layer_out.reshape(tokens.shape),
        d_tokens.reshape(tokens.shape),
        d_time.reshape(time_embed.shape),
        mine[6],
        mine[7],
        own_attn[:, : 3 * width],
        mine[4],
        mine[5],
        own_attn[:, 3 * width : 4 * width],
        mine[2],
        mine[0],
        mine[1],
        own_fc * grad_scale,
        own_bfc,
        own_out * grad_scale,
        mine[3],
    )


def solution(mesh):
    in_specs = (
        P("dp", None, None),
        P("dp", None),
        P("dp", None),
        P("dp"),
        P("dp"),
        P("dp", None),
        P("dp"),
        P("dp"),
        P("dp", None),
        P("dp"),
        P("dp"),
        P("dp"),
        P("dp", None),
        P("dp"),
        P("dp", None),
        P("dp"),
        P("dp", None, None),
    )
    out_specs = (
        P("dp", None, None),
        P("dp", None, None),
        P("dp", None),
        P("dp"),
        P("dp"),
        P("dp", None),
        P("dp"),
        P("dp"),
        P("dp", None),
        P("dp"),
        P("dp"),
        P("dp"),
        P("dp", None),
        P("dp"),
        P("dp", None),
        P("dp"),
    )
    return jax.shard_map(
        on_device, mesh=mesh, in_specs=in_specs, out_specs=out_specs, check_vma=False
    )
```

```python
import functools
import math

import jax
import jax.numpy as jnp
from jax import lax
from jax.experimental import pallas as pl
from jax.experimental.pallas import tpu as pltpu
from jax.sharding import PartitionSpec as P

HD = 64
EPS = 1e-05
MASKED = -1e30
F32 = jnp.float32
BF16 = jnp.bfloat16
VMEM_LIMIT = 48 * 1024 * 1024
FFN_VMEM_LIMIT = 40 * 1024 * 1024


def dot(a, b, a_dim, b_dim):
    return lax.dot_general(a, b, (((a_dim,), (b_dim,)), ((), ())), preferred_element_type=F32)


def normalise(values):
    centered = values - jnp.mean(values, axis=-1, keepdims=True)
    spread = jnp.mean(centered * centered, axis=-1, keepdims=True)
    inv = lax.rsqrt(spread + EPS)
    return centered * inv, inv


def head_pair(block):
    lane = lax.broadcasted_iota(jnp.int32, block.shape, 1)
    zero = jnp.zeros_like(block)
    return jnp.concatenate([jnp.where(lane < HD, block, zero), jnp.where(lane >= HD, block, zero)], axis=0)


def own_lanes(stacked):
    half = stacked.shape[0] // 2
    lane = lax.broadcasted_iota(jnp.int32, (half, stacked.shape[1]), 1)
    return jnp.where(lane < HD, stacked[:half], stacked[half:])


def row_mask(seg_row):
    size = seg_row.shape[1]
    across = jnp.broadcast_to(seg_row.astype(F32), (size, size))
    return jnp.where(across == across.T, 0.0, MASKED)


def colsum(v):
    return jnp.sum(v, axis=0, keepdims=True)


Z, Y, X, CORES = 4, 2, 2, 2
PIECES = Z * Y * X * CORES


def merge_rows(blocks):
    count, rows, width = blocks.shape
    return blocks.astype(F32).reshape(count * rows, width).astype(BF16)


def slots(place, z, y, x):
    ys, xs = y ^ place[1], x ^ place[2]
    first = jnp.where(place[3] == 0, ys, xs)
    second = jnp.where(place[3] == 0, xs, ys)
    return first, second, (place[0] - z + Z) % Z


def put_blocks(place, z, y, x, even, odd, keep, send, tail=()):
    first, second, deep = slots(place, z, y, x)
    mine = place[3] == 0
    keep[(first, second, deep) + tail] = jnp.where(mine, even, odd)
    send[(second, first, deep) + tail] = jnp.where(mine, odd, even)


def pick(place, parts, z, y, x, tail=()):
    mine0, mine1, other0, other1 = parts
    first, second, deep = slots(place, z, y, x)
    mine = jnp.where(first == 0, mine0[(second, deep) + tail], mine1[(second, deep) + tail])
    other = jnp.where(second == 0, other0[(first, deep) + tail], other1[(first, deep) + tail])
    even = place[3] == 0
    return jnp.where(even, mine, other), jnp.where(even, other, mine)


def spread(small, cut, row, stride, start, length):
    lane = lax.broadcasted_iota(jnp.int32, (8, 128), 1)
    tiles = [jnp.zeros((8, 128), F32) for _ in range(length // 128)]
    for i in range(PIECES):
        at = start + i * stride
        tile, shift = at // 128, at % 128
        block = small[i * cut + row : i * cut + row + 8]
        if shift:
            block = pltpu.roll(block, shift, 1)
        if shift + cut <= 128:
            tiles[tile] = tiles[tile] + block
        else:
            tiles[tile] = tiles[tile] + jnp.where(lane >= shift, block, 0.0)
            tiles[tile + 1] = tiles[tile + 1] + jnp.where(lane < shift, block, 0.0)
    return jnp.concatenate(tiles, axis=1)


def attn_forward_body(
    place, tok, time, seg, mine0, mine1, other0, other1, n1, qkv, probs, att, hid, n2, weights, vec, bfc, *, rows
):
    size = tok.shape[0] // rows
    width = tok.shape[1]

    @pl.when(pl.program_id(0) == 0)
    def _():
        for z in range(Z):
            for y in range(Y):
                for x in range(X):
                    both = pick(place, (mine0, mine1, other0, other1), z, y, x)
                    both = jnp.concatenate([b.astype(F32) for b in both], axis=0)
                    step = both.shape[0]
                    at = ((z * Y + y) * X + x) * step
                    weights[at : at + step, :] = both.astype(BF16)
        small = weights[:, 4 * width :].astype(F32)
        cut = width // PIECES
        vec[...] = spread(small, cut, 0, cut, 0, width)
        early = spread(small, cut, 8, 2 * cut, 0, bfc.shape[1])
        late = spread(small, cut, 8, 2 * cut, cut, bfc.shape[1])
        bfc[...] = early[0:2] + late[2:4]

    x = tok[...].astype(F32)
    x = jnp.concatenate(
        [x[r * size : (r + 1) * size] + time[r].astype(F32) for r in range(rows)], axis=0
    )
    nhat, _ = normalise(x)
    normed = (nhat * vec[0:1, :] + vec[1:2, :]).astype(BF16)
    n1[...] = normed
    for part in range(3):
        cols = slice(part * width, (part + 1) * width)
        block = dot(normed, weights[:, cols], 1, 0)
        if part == 0:
            block = block + vec[2:3, :]
        if part == 2:
            block = block + vec[3:4, :]
        qkv[:, cols] = block.astype(BF16)
    pairs = width // (2 * HD)
    for r in range(rows):
        sl = slice(r * size, (r + 1) * size)
        mask = row_mask(seg[r])
        for p in range(pairs):
            c = 2 * HD * p
            q = qkv[sl, c : c + 2 * HD] * jnp.asarray(HD**-0.5, BF16)
            k = head_pair(qkv[sl, width + c : width + c + 2 * HD])
            v = head_pair(qkv[sl, 2 * width + c : 2 * width + c + 2 * HD])
            s = dot(k, q, 1, 1)
            halves = []
            for h in range(2):
                sh = s[h * size : (h + 1) * size] + mask
                e = jnp.exp(sh - jnp.max(sh, axis=0, keepdims=True))
                halves.append((e * (1.0 / jnp.sum(e, axis=0, keepdims=True))).astype(BF16))
            pr = jnp.concatenate(halves, axis=0)
            probs[r, p] = pr
            att[sl, c : c + 2 * HD] = dot(pr, v, 0, 0).astype(BF16)
    hidden = x + dot(att[...], weights[:, 3 * width : 4 * width], 1, 0) + vec[4:5, :]
    hid[...] = hidden
    nhat2, _ = normalise(hidden)
    n2[...] = (nhat2 * vec[5:6, :] + vec[6:7, :]).astype(BF16)


def attn_forward(place, tok, time, seg, gathered, rows=2):
    row_count = seg.shape[0]
    toks, width = tok.shape
    size = toks // row_count
    tm = rows * size
    pairs = width // (2 * HD)
    wide = gathered[0].shape[-1]
    full = lambda s: pl.BlockSpec(s, lambda i: (0,) * len(s))
    tile = lambda cols: pl.BlockSpec((tm, cols), lambda i: (i, 0))
    return pl.pallas_call(
        functools.partial(attn_forward_body, rows=rows),
        grid=(row_count // rows,),
        in_specs=[
            pl.BlockSpec(memory_space=pltpu.SMEM),
            tile(width),
            pl.BlockSpec((rows, 1, width), lambda i: (i, 0, 0)),
            pl.BlockSpec((rows, 1, size), lambda i: (i, 0, 0)),
        ]
        + [full(g.shape) for g in gathered],
        out_specs=[
            tile(width),
            tile(3 * width),
            pl.BlockSpec((rows, pairs, 2 * size, size), lambda i: (i, 0, 0, 0)),
            tile(width),
            tile(width),
            tile(width),
            full((width, wide)),
            full((8, width)),
            full((2, 2 * width)),
        ],
        out_shape=[
            jax.ShapeDtypeStruct((toks, width), BF16),
            jax.ShapeDtypeStruct((toks, 3 * width), BF16),
            jax.ShapeDtypeStruct((row_count, pairs, 2 * size, size), BF16),
            jax.ShapeDtypeStruct((toks, width), BF16),
            jax.ShapeDtypeStruct((toks, width), F32),
            jax.ShapeDtypeStruct((toks, width), BF16),
            jax.ShapeDtypeStruct((width, wide), BF16),
            jax.ShapeDtypeStruct((8, width), F32),
            jax.ShapeDtypeStruct((2, 2 * width), F32),
        ],
        compiler_params=pltpu.CompilerParams(vmem_limit_bytes=VMEM_LIMIT),
        cost_estimate=pl.CostEstimate(flops=16 * 10**9, bytes_accessed=20 * 10**6, transcendentals=2 * 10**6),
        name="attn_forward",
    )(place, tok, time, seg, *gathered)


def ffn_body(
    place, n2, cot, mine0, mine1, other0, other1, bfc, sum_out, sum_dn2, dbfc, keep, send, acc_out, acc_dn2, fc_s, out_s, act_s, dpre_s, *, tm, sub, half
):
    step = pl.program_id(0)

    @pl.when(step == 0)
    def _():
        acc_out[...] = jnp.zeros_like(acc_out)
        acc_dn2[...] = jnp.zeros_like(acc_dn2)

    gathered = (mine0, mine1, other0, other1)
    blocks, rows = 2, mine0.shape[-2]
    for z in range(Z):
        for y in range(Y):
            for x in range(X):
                both = pick(place, gathered, z, y, x, (step,))
                at = ((z * Y + y) * X + x) * CORES * rows
                fc_s[at : at + CORES * rows, :] = merge_rows(jnp.stack(both))
    for z in range(Z // blocks):
        for y in range(Y):
            for x in range(X):
                both = pick(place, gathered, step * (Z // blocks) + z, y, x, (slice(blocks, 2 * blocks),))
                at = ((z * Y + y) * X + x) * CORES * blocks * rows
                out_s[at : at + CORES * blocks * rows, :] = merge_rows(jnp.concatenate(both, axis=0))
    chunk = fc_s.shape[1]
    for part in range(chunk // sub):
        cols = slice(part * sub, (part + 1) * sub)
        bias = bfc[half : half + 1, cols]
        db = jnp.zeros_like(bias)
        for m in range(n2.shape[0] // tm):
            sl = slice(m * tm, (m + 1) * tm)
            pre = dot(n2[sl, :], fc_s[:, cols], 1, 0) + bias
            d_act = dot(cot[sl, :], out_s[cols, :], 1, 1)
            cdf = 0.5 * lax.erf(pre * math.sqrt(0.5)) + 0.5
            density = jnp.exp(pre * pre * -0.5) * (1.0 / math.sqrt(2.0 * math.pi))
            act = (pre * cdf).astype(BF16)
            d_pre = (d_act * (cdf + pre * density)).astype(BF16)
            act_s[sl, cols] = act
            dpre_s[sl, cols] = d_pre
            db = db + jnp.sum(d_pre.astype(F32), axis=0, keepdims=True)
            acc_out[sl, :] += dot(act, out_s[cols, :], 1, 0)
            acc_dn2[sl, :] += dot(d_pre, fc_s[:, cols], 1, 1)
        dbfc[:, cols] = db

    @pl.when(step == pl.num_programs(0) - 1)
    def _():
        sum_out[...] = acc_out[...].astype(BF16)
        sum_dn2[...] = acc_dn2[...].astype(BF16)

    grad = dot(act_s[...], cot[...], 0, 0)
    planes = Z // blocks
    for z in range(planes):
        for y in range(Y):
            for x in range(X):
                for b in range(blocks):
                    at = (((z * Y + y) * X + x) * CORES * blocks + b) * rows
                    even = grad[at : at + rows].astype(BF16)
                    odd = grad[at + blocks * rows : at + (blocks + 1) * rows].astype(BF16)
                    put_blocks(place, step * planes + z, y, x, even, odd, keep, send, (blocks + b,))
    grad = dot(n2[...], dpre_s[...], 0, 0)
    for z in range(Z):
        for y in range(Y):
            for x in range(X):
                at = ((z * Y + y) * X + x) * CORES * rows
                even = grad[at : at + rows].astype(BF16)
                odd = grad[at + rows : at + 2 * rows].astype(BF16)
                put_blocks(place, z, y, x, even, odd, keep, send, (step,))


def ffn(place, n2, cot, gathered, bfc, half, tm=512, sub=768):
    toks, width = n2.shape
    rows = width // PIECES
    blocks = 2
    count = 2 * blocks
    once = pl.Buffered(buffer_count=1)
    full = lambda s: pl.BlockSpec(s, lambda j: (0,) * len(s), pipeline_mode=once)
    whole = lambda s: pl.BlockSpec(s, lambda j: (0,) * len(s))
    parted = (Y, X, Z, count, rows, width)
    return pl.pallas_call(
        functools.partial(ffn_body, tm=tm, sub=sub, half=half),
        grid=(blocks,),
        in_specs=[
            pl.BlockSpec(memory_space=pltpu.SMEM),
            full((toks, width)),
            full((toks, width)),
        ]
        + [full(g.shape) for g in gathered]
        + [
            pl.BlockSpec((2, width), lambda j: (0, j)),
        ],
        out_specs=[
            whole((toks, width)),
            whole((toks, width)),
            pl.BlockSpec((1, width), lambda j: (0, j)),
            whole(parted),
            whole(parted),
        ],
        out_shape=[
            pltpu.HBM((toks, width), BF16),
            pltpu.HBM((toks, width), BF16),
            jax.ShapeDtypeStruct((1, blocks * width), F32),
            jax.ShapeDtypeStruct(parted, BF16),
            jax.ShapeDtypeStruct(parted, BF16),
        ],
        scratch_shapes=[
            pltpu.VMEM((toks, width), F32),
            pltpu.VMEM((toks, width), F32),
            pltpu.VMEM((width, width), BF16),
            pltpu.VMEM((width, width), BF16),
            pltpu.VMEM((toks, width), BF16),
            pltpu.VMEM((toks, width), BF16),
        ],
        compiler_params=pltpu.CompilerParams(vmem_limit_bytes=FFN_VMEM_LIMIT),
        cost_estimate=pl.CostEstimate(flops=15 * 10**9, bytes_accessed=20 * 10**6, transcendentals=3 * 10**6),
        name="ffn",
    )(place, n2, cot, *gathered, bfc)


def attn_backward_body(
    tok, time, hid, out0, out1, dn20, dn21, cot, qkv, probs, weights, vec, layer_out, dtok, dtime, dbr, dqkv, sums, *, rows
):
    width = hid.shape[1]
    size = hid.shape[0] // rows

    @pl.when(pl.program_id(0) == 0)
    def _():
        sums[...] = jnp.zeros_like(sums)

    hidden = hid[...]
    layer_out[...] = (hidden + (out0[...].astype(F32) + out1[...].astype(F32)) + vec[7:8, :]).astype(BF16)
    nhat, inv = normalise(hidden)
    dn2 = dn20[...].astype(F32) + dn21[...].astype(F32)
    cotangent = cot[...].astype(F32)
    q = dn2 * vec[5:6, :]
    mean_q = jnp.mean(q, axis=-1, keepdims=True)
    mean_qn = jnp.mean(q * nhat, axis=-1, keepdims=True)
    d_hidden = cotangent + (q - mean_q - nhat * mean_qn) * inv
    dtok[...] = d_hidden
    branch = d_hidden.astype(BF16)
    dbr[...] = branch
    sums[0:1, :] += colsum(dn2 * nhat)
    sums[1:2, :] += colsum(dn2)
    sums[2:3, :] += colsum(branch.astype(F32))
    sums[3:4, :] += colsum(cotangent)
    d_mixed = dot(branch, weights[:, 3 * width : 4 * width], 1, 1).astype(BF16)
    pairs = width // (2 * HD)
    for r in range(rows):
        sl = slice(r * size, (r + 1) * size)
        for p in range(pairs):
            c = 2 * HD * p
            qb = qkv[sl, c : c + 2 * HD] * jnp.asarray(HD**-0.5, BF16)
            k = head_pair(qkv[sl, width + c : width + c + 2 * HD])
            v = head_pair(qkv[sl, 2 * width + c : 2 * width + c + 2 * HD])
            dm = d_mixed[sl, c : c + 2 * HD]
            pr = probs[r, p]
            dp = dot(v, dm, 1, 1)
            halves = []
            for h in range(2):
                pf = pr[h * size : (h + 1) * size].astype(F32)
                dph = dp[h * size : (h + 1) * size]
                halves.append((pf * (dph - jnp.sum(dph * pf, axis=0, keepdims=True))).astype(BF16))
            ds = jnp.concatenate(halves, axis=0)
            dv = own_lanes(dot(pr, dm, 1, 0))
            dk = own_lanes(dot(ds, qb, 1, 0))
            dq = dot(ds, k, 0, 0) * HD**-0.5
            dqkv[sl, c : c + 2 * HD] = dq.astype(BF16)
            dqkv[sl, width + c : width + c + 2 * HD] = dk.astype(BF16)
            dqkv[sl, 2 * width + c : 2 * width + c + 2 * HD] = dv.astype(BF16)
    sums[4:5, :] += colsum(dqkv[:, :width].astype(F32))
    sums[5:6, :] += colsum(dqkv[:, 2 * width :].astype(F32))

    x = tok[...].astype(F32)
    x = jnp.concatenate(
        [x[r * size : (r + 1) * size] + time[r].astype(F32) for r in range(rows)], axis=0
    )
    nhat, inv = normalise(x)
    dn1 = dot(dqkv[...], weights[:, : 3 * width], 1, 1)
    sums[6:7, :] += colsum(dn1 * nhat)
    sums[7:8, :] += colsum(dn1)
    q = dn1 * vec[0:1, :]
    mean_q = jnp.mean(q, axis=-1, keepdims=True)
    mean_qn = jnp.mean(q * nhat, axis=-1, keepdims=True)
    d_tok = dtok[...] + (q - mean_q - nhat * mean_qn) * inv
    dtok[...] = d_tok
    for r in range(rows):
        dtime[r] = colsum(d_tok[r * size : (r + 1) * size])


def attn_backward(tok, time, hid, outs, dn2s, cot, qkv, probs, weights, vec, rows=2):
    row_count, pairs, _, size = probs.shape
    width = hid.shape[1]
    tm = rows * size
    toks = row_count * size
    steps = row_count // rows
    once = pl.Buffered(buffer_count=1)
    full = lambda s: pl.BlockSpec(s, lambda i: (0,) * len(s), pipeline_mode=once)
    tile = lambda cols: pl.BlockSpec((tm, cols), lambda i: (i, 0))
    per_row = pl.BlockSpec((rows, 1, width), lambda i: (i, 0, 0))
    return pl.pallas_call(
        functools.partial(attn_backward_body, rows=rows),
        grid=(steps,),
        in_specs=[tile(width), per_row]
        + [tile(width)] * 6
        + [
            tile(3 * width),
            pl.BlockSpec((rows, pairs, 2 * size, size), lambda i: (i, 0, 0, 0)),
            full(weights.shape),
            full(vec.shape),
        ],
        out_specs=[
            tile(width),
            tile(width),
            per_row,
            tile(width),
            tile(3 * width),
            pl.BlockSpec((8, width), lambda i: (0, 0)),
        ],
        out_shape=[
            jax.ShapeDtypeStruct((toks, width), BF16),
            jax.ShapeDtypeStruct((toks, width), F32),
            jax.ShapeDtypeStruct((row_count, 1, width), F32),
            jax.ShapeDtypeStruct((toks, width), BF16),
            jax.ShapeDtypeStruct((toks, 3 * width), BF16),
            jax.ShapeDtypeStruct((8, width), F32),
        ],
        compiler_params=pltpu.CompilerParams(vmem_limit_bytes=VMEM_LIMIT),
        cost_estimate=pl.CostEstimate(flops=6 * 10**9 * steps, bytes_accessed=10 * 10**6 * steps, transcendentals=0),
        name="attn_backward",
    )(tok, time, hid, *outs, *dn2s, cot, qkv, probs, weights, vec)


def collect(vectors, cut, stride, start, piece):
    at = start + piece * stride
    tile, shift = at // 128, at % 128
    lane = lax.broadcasted_iota(jnp.int32, (vectors.shape[0], 128), 1)
    block = vectors[:, tile * 128 : (tile + 1) * 128]
    if shift + cut > 128:
        block = jnp.where(lane >= shift, block, vectors[:, (tile + 1) * 128 : (tile + 2) * 128])
    if shift:
        block = pltpu.roll(block, 128 - shift, 1)
    return jnp.where(lane < cut, block, 0.0)


def weight_grad_body(place, n1, dqkv, att, dbr, sums, dbfc0, dbfc1, keep0, send0, keep1, send1):
    rows = keep0.shape[3]
    width = n1.shape[1]
    step = pl.program_id(0)

    def emit(grad, keep, send, at_column):
        tail = (slice(None), slice(at_column, at_column + grad.shape[1]))
        for z in range(Z):
            for y in range(Y):
                for x in range(X):
                    at = ((z * Y + y) * X + x) * CORES * rows
                    even = grad[at : at + rows].astype(BF16)
                    odd = grad[at + rows : at + 2 * rows].astype(BF16)
                    put_blocks(place, z, y, x, even, odd, keep, send, tail)

    for k in range(2):

        @pl.when(step == k)
        def _(k=k):
            emit(dot(n1[...], dqkv[...], 0, 0), keep0, send0, k * width)

    @pl.when(step == 2)
    def _():
        emit(dot(n1[...], dqkv[...], 0, 0), keep1, send1, 0)

    @pl.when(step == 3)
    def _():
        emit(dot(att[...], dbr[...], 0, 0), keep1, send1, width)
        vectors = sums[...]
        pad = jnp.zeros((6, dbfc0.shape[1]), F32)
        hidden = jnp.concatenate([dbfc0[...], dbfc1[...], pad], axis=0)

        def block(piece):
            early = collect(hidden, rows, 2 * rows, 0, piece)
            late = collect(hidden, rows, 2 * rows, rows, piece)
            top = collect(vectors, rows, rows, 0, piece)
            rest = [early[:2], late[:2], jnp.zeros((rows - 12, 128), F32)]
            return jnp.concatenate([top] + rest, axis=0).astype(BF16)

        tail = (slice(None), slice(2 * width, 2 * width + 128))
        for z in range(Z):
            for y in range(Y):
                for x in range(X):
                    piece = ((z * Y + y) * X + x) * CORES
                    put_blocks(place, z, y, x, block(piece), block(piece + 1), keep1, send1, tail)


def weight_grad(place, n1, dqkv, att, dbr, sums, dbfc0, dbfc1):
    toks, width = n1.shape
    rows = width // PIECES
    once = pl.Buffered(buffer_count=1)
    full = lambda a: pl.BlockSpec(a.shape, lambda j: (0, 0), pipeline_mode=once)
    shapes = [(Y, X, Z, rows, columns) for columns in (2 * width, 2 * width + 128) for _ in range(2)]
    return pl.pallas_call(
        weight_grad_body,
        grid=(4,),
        in_specs=[
            pl.BlockSpec(memory_space=pltpu.SMEM),
            full(n1),
            pl.BlockSpec((toks, width), lambda j: (0, jnp.minimum(j, 2))),
        ]
        + [full(e) for e in (att, dbr, sums, dbfc0, dbfc1)],
        out_specs=[pl.BlockSpec(shape, lambda j: (0,) * 5) for shape in shapes],
        out_shape=[jax.ShapeDtypeStruct(shape, BF16) for shape in shapes],
        compiler_params=pltpu.CompilerParams(vmem_limit_bytes=VMEM_LIMIT),
        cost_estimate=pl.CostEstimate(flops=5 * 10**9, bytes_accessed=16 * 10**6, transcendentals=0),
        name="weight_grad",
    )(place, n1, dqkv, att, dbr, sums, dbfc0, dbfc1)


def flip(position):
    return lambda i: i ^ position


def exchange(array, partner):
    return lax.ppermute(array, "dp", [(i, partner(i)) for i in range(PIECES)])


def plane_partner(stage):
    def partner(i):
        along_y = (i % 2 == 0) == (stage == "first")
        return i ^ (4 if along_y else 2)

    return partner


class CubeGather:
    def __init__(self, block):
        self.ready, self.came, self.parts = block, None, None

    def over_z(self, *steps):
        self.came = tuple(exchange(self.ready, lambda i, k=k: (i + 8 * k) % PIECES) for k in steps)

    def over_plane(self, stage):
        self.came = (exchange(self.ready, plane_partner(stage)),)

    def take(self, axis=0):
        self.ready = jnp.stack((self.ready,) + tuple(self.came), axis=axis)

    def finish(self):
        self.parts = (self.ready, self.came[0])

    def share(self):
        self.parts = self.parts + tuple(exchange(half, flip(1)) for half in self.parts)


def meet(*things):
    return lax.optimization_barrier(things)


def total_body(*refs, scale, counts):
    outs = refs[7 * counts :]
    totals = []
    for k in range(counts):
        parts = [r[...].astype(F32) for r in refs[7 * k : 7 * k + 7]]
        totals.append(sum(parts[1:], parts[0]).reshape(parts[-1].shape) * scale)
    return totals, outs


def ffn_total_body(*refs, scale):
    totals, (d_fc, d_out) = total_body(*refs, scale=scale, counts=2)
    _, rows, width = totals[0].shape
    lane = lax.broadcasted_iota(jnp.int32, (rows, 128), 1)
    columns = [jnp.concatenate([t[0], t[1]], axis=1) for t in totals]
    for half, total in enumerate(totals):
        for b in range(2):
            at = (half * 2 + b) * rows
            d_out[at : at + rows, :] = total[2 + b]
    step = 2 * rows
    tiles = [jnp.zeros((rows, 128), F32) for _ in range(4 * width // 128)]
    for piece in range(PIECES):
        for half in range(2):
            block = collect(columns[half], step, step, 0, piece)
            at = (2 * piece + half) * step
            tile, shift = at // 128, at % 128
            if shift:
                block = pltpu.roll(block, shift, 1)
            if shift + step <= 128:
                tiles[tile] = tiles[tile] + block
            else:
                tiles[tile] = tiles[tile] + jnp.where(lane >= shift, block, 0.0)
                tiles[tile + 1] = tiles[tile + 1] + jnp.where(lane < shift, block, 0.0)
    for t, tile in enumerate(tiles):
        d_fc[:, t * 128 : (t + 1) * 128] = tile


def attn_total_body(*refs, scale):
    (left, right), (d_qkv, d_proj, vectors) = total_body(*refs, scale=scale, counts=2)
    width = d_proj.shape[1]
    d_qkv[:, : 2 * width] = left
    d_qkv[:, 2 * width :] = right[:, :width]
    d_proj[...] = right[:, width : 2 * width]
    vectors[...] = right[:, 2 * width :]


def totals(body, sums, scale, shapes, name):
    pieces = [a for s in sums for a in (s.keep, s.came, s.first, s.second) + tuple(s.rest)]
    arrays = [a[0] if isinstance(a, tuple) else a for a in pieces]
    blocks = [s.rest[0].shape for s in sums for _ in range(7)]

    def spec(piece, block):
        array, index = piece if isinstance(piece, tuple) else (piece, 0)
        lead = len(array.shape) - len(block)
        at = (index,) + (0,) * (len(array.shape) - 1)
        return pl.BlockSpec((1,) * lead + tuple(block), lambda i: at)

    return pl.pallas_call(
        functools.partial(body, scale=scale),
        grid=(1,),
        in_specs=[spec(p, b) for p, b in zip(pieces, blocks)],
        out_shape=[jax.ShapeDtypeStruct(shape, F32) for shape in shapes],
        compiler_params=pltpu.CompilerParams(vmem_limit_bytes=VMEM_LIMIT),
        cost_estimate=pl.CostEstimate(flops=10**6, bytes_accessed=5 * 10**6, transcendentals=0),
        name=name,
    )(*arrays)


def over_z(block, k):
    return exchange(block, lambda i: (i - 8 * k) % PIECES)


class CubeSum:
    def __init__(self, keep, send):
        self.grads, self.keep, self.ahead = (keep, send), keep, send
        self.came, self.first, self.second, self.rest = None, None, None, None

    def part(self, *at):
        total = self.keep[at].astype(F32) + self.came[at].astype(F32)
        if self.first is not None:
            total = total + self.first[at[1:]].astype(F32)
        if self.second is not None:
            total = total + self.second[at[2:]].astype(F32)
        return total

    def send(self):
        if self.came is None:
            self.came = exchange(self.ahead, flip(1))
        elif self.first is None:
            self.ahead = self.part(1).astype(BF16)
            self.first = exchange(self.ahead, plane_partner("first"))
        elif self.second is None:
            self.ahead = self.part(0, 1).astype(BF16)
            self.second = exchange(self.ahead, plane_partner("second"))
        else:
            self.ahead = [self.part(0, 0, k).astype(BF16) for k in range(1, Z)]
            self.rest = [over_z(block, k) for k, block in enumerate(self.ahead, 1)]


def hold(first, *then):
    return tuple(lax.optimization_barrier((first, one))[1] for one in then)


def sum_over(values, *bits):
    for bit in bits:
        values = values + exchange(values, flip(bit))
    return values


def cut_any(blocks):
    every = blocks.reshape((Z, Y, X, CORES) + blocks.shape[1:])
    deep = jnp.array([0, 3, 2, 1])
    rest = tuple(range(3, every.ndim - 1))
    even = jnp.transpose(every[:, :, :, 0], (1, 2, 0) + rest)[:, :, deep]
    odd = jnp.transpose(every[:, :, :, 1], (2, 1, 0) + rest)[:, :, deep]
    return even[0], even[1], odd[0], odd[1]


def natural_blocks(keep, send):
    deep = jnp.array([0, 3, 2, 1])
    rest = tuple(range(3, keep.ndim))
    even = jnp.transpose(keep[:, :, deep], (2, 0, 1) + rest)
    odd = jnp.transpose(send[:, :, deep], (2, 1, 0) + rest)
    both = jnp.stack([even, odd], axis=3)
    return both.reshape((PIECES,) + both.shape[4:])


def on_device(
    tokens,
    segment_ids,
    time_embed,
    norm1_gain,
    norm1_shift,
    w_qkv,
    b_query,
    b_value,
    w_proj,
    b_proj,
    norm2_gain,
    norm2_shift,
    w_fc,
    b_fc,
    w_out,
    b_out,
    cotangent,
):
    row_count, row_len, width = tokens.shape
    toks = row_count * row_len
    devices = lax.axis_size("dp")
    cube = devices == PIECES
    rank = lax.axis_index("dp")
    grad_scale = 1.0 / math.sqrt(toks * devices)
    own = w_proj.shape[0]
    ratio = b_fc.shape[0] // own
    if cube:
        place = jnp.stack([rank // 8, (rank // 4) % 2, (rank // 2) % 2, rank % 2]).astype(jnp.int32)
    else:
        place = jnp.zeros((4,), jnp.int32)

    small = jnp.concatenate(
        [norm1_gain, norm1_shift, b_query, b_value, b_proj, norm2_gain, norm2_shift, b_out, b_fc]
    ).reshape(8 + ratio, own)
    order = list(range(8)) + [8 + 2 * h + k for k in range(ratio // 2) for h in range(2)]
    small = jnp.concatenate([small[v : v + 1] for v in order], axis=0)
    cut = width // PIECES
    halves = 2
    blocks = ratio // halves
    ffn_fc = lambda w: w.reshape(-1, PIECES, halves, blocks * cut).transpose(2, 0, 1, 3).reshape(halves, -1, blocks, width)
    if cube:
        ffn_block = jnp.concatenate(
            [ffn_fc(w_fc).transpose(0, 2, 1, 3), w_out.reshape(halves, blocks, own, width)], axis=1
        )
        small = jnp.pad(small, ((0, own - small.shape[0]), (0, 128 - own)))
        attn_gather = CubeGather(jnp.concatenate([w_qkv, w_proj, small], axis=1))
        early, late = CubeGather(ffn_block[0]), CubeGather(ffn_block[1])
        attn_gather.over_z(1, 2, 3)
        early.over_plane("second")
        late.over_plane("second")
        attn_gather.came, early.came, late.came = meet(attn_gather.came, early.came, late.came)
        attn_gather.take()
        early.take()
        late.take()
        attn_gather.over_plane("second")
        early.over_z(1, 3)
        attn_gather.came, early.came, late.ready = meet(attn_gather.came, early.came, late.ready)
        near = early.came
        attn_gather.take()
        attn_gather.over_plane("first")
        early.over_z(2)
        late.over_z(1, 2, 3)
        attn_gather.came, early.came = meet(attn_gather.came, early.came)
        attn_gather.finish()
        attn_gather.share()
        early.came = (near[0], early.came[0], near[1])
        early.take(axis=1)
        early.over_plane("first")
        attn_full = attn_gather.parts
    else:
        whole = lambda w: lax.all_gather(w, "dp", axis=0, tiled=True)
        natural = whole(small.T.reshape(own, -1))
        vectors = natural[:, :8].T
        hidden_bias = whole(b_fc).reshape(PIECES, ratio, cut)
        small = jnp.concatenate(
            [vectors.reshape(8, PIECES, cut).transpose(1, 0, 2), hidden_bias[:, jnp.array([0, 2, 1, 3])]], axis=1
        )
        small = jnp.pad(small, ((0, 0), (0, cut - small.shape[1]), (0, 128 - cut))).reshape(width, 128)
        attn_full = jnp.concatenate([whole(w_qkv), whole(w_proj), small], axis=1)
        attn_full = cut_any(attn_full.reshape(PIECES, cut, -1))
        fc_full = ffn_fc(whole(w_fc)).reshape(halves, PIECES, cut, blocks, width).transpose(1, 0, 3, 2, 4)
        out_full = whole(w_out).reshape(PIECES, halves, blocks, cut, width)
        ffn_full = jnp.concatenate([fc_full, out_full], axis=2)
        early, late = [cut_any(ffn_full[:, h].reshape(PIECES, -1, cut, width)) for h in range(halves)]

    flat = tokens.reshape(toks, width)
    times = time_embed.reshape(row_count, 1, width)
    segments = segment_ids.reshape(row_count, 1, row_len)
    cot = cotangent.reshape(toks, width)
    if cube:
        (segments,) = hold(early.ready, segments)
    n1, qkv, probs, att, hid, n2, attn_w, vec, bfc = attn_forward(place, flat, times, segments, attn_full)
    if cube:
        n2, early.came, late.came = meet(n2, early.came, late.came)
        early.finish()
        early.share()
        late.take(axis=1)
        late.over_plane("first")
        (n2,) = hold(late.ready, n2)
        early = early.parts
    out0, dn20, dbfc0, *grads0 = ffn(place, n2, cot, early, bfc, 0)
    sum0 = CubeSum(*grads0)
    if cube:
        out0, late.came, sum0.ahead = meet(out0, late.came, sum0.ahead)
        late.finish()
        late.share()
        sum0.send()
        sum0.send()
        (n2,) = hold(sum0.ahead, n2)
        late = late.parts
    out1, dn21, dbfc1, *grads1 = ffn(place, n2, cot, late, bfc, 1)
    sum1 = CubeSum(*grads1)
    if cube:
        out1, sum1.ahead, sum0.first = meet(out1, sum1.ahead, sum0.first)
        sum1.send()
        sum0.send()
        sum1.send()
        (hid,) = hold(sum1.ahead, *hold(sum0.ahead, hid))
    layer_out, d_tokens, d_time, dbr, dqkv, sums = attn_backward(
        flat, times, hid, (out0, out1), (dn20, dn21), cot, qkv, probs, attn_w, vec
    )
    if cube:
        dqkv, sum0.second, sum1.first = meet(dqkv, sum0.second, sum1.first)
        sum1.send()
        deep0 = [sum0.part(0, 0, k).astype(BF16) for k in (1, 3)]
        near0, wrap0 = over_z(deep0[0], 1), over_z(deep0[1], 3)
        (dqkv,) = hold(sum1.ahead, *hold(deep0[0], *hold(deep0[1], dqkv)))
    grads = weight_grad(place, n1, dqkv, att, dbr, sums, dbfc0, dbfc1)
    attn0, attn1 = CubeSum(*grads[:2]), CubeSum(*grads[2:])
    if cube:
        attn0.ahead, attn1.ahead, sum1.second, near0, wrap0 = meet(
            attn0.ahead, attn1.ahead, sum1.second, near0, wrap0
        )
        attn0.send()
        attn1.send()
        attn0.send()
        attn1.send()
        (sum1.second,) = hold(attn1.ahead, sum1.second)
        near1, wrap1 = [over_z(sum1.part(0, 0, k).astype(BF16), k) for k in (1, 3)]
        far = over_z(jnp.stack([s.part(0, 0, 2).astype(BF16) for s in (sum0, sum1)]), 2)
        sum0.rest = [near0, (far, 0), wrap0]
        sum1.rest = [near1, (far, 1), wrap1]
        attn0.send()
        for there in (attn0.second, near1, wrap1):
            (attn1.first,) = hold(there, attn1.first)
        attn1.send()
        attn0.send()
        own_fc, own_out = totals(
            ffn_total_body, (sum0, sum1), grad_scale, [(own, ratio * width), (ratio * own, width)], "ffn_total"
        )
        for there in (own_fc, attn0.rest[0], attn0.rest[2]):
            (attn1.second,) = hold(there, attn1.second)
        attn1.send()
        attn0.rest = hold(attn1.ahead[0], *attn0.rest)
        own_qkv, own_proj, vectors = totals(
            attn_total_body,
            (attn0, attn1),
            grad_scale,
            [(own, 3 * width), (own, width), (own, 128)],
            "attn_total",
        )
        mine = vectors[:8, :own]
        own_bfc = jnp.concatenate([vectors[8 + v, :own] for v in (0, 2, 1, 3)])
    else:
        scatter = lambda g: lax.psum_scatter(g, "dp", scatter_dimension=0, tiled=True)
        grads = jnp.concatenate([natural_blocks(*a.grads) for a in (attn0, attn1)], axis=-1).astype(F32)
        own_qkv = scatter(grads[:, :, : 3 * width].reshape(width, -1))
        own_proj = scatter(grads[:, :, 3 * width : 4 * width].reshape(width, -1))
        vectors = lax.psum(grads[:, :, 4 * width : 4 * width + cut], "dp")
        mine = lax.dynamic_slice(
            vectors[:, :8].transpose(1, 0, 2).reshape(8, width), (0, rank * own), (8, own)
        )
        hidden_grad = vectors[:, jnp.array([8, 10, 9, 11])].reshape(-1)
        own_bfc = lax.dynamic_slice(hidden_grad, (rank * own * ratio,), (own * ratio,))
        grads = jnp.stack([natural_blocks(*s.grads) for s in (sum0, sum1)], axis=1).astype(F32)
        out_grad = grads[:, :, blocks:].reshape(ratio * width, width)
        own_out = scatter(out_grad)
        fc_grad = grads[:, :, :blocks].transpose(0, 3, 1, 2, 4).reshape(width, halves, PIECES, blocks * cut)
        own_fc = scatter(fc_grad.transpose(0, 2, 1, 3).reshape(width, ratio * width))
        mine, own_bfc, own_qkv, own_proj, own_fc, own_out = [
            member * grad_scale for member in (mine, own_bfc, own_qkv, own_proj, own_fc, own_out)
        ]
    return (
        layer_out.reshape(tokens.shape),
        d_tokens.reshape(tokens.shape),
        d_time.reshape(time_embed.shape),
        mine[6],
        mine[7],
        own_qkv,
        mine[4],
        mine[5],
        own_proj,
        mine[2],
        mine[0],
        mine[1],
        own_fc,
        own_bfc,
        own_out,
        mine[3],
    )


def solution(mesh):
    in_specs = (
        P("dp", None, None),
        P("dp", None),
        P("dp", None),
        P("dp"),
        P("dp"),
        P("dp", None),
        P("dp"),
        P("dp"),
        P("dp", None),
        P("dp"),
        P("dp"),
        P("dp"),
        P("dp", None),
        P("dp"),
        P("dp", None),
        P("dp"),
        P("dp", None, None),
    )
    out_specs = (
        P("dp", None, None),
        P("dp", None, None),
        P("dp", None),
        P("dp"),
        P("dp"),
        P("dp", None),
        P("dp"),
        P("dp"),
        P("dp", None),
        P("dp"),
        P("dp"),
        P("dp"),
        P("dp", None),
        P("dp"),
        P("dp", None),
        P("dp"),
    )
    return jax.shard_map(
        on_device, mesh=mesh, in_specs=in_specs, out_specs=out_specs, check_vma=False
    )
```

```python
import functools
import math

import jax
import jax.numpy as jnp
from jax import lax
from jax.experimental import pallas as pl
from jax.experimental.pallas import tpu as pltpu
from jax.sharding import PartitionSpec as P

HD = 64
EPS = 1e-05
MASKED = -1e30
F32 = jnp.float32
BF16 = jnp.bfloat16
VMEM_LIMIT = 48 * 1024 * 1024
FFN_VMEM_LIMIT = 40 * 1024 * 1024


def dot(a, b, a_dim, b_dim):
    return lax.dot_general(a, b, (((a_dim,), (b_dim,)), ((), ())), preferred_element_type=F32)


def normalise(values):
    centered = values - jnp.mean(values, axis=-1, keepdims=True)
    spread = jnp.mean(centered * centered, axis=-1, keepdims=True)
    inv = lax.rsqrt(spread + EPS)
    return centered * inv, inv


def head_pair(block):
    lane = lax.broadcasted_iota(jnp.int32, block.shape, 1)
    zero = jnp.zeros_like(block)
    return jnp.concatenate([jnp.where(lane < HD, block, zero), jnp.where(lane >= HD, block, zero)], axis=0)


def own_lanes(stacked):
    half = stacked.shape[0] // 2
    lane = lax.broadcasted_iota(jnp.int32, (half, stacked.shape[1]), 1)
    return jnp.where(lane < HD, stacked[:half], stacked[half:])


def row_mask(seg_row):
    size = seg_row.shape[1]
    across = jnp.broadcast_to(seg_row.astype(F32), (size, size))
    return jnp.where(across == across.T, 0.0, MASKED)


def colsum(v):
    return jnp.sum(v, axis=0, keepdims=True)


Z, Y, X, CORES = 4, 2, 2, 2
PIECES = Z * Y * X * CORES


def merge_rows(blocks):
    count, rows, width = blocks.shape
    return blocks.astype(F32).reshape(count * rows, width).astype(BF16)


def slots(place, z, y, x):
    ys, xs = y ^ place[1], x ^ place[2]
    first = jnp.where(place[3] == 0, ys, xs)
    second = jnp.where(place[3] == 0, xs, ys)
    return first, second, place[0] ^ z


def put_blocks(place, z, y, x, even, odd, keep, send, tail=()):
    first, second, deep = slots(place, z, y, x)
    mine = place[3] == 0
    keep[(first, second, deep) + tail] = jnp.where(mine, even, odd)
    send[(second, first, deep) + tail] = jnp.where(mine, odd, even)


def pick(place, parts, z, y, x, tail=()):
    mine0, mine1, other0, other1 = parts
    first, second, deep = slots(place, z, y, x)
    mine = jnp.where(first == 0, mine0[(second, deep) + tail], mine1[(second, deep) + tail])
    other = jnp.where(second == 0, other0[(first, deep) + tail], other1[(first, deep) + tail])
    even = place[3] == 0
    return jnp.where(even, mine, other), jnp.where(even, other, mine)


def spread(small, cut, row, stride, start, length):
    lane = lax.broadcasted_iota(jnp.int32, (8, 128), 1)
    tiles = [jnp.zeros((8, 128), F32) for _ in range(length // 128)]
    for i in range(PIECES):
        at = start + i * stride
        tile, shift = at // 128, at % 128
        block = small[i * cut + row : i * cut + row + 8]
        if shift:
            block = pltpu.roll(block, shift, 1)
        if shift + cut <= 128:
            tiles[tile] = tiles[tile] + block
        else:
            tiles[tile] = tiles[tile] + jnp.where(lane >= shift, block, 0.0)
            tiles[tile + 1] = tiles[tile + 1] + jnp.where(lane < shift, block, 0.0)
    return jnp.concatenate(tiles, axis=1)


def attn_forward_body(
    place, tok, time, seg, mine0, mine1, other0, other1, n1, qkv, probs, att, hid, n2, weights, vec, bfc, *, rows
):
    size = tok.shape[0] // rows
    width = tok.shape[1]

    @pl.when(pl.program_id(0) == 0)
    def _():
        for z in range(Z):
            for y in range(Y):
                for x in range(X):
                    both = pick(place, (mine0, mine1, other0, other1), z, y, x)
                    both = jnp.concatenate([b.astype(F32) for b in both], axis=0)
                    step = both.shape[0]
                    at = ((z * Y + y) * X + x) * step
                    weights[at : at + step, :] = both.astype(BF16)
        small = weights[:, 4 * width :].astype(F32)
        cut = width // PIECES
        vec[...] = spread(small, cut, 0, cut, 0, width)
        early = spread(small, cut, 8, 2 * cut, 0, bfc.shape[1])
        late = spread(small, cut, 8, 2 * cut, cut, bfc.shape[1])
        bfc[...] = early[0:2] + late[2:4]

    x = tok[...].astype(F32)
    x = jnp.concatenate(
        [x[r * size : (r + 1) * size] + time[r].astype(F32) for r in range(rows)], axis=0
    )
    nhat, _ = normalise(x)
    normed = (nhat * vec[0:1, :] + vec[1:2, :]).astype(BF16)
    n1[...] = normed
    for part in range(3):
        cols = slice(part * width, (part + 1) * width)
        block = dot(normed, weights[:, cols], 1, 0)
        if part == 0:
            block = block + vec[2:3, :]
        if part == 2:
            block = block + vec[3:4, :]
        qkv[:, cols] = block.astype(BF16)
    pairs = width // (2 * HD)
    for r in range(rows):
        sl = slice(r * size, (r + 1) * size)
        mask = row_mask(seg[r])
        for p in range(pairs):
            c = 2 * HD * p
            q = qkv[sl, c : c + 2 * HD] * jnp.asarray(HD**-0.5, BF16)
            k = head_pair(qkv[sl, width + c : width + c + 2 * HD])
            v = head_pair(qkv[sl, 2 * width + c : 2 * width + c + 2 * HD])
            s = dot(k, q, 1, 1)
            halves = []
            for h in range(2):
                sh = s[h * size : (h + 1) * size] + mask
                e = jnp.exp(sh - jnp.max(sh, axis=0, keepdims=True))
                halves.append((e * (1.0 / jnp.sum(e, axis=0, keepdims=True))).astype(BF16))
            pr = jnp.concatenate(halves, axis=0)
            probs[r, p] = pr
            att[sl, c : c + 2 * HD] = dot(pr, v, 0, 0).astype(BF16)
    hidden = x + dot(att[...], weights[:, 3 * width : 4 * width], 1, 0) + vec[4:5, :]
    hid[...] = hidden
    nhat2, _ = normalise(hidden)
    n2[...] = (nhat2 * vec[5:6, :] + vec[6:7, :]).astype(BF16)


def attn_forward(place, tok, time, seg, gathered, rows=2):
    row_count = seg.shape[0]
    toks, width = tok.shape
    size = toks // row_count
    tm = rows * size
    pairs = width // (2 * HD)
    wide = gathered[0].shape[-1]
    full = lambda s: pl.BlockSpec(s, lambda i: (0,) * len(s))
    tile = lambda cols: pl.BlockSpec((tm, cols), lambda i: (i, 0))
    return pl.pallas_call(
        functools.partial(attn_forward_body, rows=rows),
        grid=(row_count // rows,),
        in_specs=[
            pl.BlockSpec(memory_space=pltpu.SMEM),
            tile(width),
            pl.BlockSpec((rows, 1, width), lambda i: (i, 0, 0)),
            pl.BlockSpec((rows, 1, size), lambda i: (i, 0, 0)),
        ]
        + [full(g.shape) for g in gathered],
        out_specs=[
            tile(width),
            tile(3 * width),
            pl.BlockSpec((rows, pairs, 2 * size, size), lambda i: (i, 0, 0, 0)),
            tile(width),
            tile(width),
            tile(width),
            full((width, wide)),
            full((8, width)),
            full((2, 2 * width)),
        ],
        out_shape=[
            jax.ShapeDtypeStruct((toks, width), BF16),
            jax.ShapeDtypeStruct((toks, 3 * width), BF16),
            jax.ShapeDtypeStruct((row_count, pairs, 2 * size, size), BF16),
            jax.ShapeDtypeStruct((toks, width), BF16),
            jax.ShapeDtypeStruct((toks, width), F32),
            jax.ShapeDtypeStruct((toks, width), BF16),
            jax.ShapeDtypeStruct((width, wide), BF16),
            jax.ShapeDtypeStruct((8, width), F32),
            jax.ShapeDtypeStruct((2, 2 * width), F32),
        ],
        compiler_params=pltpu.CompilerParams(vmem_limit_bytes=VMEM_LIMIT),
        cost_estimate=pl.CostEstimate(flops=16 * 10**9, bytes_accessed=20 * 10**6, transcendentals=2 * 10**6),
        name="attn_forward",
    )(place, tok, time, seg, *gathered)


def ffn_body(
    place, n2, cot, mine0, mine1, other0, other1, bfc, sum_out, sum_dn2, dbfc, keep, send, acc_out, acc_dn2, fc_s, out_s, act_s, dpre_s, *, tm, sub, half
):
    step = pl.program_id(0)

    @pl.when(step == 0)
    def _():
        acc_out[...] = jnp.zeros_like(acc_out)
        acc_dn2[...] = jnp.zeros_like(acc_dn2)

    gathered = (mine0, mine1, other0, other1)
    blocks, rows = 2, mine0.shape[-2]
    for z in range(Z):
        for y in range(Y):
            for x in range(X):
                both = pick(place, gathered, z, y, x, (step,))
                at = ((z * Y + y) * X + x) * CORES * rows
                fc_s[at : at + CORES * rows, :] = merge_rows(jnp.stack(both))
    for z in range(Z // blocks):
        for y in range(Y):
            for x in range(X):
                both = pick(place, gathered, step * (Z // blocks) + z, y, x, (slice(blocks, 2 * blocks),))
                at = ((z * Y + y) * X + x) * CORES * blocks * rows
                out_s[at : at + CORES * blocks * rows, :] = merge_rows(jnp.concatenate(both, axis=0))
    chunk = fc_s.shape[1]
    for part in range(chunk // sub):
        cols = slice(part * sub, (part + 1) * sub)
        bias = bfc[half : half + 1, cols]
        db = jnp.zeros_like(bias)
        for m in range(n2.shape[0] // tm):
            sl = slice(m * tm, (m + 1) * tm)
            pre = dot(n2[sl, :], fc_s[:, cols], 1, 0) + bias
            d_act = dot(cot[sl, :], out_s[cols, :], 1, 1)
            cdf = 0.5 * lax.erf(pre * math.sqrt(0.5)) + 0.5
            density = jnp.exp(pre * pre * -0.5) * (1.0 / math.sqrt(2.0 * math.pi))
            act = (pre * cdf).astype(BF16)
            d_pre = (d_act * (cdf + pre * density)).astype(BF16)
            act_s[sl, cols] = act
            dpre_s[sl, cols] = d_pre
            db = db + jnp.sum(d_pre.astype(F32), axis=0, keepdims=True)
            acc_out[sl, :] += dot(act, out_s[cols, :], 1, 0)
            acc_dn2[sl, :] += dot(d_pre, fc_s[:, cols], 1, 1)
        dbfc[:, cols] = db

    @pl.when(step == pl.num_programs(0) - 1)
    def _():
        sum_out[...] = acc_out[...].astype(BF16)
        sum_dn2[...] = acc_dn2[...].astype(BF16)

    grad = dot(act_s[...], cot[...], 0, 0)
    planes = Z // blocks
    for z in range(planes):
        for y in range(Y):
            for x in range(X):
                for b in range(blocks):
                    at = (((z * Y + y) * X + x) * CORES * blocks + b) * rows
                    even = grad[at : at + rows].astype(BF16)
                    odd = grad[at + blocks * rows : at + (blocks + 1) * rows].astype(BF16)
                    put_blocks(place, step * planes + z, y, x, even, odd, keep, send, (blocks + b,))
    grad = dot(n2[...], dpre_s[...], 0, 0)
    for z in range(Z):
        for y in range(Y):
            for x in range(X):
                at = ((z * Y + y) * X + x) * CORES * rows
                even = grad[at : at + rows].astype(BF16)
                odd = grad[at + rows : at + 2 * rows].astype(BF16)
                put_blocks(place, z, y, x, even, odd, keep, send, (step,))


def ffn(place, n2, cot, gathered, bfc, half, tm=512, sub=768):
    toks, width = n2.shape
    rows = width // PIECES
    blocks = 2
    count = 2 * blocks
    once = pl.Buffered(buffer_count=1)
    full = lambda s: pl.BlockSpec(s, lambda j: (0,) * len(s), pipeline_mode=once)
    whole = lambda s: pl.BlockSpec(s, lambda j: (0,) * len(s))
    parted = (Y, X, Z, count, rows, width)
    return pl.pallas_call(
        functools.partial(ffn_body, tm=tm, sub=sub, half=half),
        grid=(blocks,),
        in_specs=[
            pl.BlockSpec(memory_space=pltpu.SMEM),
            full((toks, width)),
            full((toks, width)),
        ]
        + [full(g.shape) for g in gathered]
        + [
            pl.BlockSpec((2, width), lambda j: (0, j)),
        ],
        out_specs=[
            whole((toks, width)),
            whole((toks, width)),
            pl.BlockSpec((1, width), lambda j: (0, j)),
            whole(parted),
            whole(parted),
        ],
        out_shape=[
            pltpu.HBM((toks, width), BF16),
            pltpu.HBM((toks, width), BF16),
            jax.ShapeDtypeStruct((1, blocks * width), F32),
            jax.ShapeDtypeStruct(parted, BF16),
            jax.ShapeDtypeStruct(parted, BF16),
        ],
        scratch_shapes=[
            pltpu.VMEM((toks, width), F32),
            pltpu.VMEM((toks, width), F32),
            pltpu.VMEM((width, width), BF16),
            pltpu.VMEM((width, width), BF16),
            pltpu.VMEM((toks, width), BF16),
            pltpu.VMEM((toks, width), BF16),
        ],
        compiler_params=pltpu.CompilerParams(vmem_limit_bytes=FFN_VMEM_LIMIT),
        cost_estimate=pl.CostEstimate(flops=15 * 10**9, bytes_accessed=20 * 10**6, transcendentals=3 * 10**6),
        name="ffn",
    )(place, n2, cot, *gathered, bfc)


def attn_backward_body(
    tok, time, hid, out0, out1, dn20, dn21, cot, qkv, probs, weights, vec, layer_out, dtok, dtime, dbr, dqkv, sums, *, rows
):
    width = hid.shape[1]
    size = hid.shape[0] // rows

    @pl.when(pl.program_id(0) == 0)
    def _():
        sums[...] = jnp.zeros_like(sums)

    hidden = hid[...]
    layer_out[...] = (hidden + (out0[...].astype(F32) + out1[...].astype(F32)) + vec[7:8, :]).astype(BF16)
    nhat, inv = normalise(hidden)
    dn2 = dn20[...].astype(F32) + dn21[...].astype(F32)
    cotangent = cot[...].astype(F32)
    q = dn2 * vec[5:6, :]
    mean_q = jnp.mean(q, axis=-1, keepdims=True)
    mean_qn = jnp.mean(q * nhat, axis=-1, keepdims=True)
    d_hidden = cotangent + (q - mean_q - nhat * mean_qn) * inv
    dtok[...] = d_hidden
    branch = d_hidden.astype(BF16)
    dbr[...] = branch
    sums[0:1, :] += colsum(dn2 * nhat)
    sums[1:2, :] += colsum(dn2)
    sums[2:3, :] += colsum(branch.astype(F32))
    sums[3:4, :] += colsum(cotangent)
    d_mixed = dot(branch, weights[:, 3 * width : 4 * width], 1, 1).astype(BF16)
    pairs = width // (2 * HD)
    for r in range(rows):
        sl = slice(r * size, (r + 1) * size)
        for p in range(pairs):
            c = 2 * HD * p
            qb = qkv[sl, c : c + 2 * HD] * jnp.asarray(HD**-0.5, BF16)
            k = head_pair(qkv[sl, width + c : width + c + 2 * HD])
            v = head_pair(qkv[sl, 2 * width + c : 2 * width + c + 2 * HD])
            dm = d_mixed[sl, c : c + 2 * HD]
            pr = probs[r, p]
            dp = dot(v, dm, 1, 1)
            halves = []
            for h in range(2):
                pf = pr[h * size : (h + 1) * size].astype(F32)
                dph = dp[h * size : (h + 1) * size]
                halves.append((pf * (dph - jnp.sum(dph * pf, axis=0, keepdims=True))).astype(BF16))
            ds = jnp.concatenate(halves, axis=0)
            dv = own_lanes(dot(pr, dm, 1, 0))
            dk = own_lanes(dot(ds, qb, 1, 0))
            dq = dot(ds, k, 0, 0) * HD**-0.5
            dqkv[sl, c : c + 2 * HD] = dq.astype(BF16)
            dqkv[sl, width + c : width + c + 2 * HD] = dk.astype(BF16)
            dqkv[sl, 2 * width + c : 2 * width + c + 2 * HD] = dv.astype(BF16)
    sums[4:5, :] += colsum(dqkv[:, :width].astype(F32))
    sums[5:6, :] += colsum(dqkv[:, 2 * width :].astype(F32))

    x = tok[...].astype(F32)
    x = jnp.concatenate(
        [x[r * size : (r + 1) * size] + time[r].astype(F32) for r in range(rows)], axis=0
    )
    nhat, inv = normalise(x)
    dn1 = dot(dqkv[...], weights[:, : 3 * width], 1, 1)
    sums[6:7, :] += colsum(dn1 * nhat)
    sums[7:8, :] += colsum(dn1)
    q = dn1 * vec[0:1, :]
    mean_q = jnp.mean(q, axis=-1, keepdims=True)
    mean_qn = jnp.mean(q * nhat, axis=-1, keepdims=True)
    d_tok = dtok[...] + (q - mean_q - nhat * mean_qn) * inv
    dtok[...] = d_tok
    for r in range(rows):
        dtime[r] = colsum(d_tok[r * size : (r + 1) * size])


def attn_backward(tok, time, hid, outs, dn2s, cot, qkv, probs, weights, vec, rows=2):
    row_count, pairs, _, size = probs.shape
    width = hid.shape[1]
    tm = rows * size
    toks = row_count * size
    steps = row_count // rows
    once = pl.Buffered(buffer_count=1)
    full = lambda s: pl.BlockSpec(s, lambda i: (0,) * len(s), pipeline_mode=once)
    tile = lambda cols: pl.BlockSpec((tm, cols), lambda i: (i, 0))
    per_row = pl.BlockSpec((rows, 1, width), lambda i: (i, 0, 0))
    return pl.pallas_call(
        functools.partial(attn_backward_body, rows=rows),
        grid=(steps,),
        in_specs=[tile(width), per_row]
        + [tile(width)] * 6
        + [
            tile(3 * width),
            pl.BlockSpec((rows, pairs, 2 * size, size), lambda i: (i, 0, 0, 0)),
            full(weights.shape),
            full(vec.shape),
        ],
        out_specs=[
            tile(width),
            tile(width),
            per_row,
            tile(width),
            tile(3 * width),
            pl.BlockSpec((8, width), lambda i: (0, 0)),
        ],
        out_shape=[
            jax.ShapeDtypeStruct((toks, width), BF16),
            jax.ShapeDtypeStruct((toks, width), F32),
            jax.ShapeDtypeStruct((row_count, 1, width), F32),
            jax.ShapeDtypeStruct((toks, width), BF16),
            jax.ShapeDtypeStruct((toks, 3 * width), BF16),
            jax.ShapeDtypeStruct((8, width), F32),
        ],
        compiler_params=pltpu.CompilerParams(vmem_limit_bytes=VMEM_LIMIT),
        cost_estimate=pl.CostEstimate(flops=6 * 10**9 * steps, bytes_accessed=10 * 10**6 * steps, transcendentals=0),
        name="attn_backward",
    )(tok, time, hid, *outs, *dn2s, cot, qkv, probs, weights, vec)


def collect(vectors, cut, stride, start, piece):
    at = start + piece * stride
    tile, shift = at // 128, at % 128
    lane = lax.broadcasted_iota(jnp.int32, (vectors.shape[0], 128), 1)
    block = vectors[:, tile * 128 : (tile + 1) * 128]
    if shift + cut > 128:
        block = jnp.where(lane >= shift, block, vectors[:, (tile + 1) * 128 : (tile + 2) * 128])
    if shift:
        block = pltpu.roll(block, 128 - shift, 1)
    return jnp.where(lane < cut, block, 0.0)


def weight_grad_body(place, n1, dqkv, att, dbr, sums, dbfc0, dbfc1, keep0, send0, keep1, send1):
    rows = keep0.shape[3]
    width = n1.shape[1]
    step = pl.program_id(0)

    def emit(grad, keep, send, at_column):
        tail = (slice(None), slice(at_column, at_column + grad.shape[1]))
        for z in range(Z):
            for y in range(Y):
                for x in range(X):
                    at = ((z * Y + y) * X + x) * CORES * rows
                    even = grad[at : at + rows].astype(BF16)
                    odd = grad[at + rows : at + 2 * rows].astype(BF16)
                    put_blocks(place, z, y, x, even, odd, keep, send, tail)

    for k in range(2):

        @pl.when(step == k)
        def _(k=k):
            emit(dot(n1[...], dqkv[...], 0, 0), keep0, send0, k * width)

    @pl.when(step == 2)
    def _():
        emit(dot(n1[...], dqkv[...], 0, 0), keep1, send1, 0)

    @pl.when(step == 3)
    def _():
        emit(dot(att[...], dbr[...], 0, 0), keep1, send1, width)
        vectors = sums[...]
        pad = jnp.zeros((6, dbfc0.shape[1]), F32)
        hidden = jnp.concatenate([dbfc0[...], dbfc1[...], pad], axis=0)

        def block(piece):
            early = collect(hidden, rows, 2 * rows, 0, piece)
            late = collect(hidden, rows, 2 * rows, rows, piece)
            top = collect(vectors, rows, rows, 0, piece)
            rest = [early[:2], late[:2], jnp.zeros((rows - 12, 128), F32)]
            return jnp.concatenate([top] + rest, axis=0).astype(BF16)

        tail = (slice(None), slice(2 * width, 2 * width + 128))
        for z in range(Z):
            for y in range(Y):
                for x in range(X):
                    piece = ((z * Y + y) * X + x) * CORES
                    put_blocks(place, z, y, x, block(piece), block(piece + 1), keep1, send1, tail)


def weight_grad(place, n1, dqkv, att, dbr, sums, dbfc0, dbfc1):
    toks, width = n1.shape
    rows = width // PIECES
    once = pl.Buffered(buffer_count=1)
    full = lambda a: pl.BlockSpec(a.shape, lambda j: (0, 0), pipeline_mode=once)
    shapes = [(Y, X, Z, rows, columns) for columns in (2 * width, 2 * width + 128) for _ in range(2)]
    return pl.pallas_call(
        weight_grad_body,
        grid=(4,),
        in_specs=[
            pl.BlockSpec(memory_space=pltpu.SMEM),
            full(n1),
            pl.BlockSpec((toks, width), lambda j: (0, jnp.minimum(j, 2))),
        ]
        + [full(e) for e in (att, dbr, sums, dbfc0, dbfc1)],
        out_specs=[pl.BlockSpec(shape, lambda j: (0,) * 5) for shape in shapes],
        out_shape=[jax.ShapeDtypeStruct(shape, BF16) for shape in shapes],
        compiler_params=pltpu.CompilerParams(vmem_limit_bytes=VMEM_LIMIT),
        cost_estimate=pl.CostEstimate(flops=5 * 10**9, bytes_accessed=16 * 10**6, transcendentals=0),
        name="weight_grad",
    )(place, n1, dqkv, att, dbr, sums, dbfc0, dbfc1)


def flip(position):
    return lambda i: i ^ position


def exchange(array, partner):
    return lax.ppermute(array, "dp", [(i, partner(i)) for i in range(PIECES)])


def plane_partner(stage):
    def partner(i):
        along_y = (i % 2 == 0) == (stage == "first")
        return i ^ (4 if along_y else 2)

    return partner


class CubeGather:
    def __init__(self, block):
        self.ready, self.came, self.parts = block, None, None

    def over_z(self, *steps):
        self.came = tuple(exchange(self.ready, flip(8 * k)) for k in steps)

    def over_plane(self, stage):
        self.came = (exchange(self.ready, plane_partner(stage)),)

    def take(self, axis=0):
        self.ready = jnp.stack((self.ready,) + tuple(self.came), axis=axis)

    def share(self):
        self.shared = exchange(self.ready, flip(1))

    def finish(self):
        self.parts = (self.ready, self.came[0], self.shared, exchange(self.came[0], flip(1)))


def meet(*things):
    return lax.optimization_barrier(things)


def total_body(*refs, scale, counts):
    outs = refs[7 * counts :]
    totals = []
    for k in range(counts):
        parts = [r[...].astype(F32) for r in refs[7 * k : 7 * k + 7]]
        totals.append(sum(parts[1:], parts[0]).reshape(parts[-1].shape) * scale)
    return totals, outs


def ffn_total_body(*refs, scale):
    totals, (d_fc, d_out) = total_body(*refs, scale=scale, counts=2)
    _, rows, width = totals[0].shape
    lane = lax.broadcasted_iota(jnp.int32, (rows, 128), 1)
    columns = [jnp.concatenate([t[0], t[1]], axis=1) for t in totals]
    for half, total in enumerate(totals):
        for b in range(2):
            at = (half * 2 + b) * rows
            d_out[at : at + rows, :] = total[2 + b]
    step = 2 * rows
    for t in range(4 * width // 128):
        tile = jnp.zeros((rows, 128), F32)
        for q in range(t * 128 // step, (t * 128 + 127) // step + 1):
            at, source = q * step - t * 128, (q // 2) * step
            first, shift = source // 128, source % 128
            block = columns[q % 2][:, first * 128 : (first + 1) * 128]
            if shift + step > 128:
                following = columns[q % 2][:, (first + 1) * 128 : (first + 2) * 128]
                block = jnp.where(lane >= shift, block, following)
            if (at - shift) % 128:
                block = pltpu.roll(block, (at - shift) % 128, 1)
            tile = jnp.where((lane >= at) & (lane < at + step), block, tile)
        d_fc[:, t * 128 : (t + 1) * 128] = tile


def attn_total_body(*refs, scale):
    (left, right), (d_qkv, d_proj, vectors) = total_body(*refs, scale=scale, counts=2)
    width = d_proj.shape[1]
    d_qkv[:, : 2 * width] = left
    d_qkv[:, 2 * width :] = right[:, :width]
    d_proj[...] = right[:, width : 2 * width]
    vectors[...] = right[:, 2 * width :]


def totals(body, sums, scale, shapes, name):
    pieces = [a for s in sums for a in (s.keep, s.came, s.first, s.second) + tuple(s.rest)]
    arrays = [a[0] if isinstance(a, tuple) else a for a in pieces]
    blocks = [s.rest[0].shape for s in sums for _ in range(7)]

    def spec(piece, block):
        array, index = piece if isinstance(piece, tuple) else (piece, 0)
        lead = len(array.shape) - len(block)
        at = (index,) + (0,) * (len(array.shape) - 1)
        return pl.BlockSpec((1,) * lead + tuple(block), lambda i: at)

    return pl.pallas_call(
        functools.partial(body, scale=scale),
        grid=(1,),
        in_specs=[spec(p, b) for p, b in zip(pieces, blocks)],
        out_shape=[jax.ShapeDtypeStruct(shape, F32) for shape in shapes],
        compiler_params=pltpu.CompilerParams(vmem_limit_bytes=VMEM_LIMIT),
        cost_estimate=pl.CostEstimate(flops=10**6, bytes_accessed=5 * 10**6, transcendentals=0),
        name=name,
    )(*arrays)


def over_z(block, k):
    return exchange(block, flip(8 * k))


class CubeSum:
    def __init__(self, keep, send):
        self.grads, self.keep, self.ahead = (keep, send), keep, send
        self.came, self.first, self.second, self.rest = None, None, None, None

    def part(self, *at):
        total = self.keep[at].astype(F32) + self.came[at].astype(F32)
        if self.first is not None:
            total = total + self.first[at[1:]].astype(F32)
        if self.second is not None:
            total = total + self.second[at[2:]].astype(F32)
        return total

    def send(self):
        if self.came is None:
            self.came = exchange(self.ahead, flip(1))
        elif self.first is None:
            self.ahead = self.part(1).astype(BF16)
            self.first = exchange(self.ahead, plane_partner("first"))
        elif self.second is None:
            self.ahead = self.part(0, 1).astype(BF16)
            self.second = exchange(self.ahead, plane_partner("second"))
        else:
            self.ahead = [self.part(0, 0, k).astype(BF16) for k in range(1, Z)]
            self.rest = [over_z(block, k) for k, block in enumerate(self.ahead, 1)]


def hold(first, *then):
    return tuple(lax.optimization_barrier((first, one))[1] for one in then)


def sum_over(values, *bits):
    for bit in bits:
        values = values + exchange(values, flip(bit))
    return values


def cut_any(blocks):
    every = blocks.reshape((Z, Y, X, CORES) + blocks.shape[1:])
    rest = tuple(range(3, every.ndim - 1))
    even = jnp.transpose(every[:, :, :, 0], (1, 2, 0) + rest)
    odd = jnp.transpose(every[:, :, :, 1], (2, 1, 0) + rest)
    return even[0], even[1], odd[0], odd[1]


def natural_blocks(keep, send):
    rest = tuple(range(3, keep.ndim))
    even = jnp.transpose(keep, (2, 0, 1) + rest)
    odd = jnp.transpose(send, (2, 1, 0) + rest)
    both = jnp.stack([even, odd], axis=3)
    return both.reshape((PIECES,) + both.shape[4:])


def on_device(
    tokens,
    segment_ids,
    time_embed,
    norm1_gain,
    norm1_shift,
    w_qkv,
    b_query,
    b_value,
    w_proj,
    b_proj,
    norm2_gain,
    norm2_shift,
    w_fc,
    b_fc,
    w_out,
    b_out,
    cotangent,
):
    row_count, row_len, width = tokens.shape
    toks = row_count * row_len
    devices = lax.axis_size("dp")
    cube = devices == PIECES
    rank = lax.axis_index("dp")
    grad_scale = 1.0 / math.sqrt(toks * devices)
    own = w_proj.shape[0]
    ratio = b_fc.shape[0] // own
    if cube:
        place = jnp.stack([rank // 8, (rank // 4) % 2, (rank // 2) % 2, rank % 2]).astype(jnp.int32)
    else:
        place = jnp.zeros((4,), jnp.int32)

    small = jnp.concatenate(
        [norm1_gain, norm1_shift, b_query, b_value, b_proj, norm2_gain, norm2_shift, b_out, b_fc]
    ).reshape(8 + ratio, own)
    order = list(range(8)) + [8 + 2 * h + k for k in range(ratio // 2) for h in range(2)]
    small = jnp.concatenate([small[v : v + 1] for v in order], axis=0)
    cut = width // PIECES
    halves = 2
    blocks = ratio // halves
    ffn_fc = lambda w: w.reshape(-1, PIECES, halves, blocks * cut).transpose(2, 0, 1, 3).reshape(halves, -1, blocks, width)
    if cube:
        ffn_block = jnp.concatenate(
            [ffn_fc(w_fc).transpose(0, 2, 1, 3), w_out.reshape(halves, blocks, own, width)], axis=1
        )
        small = jnp.pad(small, ((0, own - small.shape[0]), (0, 128 - own)))
        attn_gather = CubeGather(jnp.concatenate([w_qkv, w_proj, small], axis=1))
        early, late = CubeGather(ffn_block[0]), CubeGather(ffn_block[1])
        attn_gather.over_z(1, 2, 3)
        early.over_plane("second")
        late.over_plane("second")
        attn_gather.came, early.came, late.came = meet(attn_gather.came, early.came, late.came)
        attn_gather.take()
        early.take()
        late.take()
        attn_gather.over_plane("second")
        early.over_z(1, 3)
        attn_gather.came, early.came, late.ready = meet(attn_gather.came, early.came, late.ready)
        near = early.came
        attn_gather.take()
        attn_gather.over_plane("first")
        attn_gather.share()
        early.over_z(2)
        late.over_z(1, 2, 3)
        attn_gather.came, early.came = meet(attn_gather.came, early.came)
        attn_gather.finish()
        early.came = (near[0], early.came[0], near[1])
        early.take(axis=1)
        early.over_plane("first")
        early.share()
        attn_full = attn_gather.parts
    else:
        whole = lambda w: lax.all_gather(w, "dp", axis=0, tiled=True)
        natural = whole(small.T.reshape(own, -1))
        vectors = natural[:, :8].T
        hidden_bias = whole(b_fc).reshape(PIECES, ratio, cut)
        small = jnp.concatenate(
            [vectors.reshape(8, PIECES, cut).transpose(1, 0, 2), hidden_bias[:, jnp.array([0, 2, 1, 3])]], axis=1
        )
        small = jnp.pad(small, ((0, 0), (0, cut - small.shape[1]), (0, 128 - cut))).reshape(width, 128)
        attn_full = jnp.concatenate([whole(w_qkv), whole(w_proj), small], axis=1)
        attn_full = cut_any(attn_full.reshape(PIECES, cut, -1))
        fc_full = ffn_fc(whole(w_fc)).reshape(halves, PIECES, cut, blocks, width).transpose(1, 0, 3, 2, 4)
        out_full = whole(w_out).reshape(PIECES, halves, blocks, cut, width)
        ffn_full = jnp.concatenate([fc_full, out_full], axis=2)
        early, late = [cut_any(ffn_full[:, h].reshape(PIECES, -1, cut, width)) for h in range(halves)]

    flat = tokens.reshape(toks, width)
    times = time_embed.reshape(row_count, 1, width)
    segments = segment_ids.reshape(row_count, 1, row_len)
    cot = cotangent.reshape(toks, width)
    if cube:
        (segments,) = hold(early.ready, segments)
    n1, qkv, probs, att, hid, n2, attn_w, vec, bfc = attn_forward(place, flat, times, segments, attn_full)
    if cube:
        n2, early.came, early.shared, late.came = meet(n2, early.came, early.shared, late.came)
        early.finish()
        late.take(axis=1)
        late.over_plane("first")
        late.share()
        (n2,) = hold(late.ready, n2)
        early = early.parts
    out0, dn20, dbfc0, *grads0 = ffn(place, n2, cot, early, bfc, 0)
    sum0 = CubeSum(*grads0)
    if cube:
        out0, late.came, late.shared, sum0.ahead = meet(out0, late.came, late.shared, sum0.ahead)
        late.finish()
        sum0.send()
        sum0.send()
        (n2,) = hold(sum0.ahead, n2)
        late = late.parts
    out1, dn21, dbfc1, *grads1 = ffn(place, n2, cot, late, bfc, 1)
    sum1 = CubeSum(*grads1)
    if cube:
        out1, sum1.ahead, sum0.first = meet(out1, sum1.ahead, sum0.first)
        sum1.send()
        sum0.send()
        sum1.send()
        (hid,) = hold(sum1.ahead, *hold(sum0.ahead, hid))
    layer_out, d_tokens, d_time, dbr, dqkv, sums = attn_backward(
        flat, times, hid, (out0, out1), (dn20, dn21), cot, qkv, probs, attn_w, vec
    )
    if cube:
        dqkv, sum0.second, sum1.first = meet(dqkv, sum0.second, sum1.first)
        sum1.send()
        deep0 = [sum0.part(0, 0, k).astype(BF16) for k in (1, 3)]
        near0, wrap0 = over_z(deep0[0], 1), over_z(deep0[1], 3)
        (dqkv,) = hold(sum1.ahead, *hold(deep0[0], *hold(deep0[1], dqkv)))
    grads = weight_grad(place, n1, dqkv, att, dbr, sums, dbfc0, dbfc1)
    attn0, attn1 = CubeSum(*grads[:2]), CubeSum(*grads[2:])
    if cube:
        attn0.ahead, attn1.ahead, sum1.second, near0, wrap0 = meet(
            attn0.ahead, attn1.ahead, sum1.second, near0, wrap0
        )
        attn0.send()
        attn1.send()
        attn0.send()
        attn1.send()
        (sum1.second,) = hold(attn1.ahead, sum1.second)
        near1, wrap1 = [over_z(sum1.part(0, 0, k).astype(BF16), k) for k in (1, 3)]
        far = over_z(jnp.stack([s.part(0, 0, 2).astype(BF16) for s in (sum0, sum1)]), 2)
        sum0.rest = [near0, (far, 0), wrap0]
        sum1.rest = [near1, (far, 1), wrap1]
        attn0.send()
        for there in (attn0.second, near1, wrap1):
            (attn1.first,) = hold(there, attn1.first)
        attn1.send()
        attn0.send()
        own_fc, own_out = totals(
            ffn_total_body, (sum0, sum1), grad_scale, [(own, ratio * width), (ratio * own, width)], "ffn_total"
        )
        for there in (own_fc, attn0.rest[0], attn0.rest[2]):
            (attn1.second,) = hold(there, attn1.second)
        attn1.send()
        attn0.rest = hold(attn1.ahead[0], *attn0.rest)
        own_qkv, own_proj, vectors = totals(
            attn_total_body,
            (attn0, attn1),
            grad_scale,
            [(own, 3 * width), (own, width), (own, 128)],
            "attn_total",
        )
        mine = vectors[:8, :own]
        own_bfc = jnp.concatenate([vectors[8 + v, :own] for v in (0, 2, 1, 3)])
    else:
        scatter = lambda g: lax.psum_scatter(g, "dp", scatter_dimension=0, tiled=True)
        grads = jnp.concatenate([natural_blocks(*a.grads) for a in (attn0, attn1)], axis=-1).astype(F32)
        own_qkv = scatter(grads[:, :, : 3 * width].reshape(width, -1))
        own_proj = scatter(grads[:, :, 3 * width : 4 * width].reshape(width, -1))
        vectors = lax.psum(grads[:, :, 4 * width : 4 * width + cut], "dp")
        mine = lax.dynamic_slice(
            vectors[:, :8].transpose(1, 0, 2).reshape(8, width), (0, rank * own), (8, own)
        )
        hidden_grad = vectors[:, jnp.array([8, 10, 9, 11])].reshape(-1)
        own_bfc = lax.dynamic_slice(hidden_grad, (rank * own * ratio,), (own * ratio,))
        grads = jnp.stack([natural_blocks(*s.grads) for s in (sum0, sum1)], axis=1).astype(F32)
        out_grad = grads[:, :, blocks:].reshape(ratio * width, width)
        own_out = scatter(out_grad)
        fc_grad = grads[:, :, :blocks].transpose(0, 3, 1, 2, 4).reshape(width, halves, PIECES, blocks * cut)
        own_fc = scatter(fc_grad.transpose(0, 2, 1, 3).reshape(width, ratio * width))
        mine, own_bfc, own_qkv, own_proj, own_fc, own_out = [
            member * grad_scale for member in (mine, own_bfc, own_qkv, own_proj, own_fc, own_out)
        ]
    return (
        layer_out.reshape(tokens.shape),
        d_tokens.reshape(tokens.shape),
        d_time.reshape(time_embed.shape),
        mine[6],
        mine[7],
        own_qkv,
        mine[4],
        mine[5],
        own_proj,
        mine[2],
        mine[0],
        mine[1],
        own_fc,
        own_bfc,
        own_out,
        mine[3],
    )


def solution(mesh):
    in_specs = (
        P("dp", None, None),
        P("dp", None),
        P("dp", None),
        P("dp"),
        P("dp"),
        P("dp", None),
        P("dp"),
        P("dp"),
        P("dp", None),
        P("dp"),
        P("dp"),
        P("dp"),
        P("dp", None),
        P("dp"),
        P("dp", None),
        P("dp"),
        P("dp", None, None),
    )
    out_specs = (
        P("dp", None, None),
        P("dp", None, None),
        P("dp", None),
        P("dp"),
        P("dp"),
        P("dp", None),
        P("dp"),
        P("dp"),
        P("dp", None),
        P("dp"),
        P("dp"),
        P("dp"),
        P("dp", None),
        P("dp"),
        P("dp", None),
        P("dp"),
    )
    return jax.shard_map(
        on_device, mesh=mesh, in_specs=in_specs, out_specs=out_specs, check_vma=False
    )
```

```python
import functools
import math

import jax
import jax.numpy as jnp
from jax import lax
from jax.experimental import pallas as pl
from jax.experimental.pallas import tpu as pltpu
from jax.sharding import PartitionSpec as P

HD = 64
EPS = 1e-05
MASKED = -1e30
F32 = jnp.float32
BF16 = jnp.bfloat16
VMEM_LIMIT = 48 * 1024 * 1024
FFN_VMEM_LIMIT = 40 * 1024 * 1024


def dot(a, b, a_dim, b_dim):
    return lax.dot_general(a, b, (((a_dim,), (b_dim,)), ((), ())), preferred_element_type=F32)


def normalise(values):
    centered = values - jnp.mean(values, axis=-1, keepdims=True)
    spread = jnp.mean(centered * centered, axis=-1, keepdims=True)
    inv = lax.rsqrt(spread + EPS)
    return centered * inv, inv


def head_pair(block):
    lane = lax.broadcasted_iota(jnp.int32, block.shape, 1)
    zero = jnp.zeros_like(block)
    return jnp.concatenate([jnp.where(lane < HD, block, zero), jnp.where(lane >= HD, block, zero)], axis=0)


def own_lanes(stacked):
    half = stacked.shape[0] // 2
    lane = lax.broadcasted_iota(jnp.int32, (half, stacked.shape[1]), 1)
    return jnp.where(lane < HD, stacked[:half], stacked[half:])


def row_mask(seg_row):
    size = seg_row.shape[1]
    across = jnp.broadcast_to(seg_row.astype(F32), (size, size))
    return jnp.where(across == across.T, 0.0, MASKED)


def colsum(v):
    return jnp.sum(v, axis=0, keepdims=True)


Z, Y, X, CORES = 4, 2, 2, 2
PIECES = Z * Y * X * CORES


def merge_rows(blocks):
    count, rows, width = blocks.shape
    return blocks.astype(F32).reshape(count * rows, width).astype(BF16)


def slots(place, z, y, x):
    ys, xs = y ^ place[1], x ^ place[2]
    first = jnp.where(place[3] == 0, ys, xs)
    second = jnp.where(place[3] == 0, xs, ys)
    return first, second, place[0] ^ z


def put_blocks(place, z, y, x, even, odd, keep, send, tail=()):
    first, second, deep = slots(place, z, y, x)
    mine = place[3] == 0
    keep[(first, second, deep) + tail] = jnp.where(mine, even, odd)
    send[(second, first, deep) + tail] = jnp.where(mine, odd, even)


def pick(place, parts, z, y, x, tail=()):
    mine0, mine1, other0, other1 = parts
    first, second, deep = slots(place, z, y, x)
    mine = jnp.where(first == 0, mine0[(second, deep) + tail], mine1[(second, deep) + tail])
    other = jnp.where(second == 0, other0[(first, deep) + tail], other1[(first, deep) + tail])
    even = place[3] == 0
    return jnp.where(even, mine, other), jnp.where(even, other, mine)


def spread(small, cut, row, stride, start, length):
    lane = lax.broadcasted_iota(jnp.int32, (8, 128), 1)
    tiles = [jnp.zeros((8, 128), F32) for _ in range(length // 128)]
    for i in range(PIECES):
        at = start + i * stride
        tile, shift = at // 128, at % 128
        block = small[i * cut + row : i * cut + row + 8]
        if shift:
            block = pltpu.roll(block, shift, 1)
        if shift + cut <= 128:
            tiles[tile] = tiles[tile] + block
        else:
            tiles[tile] = tiles[tile] + jnp.where(lane >= shift, block, 0.0)
            tiles[tile + 1] = tiles[tile + 1] + jnp.where(lane < shift, block, 0.0)
    return jnp.concatenate(tiles, axis=1)


def attn_forward_body(
    place, tok, time, seg, mine0, mine1, other0, other1, n1, qkv, probs, att, hid, n2, weights, vec, bfc, *, rows
):
    size = tok.shape[0] // rows
    width = tok.shape[1]

    @pl.when(pl.program_id(0) == 0)
    def _():
        for z in range(Z):
            for y in range(Y):
                for x in range(X):
                    both = pick(place, (mine0, mine1, other0, other1), z, y, x)
                    both = jnp.concatenate([b.astype(F32) for b in both], axis=0)
                    step = both.shape[0]
                    at = ((z * Y + y) * X + x) * step
                    weights[at : at + step, :] = both.astype(BF16)
        small = weights[:, 4 * width :].astype(F32)
        cut = width // PIECES
        vec[...] = spread(small, cut, 0, cut, 0, width)
        early = spread(small, cut, 8, 2 * cut, 0, bfc.shape[1])
        late = spread(small, cut, 8, 2 * cut, cut, bfc.shape[1])
        bfc[...] = early[0:2] + late[2:4]

    x = tok[...].astype(F32)
    x = jnp.concatenate(
        [x[r * size : (r + 1) * size] + time[r].astype(F32) for r in range(rows)], axis=0
    )
    nhat, _ = normalise(x)
    normed = (nhat * vec[0:1, :] + vec[1:2, :]).astype(BF16)
    n1[...] = normed
    for part in range(3):
        cols = slice(part * width, (part + 1) * width)
        block = dot(normed, weights[:, cols], 1, 0)
        if part == 0:
            block = block + vec[2:3, :]
        if part == 2:
            block = block + vec[3:4, :]
        qkv[:, cols] = block.astype(BF16)
    pairs = width // (2 * HD)
    for r in range(rows):
        sl = slice(r * size, (r + 1) * size)
        mask = row_mask(seg[r])
        for p in range(pairs):
            c = 2 * HD * p
            q = qkv[sl, c : c + 2 * HD] * jnp.asarray(HD**-0.5, BF16)
            k = head_pair(qkv[sl, width + c : width + c + 2 * HD])
            v = head_pair(qkv[sl, 2 * width + c : 2 * width + c + 2 * HD])
            s = dot(k, q, 1, 1)
            halves = []
            for h in range(2):
                sh = s[h * size : (h + 1) * size] + mask
                e = jnp.exp(sh - jnp.max(sh, axis=0, keepdims=True))
                halves.append((e * (1.0 / jnp.sum(e, axis=0, keepdims=True))).astype(BF16))
            pr = jnp.concatenate(halves, axis=0)
            probs[r, p] = pr
            att[sl, c : c + 2 * HD] = dot(pr, v, 0, 0).astype(BF16)
    hidden = x + dot(att[...], weights[:, 3 * width : 4 * width], 1, 0) + vec[4:5, :]
    hid[...] = hidden
    nhat2, _ = normalise(hidden)
    n2[...] = (nhat2 * vec[5:6, :] + vec[6:7, :]).astype(BF16)


def attn_forward(place, tok, time, seg, gathered, rows=2):
    row_count = seg.shape[0]
    toks, width = tok.shape
    size = toks // row_count
    tm = rows * size
    pairs = width // (2 * HD)
    wide = gathered[0].shape[-1]
    full = lambda s: pl.BlockSpec(s, lambda i: (0,) * len(s))
    tile = lambda cols: pl.BlockSpec((tm, cols), lambda i: (i, 0))
    return pl.pallas_call(
        functools.partial(attn_forward_body, rows=rows),
        grid=(row_count // rows,),
        in_specs=[
            pl.BlockSpec(memory_space=pltpu.SMEM),
            tile(width),
            pl.BlockSpec((rows, 1, width), lambda i: (i, 0, 0)),
            pl.BlockSpec((rows, 1, size), lambda i: (i, 0, 0)),
        ]
        + [full(g.shape) for g in gathered],
        out_specs=[
            tile(width),
            tile(3 * width),
            pl.BlockSpec((rows, pairs, 2 * size, size), lambda i: (i, 0, 0, 0)),
            tile(width),
            tile(width),
            tile(width),
            full((width, wide)),
            full((8, width)),
            full((2, 2 * width)),
        ],
        out_shape=[
            jax.ShapeDtypeStruct((toks, width), BF16),
            jax.ShapeDtypeStruct((toks, 3 * width), BF16),
            jax.ShapeDtypeStruct((row_count, pairs, 2 * size, size), BF16),
            jax.ShapeDtypeStruct((toks, width), BF16),
            jax.ShapeDtypeStruct((toks, width), F32),
            jax.ShapeDtypeStruct((toks, width), BF16),
            jax.ShapeDtypeStruct((width, wide), BF16),
            jax.ShapeDtypeStruct((8, width), F32),
            jax.ShapeDtypeStruct((2, 2 * width), F32),
        ],
        compiler_params=pltpu.CompilerParams(vmem_limit_bytes=VMEM_LIMIT),
        cost_estimate=pl.CostEstimate(flops=16 * 10**9, bytes_accessed=20 * 10**6, transcendentals=2 * 10**6),
        name="attn_forward",
    )(place, tok, time, seg, *gathered)


def ffn_body(
    place, n2, cot, mine0, mine1, other0, other1, bfc, sum_out, sum_dn2, dbfc, keep, send, acc_out, acc_dn2, fc_s, out_s, act_s, dpre_s, *, tm, sub, half
):
    step = pl.program_id(0)

    @pl.when(step == 0)
    def _():
        acc_out[...] = jnp.zeros_like(acc_out)
        acc_dn2[...] = jnp.zeros_like(acc_dn2)

    gathered = (mine0, mine1, other0, other1)
    blocks, rows = 2, mine0.shape[-2]
    for z in range(Z):
        for y in range(Y):
            for x in range(X):
                both = pick(place, gathered, z, y, x, (step,))
                at = ((z * Y + y) * X + x) * CORES * rows
                fc_s[at : at + CORES * rows, :] = merge_rows(jnp.stack(both))
    for z in range(Z // blocks):
        for y in range(Y):
            for x in range(X):
                both = pick(place, gathered, step * (Z // blocks) + z, y, x, (slice(blocks, 2 * blocks),))
                at = ((z * Y + y) * X + x) * CORES * blocks * rows
                out_s[at : at + CORES * blocks * rows, :] = merge_rows(jnp.concatenate(both, axis=0))
    chunk = fc_s.shape[1]
    for part in range(chunk // sub):
        cols = slice(part * sub, (part + 1) * sub)
        bias = bfc[half : half + 1, cols]
        db = jnp.zeros_like(bias)
        for m in range(n2.shape[0] // tm):
            sl = slice(m * tm, (m + 1) * tm)
            pre = dot(n2[sl, :], fc_s[:, cols], 1, 0) + bias
            d_act = dot(cot[sl, :], out_s[cols, :], 1, 1)
            cdf = 0.5 * lax.erf(pre * math.sqrt(0.5)) + 0.5
            density = jnp.exp(pre * pre * -0.5) * (1.0 / math.sqrt(2.0 * math.pi))
            act = (pre * cdf).astype(BF16)
            d_pre = (d_act * (cdf + pre * density)).astype(BF16)
            act_s[sl, cols] = act
            dpre_s[sl, cols] = d_pre
            db = db + jnp.sum(d_pre.astype(F32), axis=0, keepdims=True)
            acc_out[sl, :] += dot(act, out_s[cols, :], 1, 0)
            acc_dn2[sl, :] += dot(d_pre, fc_s[:, cols], 1, 1)
        dbfc[:, cols] = db

    @pl.when(step == pl.num_programs(0) - 1)
    def _():
        sum_out[...] = acc_out[...].astype(BF16)
        sum_dn2[...] = acc_dn2[...].astype(BF16)

    grad = dot(act_s[...], cot[...], 0, 0)
    planes = Z // blocks
    for z in range(planes):
        for y in range(Y):
            for x in range(X):
                for b in range(blocks):
                    at = (((z * Y + y) * X + x) * CORES * blocks + b) * rows
                    even = grad[at : at + rows].astype(BF16)
                    odd = grad[at + blocks * rows : at + (blocks + 1) * rows].astype(BF16)
                    put_blocks(place, step * planes + z, y, x, even, odd, keep, send, (blocks + b,))
    grad = dot(n2[...], dpre_s[...], 0, 0)
    for z in range(Z):
        for y in range(Y):
            for x in range(X):
                at = ((z * Y + y) * X + x) * CORES * rows
                even = grad[at : at + rows].astype(BF16)
                odd = grad[at + rows : at + 2 * rows].astype(BF16)
                put_blocks(place, z, y, x, even, odd, keep, send, (step,))


def ffn(place, n2, cot, gathered, bfc, half, tm=512, sub=768):
    toks, width = n2.shape
    rows = width // PIECES
    blocks = 2
    count = 2 * blocks
    once = pl.Buffered(buffer_count=1)
    full = lambda s: pl.BlockSpec(s, lambda j: (0,) * len(s), pipeline_mode=once)
    whole = lambda s: pl.BlockSpec(s, lambda j: (0,) * len(s))
    parted = (Y, X, Z, count, rows, width)
    return pl.pallas_call(
        functools.partial(ffn_body, tm=tm, sub=sub, half=half),
        grid=(blocks,),
        in_specs=[
            pl.BlockSpec(memory_space=pltpu.SMEM),
            full((toks, width)),
            full((toks, width)),
        ]
        + [full(g.shape) for g in gathered]
        + [
            pl.BlockSpec((2, width), lambda j: (0, j)),
        ],
        out_specs=[
            whole((toks, width)),
            whole((toks, width)),
            pl.BlockSpec((1, width), lambda j: (0, j)),
            whole(parted),
            whole(parted),
        ],
        out_shape=[
            pltpu.HBM((toks, width), BF16),
            pltpu.HBM((toks, width), BF16),
            jax.ShapeDtypeStruct((1, blocks * width), F32),
            jax.ShapeDtypeStruct(parted, BF16),
            jax.ShapeDtypeStruct(parted, BF16),
        ],
        scratch_shapes=[
            pltpu.VMEM((toks, width), F32),
            pltpu.VMEM((toks, width), F32),
            pltpu.VMEM((width, width), BF16),
            pltpu.VMEM((width, width), BF16),
            pltpu.VMEM((toks, width), BF16),
            pltpu.VMEM((toks, width), BF16),
        ],
        compiler_params=pltpu.CompilerParams(vmem_limit_bytes=FFN_VMEM_LIMIT),
        cost_estimate=pl.CostEstimate(flops=15 * 10**9, bytes_accessed=20 * 10**6, transcendentals=3 * 10**6),
        name="ffn",
    )(place, n2, cot, *gathered, bfc)


def attn_backward_body(
    tok, time, hid, out0, out1, dn20, dn21, cot, qkv, probs, weights, vec, layer_out, dtok, dtime, dbr, dqkv, sums, *, rows
):
    width = hid.shape[1]
    size = hid.shape[0] // rows

    @pl.when(pl.program_id(0) == 0)
    def _():
        sums[...] = jnp.zeros_like(sums)

    hidden = hid[...]
    layer_out[...] = (hidden + (out0[...].astype(F32) + out1[...].astype(F32)) + vec[7:8, :]).astype(BF16)
    nhat, inv = normalise(hidden)
    dn2 = dn20[...].astype(F32) + dn21[...].astype(F32)
    cotangent = cot[...].astype(F32)
    q = dn2 * vec[5:6, :]
    mean_q = jnp.mean(q, axis=-1, keepdims=True)
    mean_qn = jnp.mean(q * nhat, axis=-1, keepdims=True)
    d_hidden = cotangent + (q - mean_q - nhat * mean_qn) * inv
    dtok[...] = d_hidden
    branch = d_hidden.astype(BF16)
    dbr[...] = branch
    sums[0:1, :] += colsum(dn2 * nhat)
    sums[1:2, :] += colsum(dn2)
    sums[2:3, :] += colsum(branch.astype(F32))
    sums[3:4, :] += colsum(cotangent)
    d_mixed = dot(branch, weights[:, 3 * width : 4 * width], 1, 1).astype(BF16)
    pairs = width // (2 * HD)
    for r in range(rows):
        sl = slice(r * size, (r + 1) * size)
        for p in range(pairs):
            c = 2 * HD * p
            qb = qkv[sl, c : c + 2 * HD] * jnp.asarray(HD**-0.5, BF16)
            k = head_pair(qkv[sl, width + c : width + c + 2 * HD])
            v = head_pair(qkv[sl, 2 * width + c : 2 * width + c + 2 * HD])
            dm = d_mixed[sl, c : c + 2 * HD]
            pr = probs[r, p]
            dp = dot(v, dm, 1, 1)
            halves = []
            for h in range(2):
                pf = pr[h * size : (h + 1) * size].astype(F32)
                dph = dp[h * size : (h + 1) * size]
                halves.append((pf * (dph - jnp.sum(dph * pf, axis=0, keepdims=True))).astype(BF16))
            ds = jnp.concatenate(halves, axis=0)
            dv = own_lanes(dot(pr, dm, 1, 0))
            dk = own_lanes(dot(ds, qb, 1, 0))
            dq = dot(ds, k, 0, 0) * HD**-0.5
            dqkv[sl, c : c + 2 * HD] = dq.astype(BF16)
            dqkv[sl, width + c : width + c + 2 * HD] = dk.astype(BF16)
            dqkv[sl, 2 * width + c : 2 * width + c + 2 * HD] = dv.astype(BF16)
    sums[4:5, :] += colsum(dqkv[:, :width].astype(F32))
    sums[5:6, :] += colsum(dqkv[:, 2 * width :].astype(F32))

    x = tok[...].astype(F32)
    x = jnp.concatenate(
        [x[r * size : (r + 1) * size] + time[r].astype(F32) for r in range(rows)], axis=0
    )
    nhat, inv = normalise(x)
    dn1 = dot(dqkv[...], weights[:, : 3 * width], 1, 1)
    sums[6:7, :] += colsum(dn1 * nhat)
    sums[7:8, :] += colsum(dn1)
    q = dn1 * vec[0:1, :]
    mean_q = jnp.mean(q, axis=-1, keepdims=True)
    mean_qn = jnp.mean(q * nhat, axis=-1, keepdims=True)
    d_tok = dtok[...] + (q - mean_q - nhat * mean_qn) * inv
    dtok[...] = d_tok
    for r in range(rows):
        dtime[r] = colsum(d_tok[r * size : (r + 1) * size])


def attn_backward(tok, time, hid, outs, dn2s, cot, qkv, probs, weights, vec, rows=2):
    row_count, pairs, _, size = probs.shape
    width = hid.shape[1]
    tm = rows * size
    toks = row_count * size
    steps = row_count // rows
    once = pl.Buffered(buffer_count=1)
    full = lambda s: pl.BlockSpec(s, lambda i: (0,) * len(s), pipeline_mode=once)
    tile = lambda cols: pl.BlockSpec((tm, cols), lambda i: (i, 0))
    per_row = pl.BlockSpec((rows, 1, width), lambda i: (i, 0, 0))
    return pl.pallas_call(
        functools.partial(attn_backward_body, rows=rows),
        grid=(steps,),
        in_specs=[tile(width), per_row]
        + [tile(width)] * 6
        + [
            tile(3 * width),
            pl.BlockSpec((rows, pairs, 2 * size, size), lambda i: (i, 0, 0, 0)),
            full(weights.shape),
            full(vec.shape),
        ],
        out_specs=[
            tile(width),
            tile(width),
            per_row,
            tile(width),
            tile(3 * width),
            pl.BlockSpec((8, width), lambda i: (0, 0)),
        ],
        out_shape=[
            jax.ShapeDtypeStruct((toks, width), BF16),
            jax.ShapeDtypeStruct((toks, width), F32),
            jax.ShapeDtypeStruct((row_count, 1, width), F32),
            jax.ShapeDtypeStruct((toks, width), BF16),
            jax.ShapeDtypeStruct((toks, 3 * width), BF16),
            jax.ShapeDtypeStruct((8, width), F32),
        ],
        compiler_params=pltpu.CompilerParams(vmem_limit_bytes=VMEM_LIMIT),
        cost_estimate=pl.CostEstimate(flops=6 * 10**9 * steps, bytes_accessed=10 * 10**6 * steps, transcendentals=0),
        name="attn_backward",
    )(tok, time, hid, *outs, *dn2s, cot, qkv, probs, weights, vec)


def collect(vectors, cut, stride, start, piece):
    at = start + piece * stride
    tile, shift = at // 128, at % 128
    lane = lax.broadcasted_iota(jnp.int32, (vectors.shape[0], 128), 1)
    block = vectors[:, tile * 128 : (tile + 1) * 128]
    if shift + cut > 128:
        block = jnp.where(lane >= shift, block, vectors[:, (tile + 1) * 128 : (tile + 2) * 128])
    if shift:
        block = pltpu.roll(block, 128 - shift, 1)
    return jnp.where(lane < cut, block, 0.0)


def weight_grad_body(place, n1, dqkv, att, dbr, sums, dbfc0, dbfc1, keep0, send0, keep1, send1):
    rows = keep0.shape[3]
    width = n1.shape[1]
    step = pl.program_id(0)

    def emit(grad, keep, send, at_column):
        tail = (slice(None), slice(at_column, at_column + grad.shape[1]))
        for z in range(Z):
            for y in range(Y):
                for x in range(X):
                    at = ((z * Y + y) * X + x) * CORES * rows
                    even = grad[at : at + rows].astype(BF16)
                    odd = grad[at + rows : at + 2 * rows].astype(BF16)
                    put_blocks(place, z, y, x, even, odd, keep, send, tail)

    for k in range(2):

        @pl.when(step == k)
        def _(k=k):
            emit(dot(n1[...], dqkv[...], 0, 0), keep0, send0, k * width)

    @pl.when(step == 2)
    def _():
        emit(dot(n1[...], dqkv[...], 0, 0), keep1, send1, 0)

    @pl.when(step == 3)
    def _():
        emit(dot(att[...], dbr[...], 0, 0), keep1, send1, width)
        vectors = sums[...]
        pad = jnp.zeros((6, dbfc0.shape[1]), F32)
        hidden = jnp.concatenate([dbfc0[...], dbfc1[...], pad], axis=0)

        def block(piece):
            early = collect(hidden, rows, 2 * rows, 0, piece)
            late = collect(hidden, rows, 2 * rows, rows, piece)
            top = collect(vectors, rows, rows, 0, piece)
            rest = [early[:2], late[:2], jnp.zeros((rows - 12, 128), F32)]
            return jnp.concatenate([top] + rest, axis=0).astype(BF16)

        tail = (slice(None), slice(2 * width, 2 * width + 128))
        for z in range(Z):
            for y in range(Y):
                for x in range(X):
                    piece = ((z * Y + y) * X + x) * CORES
                    put_blocks(place, z, y, x, block(piece), block(piece + 1), keep1, send1, tail)


def weight_grad(place, n1, dqkv, att, dbr, sums, dbfc0, dbfc1):
    toks, width = n1.shape
    rows = width // PIECES
    once = pl.Buffered(buffer_count=1)
    full = lambda a: pl.BlockSpec(a.shape, lambda j: (0, 0), pipeline_mode=once)
    shapes = [(Y, X, Z, rows, columns) for columns in (2 * width, 2 * width + 128) for _ in range(2)]
    return pl.pallas_call(
        weight_grad_body,
        grid=(4,),
        in_specs=[
            pl.BlockSpec(memory_space=pltpu.SMEM),
            full(n1),
            pl.BlockSpec((toks, width), lambda j: (0, jnp.minimum(j, 2))),
        ]
        + [full(e) for e in (att, dbr, sums, dbfc0, dbfc1)],
        out_specs=[pl.BlockSpec(shape, lambda j: (0,) * 5) for shape in shapes],
        out_shape=[jax.ShapeDtypeStruct(shape, BF16) for shape in shapes],
        compiler_params=pltpu.CompilerParams(vmem_limit_bytes=VMEM_LIMIT),
        cost_estimate=pl.CostEstimate(flops=5 * 10**9, bytes_accessed=16 * 10**6, transcendentals=0),
        name="weight_grad",
    )(place, n1, dqkv, att, dbr, sums, dbfc0, dbfc1)


def flip(position):
    return lambda i: i ^ position


def exchange(array, partner):
    return lax.ppermute(array, "dp", [(i, partner(i)) for i in range(PIECES)])


def plane_partner(stage):
    def partner(i):
        along_y = (i % 2 == 0) == (stage == "first")
        return i ^ (4 if along_y else 2)

    return partner


class CubeGather:
    def __init__(self, block):
        self.ready, self.came, self.parts = block, None, None

    def over_z(self, *steps):
        self.came = tuple(exchange(self.ready, flip(8 * k)) for k in steps)

    def over_plane(self, stage):
        self.came = (exchange(self.ready, plane_partner(stage)),)

    def take(self, axis=0):
        self.ready = jnp.stack((self.ready,) + tuple(self.came), axis=axis)

    def share(self):
        self.shared = exchange(self.ready, flip(1))

    def finish(self):
        self.parts = (self.ready, self.came[0], self.shared, exchange(self.came[0], flip(1)))


def meet(*things):
    return lax.optimization_barrier(things)


def total_body(*refs, scale, counts):
    outs = refs[7 * counts :]
    totals = []
    for k in range(counts):
        parts = [r[...].astype(F32) for r in refs[7 * k : 7 * k + 7]]
        totals.append(sum(parts[1:], parts[0]).reshape(parts[-1].shape) * scale)
    return totals, outs


def ffn_total_body(*refs, scale):
    totals, (d_fc, d_out) = total_body(*refs, scale=scale, counts=2)
    _, rows, width = totals[0].shape
    lane = lax.broadcasted_iota(jnp.int32, (rows, 128), 1)
    columns = [jnp.concatenate([t[0], t[1]], axis=1) for t in totals]
    for half, total in enumerate(totals):
        for b in range(2):
            at = (half * 2 + b) * rows
            d_out[at : at + rows, :] = total[2 + b]
    step = 2 * rows
    for t in range(4 * width // 128):
        tile = jnp.zeros((rows, 128), F32)
        for q in range(t * 128 // step, (t * 128 + 127) // step + 1):
            at, source = q * step - t * 128, (q // 2) * step
            first, shift = source // 128, source % 128
            block = columns[q % 2][:, first * 128 : (first + 1) * 128]
            if shift + step > 128:
                following = columns[q % 2][:, (first + 1) * 128 : (first + 2) * 128]
                block = jnp.where(lane >= shift, block, following)
            if (at - shift) % 128:
                block = pltpu.roll(block, (at - shift) % 128, 1)
            tile = jnp.where((lane >= at) & (lane < at + step), block, tile)
        d_fc[:, t * 128 : (t + 1) * 128] = tile


def attn_total_body(*refs, scale):
    (left, right), (d_qkv, d_proj, vectors) = total_body(*refs, scale=scale, counts=2)
    width = d_proj.shape[1]
    d_qkv[:, : 2 * width] = left
    d_qkv[:, 2 * width :] = right[:, :width]
    d_proj[...] = right[:, width : 2 * width]
    vectors[...] = right[:, 2 * width :]


def totals(body, sums, scale, shapes, name):
    pieces = [a for s in sums for a in (s.keep, s.came, s.first, s.second) + tuple(s.rest)]
    arrays = [a[0] if isinstance(a, tuple) else a for a in pieces]
    blocks = [s.rest[-1].shape for s in sums for _ in range(7)]

    def spec(piece, block):
        array, index = piece if isinstance(piece, tuple) else (piece, 0)
        lead = len(array.shape) - len(block)
        at = (index,) + (0,) * (len(array.shape) - 1)
        return pl.BlockSpec((1,) * lead + tuple(block), lambda i: at)

    return pl.pallas_call(
        functools.partial(body, scale=scale),
        grid=(1,),
        in_specs=[spec(p, b) for p, b in zip(pieces, blocks)],
        out_shape=[jax.ShapeDtypeStruct(shape, F32) for shape in shapes],
        compiler_params=pltpu.CompilerParams(vmem_limit_bytes=VMEM_LIMIT),
        cost_estimate=pl.CostEstimate(flops=10**6, bytes_accessed=5 * 10**6, transcendentals=0),
        name=name,
    )(*arrays)


def over_z(block, k):
    return exchange(block, flip(8 * k))


class CubeSum:
    def __init__(self, keep, send):
        self.grads, self.keep, self.ahead = (keep, send), keep, send
        self.came, self.first, self.second, self.rest = None, None, None, None

    def part(self, *at):
        total = self.keep[at].astype(F32) + self.came[at].astype(F32)
        if self.first is not None:
            total = total + self.first[at[1:]].astype(F32)
        if self.second is not None:
            total = total + self.second[at[2:]].astype(F32)
        return total

    def send(self):
        if self.came is None:
            self.came = exchange(self.ahead, flip(1))
        elif self.first is None:
            self.ahead = self.part(1).astype(BF16)
            self.first = exchange(self.ahead, plane_partner("first"))
        elif self.second is None:
            self.ahead = self.part(0, 1).astype(BF16)
            self.second = exchange(self.ahead, plane_partner("second"))
        else:
            self.ahead = [self.part(0, 0, k).astype(BF16) for k in range(1, Z)]
            self.rest = [over_z(block, k) for k, block in enumerate(self.ahead, 1)]


def hold(first, *then):
    return tuple(lax.optimization_barrier((first, one))[1] for one in then)


def sum_over(values, *bits):
    for bit in bits:
        values = values + exchange(values, flip(bit))
    return values


def cut_any(blocks):
    every = blocks.reshape((Z, Y, X, CORES) + blocks.shape[1:])
    rest = tuple(range(3, every.ndim - 1))
    even = jnp.transpose(every[:, :, :, 0], (1, 2, 0) + rest)
    odd = jnp.transpose(every[:, :, :, 1], (2, 1, 0) + rest)
    return even[0], even[1], odd[0], odd[1]


def natural_blocks(keep, send):
    rest = tuple(range(3, keep.ndim))
    even = jnp.transpose(keep, (2, 0, 1) + rest)
    odd = jnp.transpose(send, (2, 1, 0) + rest)
    both = jnp.stack([even, odd], axis=3)
    return both.reshape((PIECES,) + both.shape[4:])


def on_device(
    tokens,
    segment_ids,
    time_embed,
    norm1_gain,
    norm1_shift,
    w_qkv,
    b_query,
    b_value,
    w_proj,
    b_proj,
    norm2_gain,
    norm2_shift,
    w_fc,
    b_fc,
    w_out,
    b_out,
    cotangent,
):
    row_count, row_len, width = tokens.shape
    toks = row_count * row_len
    devices = lax.axis_size("dp")
    cube = devices == PIECES
    rank = lax.axis_index("dp")
    grad_scale = 1.0 / math.sqrt(toks * devices)
    own = w_proj.shape[0]
    ratio = b_fc.shape[0] // own
    if cube:
        place = jnp.stack([rank // 8, (rank // 4) % 2, (rank // 2) % 2, rank % 2]).astype(jnp.int32)
    else:
        place = jnp.zeros((4,), jnp.int32)

    small = jnp.concatenate(
        [norm1_gain, norm1_shift, b_query, b_value, b_proj, norm2_gain, norm2_shift, b_out, b_fc]
    ).reshape(8 + ratio, own)
    order = list(range(8)) + [8 + 2 * h + k for k in range(ratio // 2) for h in range(2)]
    small = jnp.concatenate([small[v : v + 1] for v in order], axis=0)
    cut = width // PIECES
    halves = 2
    blocks = ratio // halves
    ffn_fc = lambda w: w.reshape(-1, PIECES, halves, blocks * cut).transpose(2, 0, 1, 3).reshape(halves, -1, blocks, width)
    if cube:
        ffn_block = jnp.concatenate(
            [ffn_fc(w_fc).transpose(0, 2, 1, 3), w_out.reshape(halves, blocks, own, width)], axis=1
        )
        small = jnp.pad(small, ((0, own - small.shape[0]), (0, 128 - own)))
        attn_gather = CubeGather(jnp.concatenate([w_qkv, w_proj, small], axis=1))
        early, late = CubeGather(ffn_block[0]), CubeGather(ffn_block[1])
        attn_gather.over_z(1, 2, 3)
        early.over_plane("second")
        late.over_plane("second")
        attn_gather.came, early.came, late.came = meet(attn_gather.came, early.came, late.came)
        attn_gather.take()
        early.take()
        late.take()
        attn_gather.over_plane("second")
        early.over_z(3)
        attn_gather.came, early.came, late.ready = meet(attn_gather.came, early.came, late.ready)
        (wrap,) = early.came
        attn_gather.take()
        attn_gather.over_plane("first")
        attn_gather.share()
        early.over_z(1, 2)
        late.over_z(1, 2, 3)
        attn_gather.came, early.came = meet(attn_gather.came, early.came)
        attn_gather.finish()
        early.came = early.came + (wrap,)
        early.take(axis=1)
        early.over_plane("first")
        early.share()
        attn_full = attn_gather.parts
    else:
        whole = lambda w: lax.all_gather(w, "dp", axis=0, tiled=True)
        natural = whole(small.T.reshape(own, -1))
        vectors = natural[:, :8].T
        hidden_bias = whole(b_fc).reshape(PIECES, ratio, cut)
        small = jnp.concatenate(
            [vectors.reshape(8, PIECES, cut).transpose(1, 0, 2), hidden_bias[:, jnp.array([0, 2, 1, 3])]], axis=1
        )
        small = jnp.pad(small, ((0, 0), (0, cut - small.shape[1]), (0, 128 - cut))).reshape(width, 128)
        attn_full = jnp.concatenate([whole(w_qkv), whole(w_proj), small], axis=1)
        attn_full = cut_any(attn_full.reshape(PIECES, cut, -1))
        fc_full = ffn_fc(whole(w_fc)).reshape(halves, PIECES, cut, blocks, width).transpose(1, 0, 3, 2, 4)
        out_full = whole(w_out).reshape(PIECES, halves, blocks, cut, width)
        ffn_full = jnp.concatenate([fc_full, out_full], axis=2)
        early, late = [cut_any(ffn_full[:, h].reshape(PIECES, -1, cut, width)) for h in range(halves)]

    flat = tokens.reshape(toks, width)
    times = time_embed.reshape(row_count, 1, width)
    segments = segment_ids.reshape(row_count, 1, row_len)
    cot = cotangent.reshape(toks, width)
    if cube:
        (segments,) = hold(early.ready, segments)
    n1, qkv, probs, att, hid, n2, attn_w, vec, bfc = attn_forward(place, flat, times, segments, attn_full)
    if cube:
        n2, early.came, early.shared, late.came = meet(n2, early.came, early.shared, late.came)
        early.finish()
        late.take(axis=1)
        late.over_plane("first")
        late.share()
        (n2,) = hold(late.ready, n2)
        early = early.parts
    out0, dn20, dbfc0, *grads0 = ffn(place, n2, cot, early, bfc, 0)
    sum0 = CubeSum(*grads0)
    if cube:
        out0, late.came, late.shared, sum0.ahead = meet(out0, late.came, late.shared, sum0.ahead)
        late.finish()
        sum0.send()
        sum0.send()
        (n2,) = hold(sum0.ahead, n2)
        late = late.parts
    out1, dn21, dbfc1, *grads1 = ffn(place, n2, cot, late, bfc, 1)
    sum1 = CubeSum(*grads1)
    if cube:
        out1, sum1.ahead, sum0.first = meet(out1, sum1.ahead, sum0.first)
        sum1.send()
        sum0.send()
        sum1.send()
        (hid,) = hold(sum1.ahead, *hold(sum0.ahead, hid))
    layer_out, d_tokens, d_time, dbr, dqkv, sums = attn_backward(
        flat, times, hid, (out0, out1), (dn20, dn21), cot, qkv, probs, attn_w, vec
    )
    if cube:
        dqkv, sum0.second, sum1.first = meet(dqkv, sum0.second, sum1.first)
        sum1.send()
        deep0 = sum0.part(0, 0, 3).astype(BF16)
        wrap0 = over_z(deep0, 3)
        (dqkv,) = hold(sum1.ahead, *hold(deep0, dqkv))
    grads = weight_grad(place, n1, dqkv, att, dbr, sums, dbfc0, dbfc1)
    attn0, attn1 = CubeSum(*grads[:2]), CubeSum(*grads[2:])
    if cube:
        attn0.ahead, attn1.ahead, sum1.second, wrap0 = meet(attn0.ahead, attn1.ahead, sum1.second, wrap0)
        attn0.send()
        attn1.send()
        attn0.send()
        attn1.send()
        (sum1.second,) = hold(attn1.ahead, sum1.second)
        wrap1 = over_z(sum1.part(0, 0, 3).astype(BF16), 3)
        near, far = [
            over_z(jnp.stack([s.part(0, 0, k).astype(BF16) for s in (sum0, sum1)]), k) for k in (1, 2)
        ]
        sum0.rest = [(near, 0), (far, 0), wrap0]
        sum1.rest = [(near, 1), (far, 1), wrap1]
        attn0.send()
        for there in (attn0.second, near, wrap1):
            (attn1.first,) = hold(there, attn1.first)
        attn1.send()
        attn0.send()
        own_fc, own_out = totals(
            ffn_total_body, (sum0, sum1), grad_scale, [(own, ratio * width), (ratio * own, width)], "ffn_total"
        )
        for there in (own_fc, attn0.rest[0], attn0.rest[2]):
            (attn1.second,) = hold(there, attn1.second)
        attn1.send()
        attn0.rest = hold(attn1.ahead[0], *attn0.rest)
        own_qkv, own_proj, vectors = totals(
            attn_total_body,
            (attn0, attn1),
            grad_scale,
            [(own, 3 * width), (own, width), (own, 128)],
            "attn_total",
        )
        mine = vectors[:8, :own]
        own_bfc = jnp.concatenate([vectors[8 + v, :own] for v in (0, 2, 1, 3)])
    else:
        scatter = lambda g: lax.psum_scatter(g, "dp", scatter_dimension=0, tiled=True)
        grads = jnp.concatenate([natural_blocks(*a.grads) for a in (attn0, attn1)], axis=-1).astype(F32)
        own_qkv = scatter(grads[:, :, : 3 * width].reshape(width, -1))
        own_proj = scatter(grads[:, :, 3 * width : 4 * width].reshape(width, -1))
        vectors = lax.psum(grads[:, :, 4 * width : 4 * width + cut], "dp")
        mine = lax.dynamic_slice(
            vectors[:, :8].transpose(1, 0, 2).reshape(8, width), (0, rank * own), (8, own)
        )
        hidden_grad = vectors[:, jnp.array([8, 10, 9, 11])].reshape(-1)
        own_bfc = lax.dynamic_slice(hidden_grad, (rank * own * ratio,), (own * ratio,))
        grads = jnp.stack([natural_blocks(*s.grads) for s in (sum0, sum1)], axis=1).astype(F32)
        out_grad = grads[:, :, blocks:].reshape(ratio * width, width)
        own_out = scatter(out_grad)
        fc_grad = grads[:, :, :blocks].transpose(0, 3, 1, 2, 4).reshape(width, halves, PIECES, blocks * cut)
        own_fc = scatter(fc_grad.transpose(0, 2, 1, 3).reshape(width, ratio * width))
        mine, own_bfc, own_qkv, own_proj, own_fc, own_out = [
            member * grad_scale for member in (mine, own_bfc, own_qkv, own_proj, own_fc, own_out)
        ]
    return (
        layer_out.reshape(tokens.shape),
        d_tokens.reshape(tokens.shape),
        d_time.reshape(time_embed.shape),
        mine[6],
        mine[7],
        own_qkv,
        mine[4],
        mine[5],
        own_proj,
        mine[2],
        mine[0],
        mine[1],
        own_fc,
        own_bfc,
        own_out,
        mine[3],
    )


def solution(mesh):
    in_specs = (
        P("dp", None, None),
        P("dp", None),
        P("dp", None),
        P("dp"),
        P("dp"),
        P("dp", None),
        P("dp"),
        P("dp"),
        P("dp", None),
        P("dp"),
        P("dp"),
        P("dp"),
        P("dp", None),
        P("dp"),
        P("dp", None),
        P("dp"),
        P("dp", None, None),
    )
    out_specs = (
        P("dp", None, None),
        P("dp", None, None),
        P("dp", None),
        P("dp"),
        P("dp"),
        P("dp", None),
        P("dp"),
        P("dp"),
        P("dp", None),
        P("dp"),
        P("dp"),
        P("dp"),
        P("dp", None),
        P("dp"),
        P("dp", None),
        P("dp"),
    )
    return jax.shard_map(
        on_device, mesh=mesh, in_specs=in_specs, out_specs=out_specs, check_vma=False
    )
```

```python
import functools
import math

import jax
import jax.numpy as jnp
from jax import lax
from jax.experimental import pallas as pl
from jax.experimental.pallas import tpu as pltpu
from jax.sharding import PartitionSpec as P

HD = 64
EPS = 1e-05
MASKED = -1e30
F32 = jnp.float32
BF16 = jnp.bfloat16
VMEM_LIMIT = 48 * 1024 * 1024
FFN_VMEM_LIMIT = 40 * 1024 * 1024


def dot(a, b, a_dim, b_dim):
    return lax.dot_general(a, b, (((a_dim,), (b_dim,)), ((), ())), preferred_element_type=F32)


def normalise(values):
    centered = values - jnp.mean(values, axis=-1, keepdims=True)
    spread = jnp.mean(centered * centered, axis=-1, keepdims=True)
    inv = lax.rsqrt(spread + EPS)
    return centered * inv, inv


def head_pair(block):
    lane = lax.broadcasted_iota(jnp.int32, block.shape, 1)
    zero = jnp.zeros_like(block)
    return jnp.concatenate([jnp.where(lane < HD, block, zero), jnp.where(lane >= HD, block, zero)], axis=0)


def own_lanes(stacked):
    half = stacked.shape[0] // 2
    lane = lax.broadcasted_iota(jnp.int32, (half, stacked.shape[1]), 1)
    return jnp.where(lane < HD, stacked[:half], stacked[half:])


def row_mask(seg_row):
    size = seg_row.shape[1]
    across = jnp.broadcast_to(seg_row.astype(F32), (size, size))
    return jnp.where(across == across.T, 0.0, MASKED)


def colsum(v):
    return jnp.sum(v, axis=0, keepdims=True)


Z, Y, X, CORES = 4, 2, 2, 2
PIECES = Z * Y * X * CORES


def merge_rows(blocks):
    count, rows, width = blocks.shape
    return blocks.astype(F32).reshape(count * rows, width).astype(BF16)


def slots(place, z, y, x):
    ys, xs = y ^ place[1], x ^ place[2]
    first = jnp.where(place[3] == 0, ys, xs)
    second = jnp.where(place[3] == 0, xs, ys)
    return first, second, place[0] ^ z


def put_blocks(place, z, y, x, even, odd, keep, send, tail=()):
    first, second, deep = slots(place, z, y, x)
    mine = place[3] == 0
    keep[(first, second, deep) + tail] = jnp.where(mine, even, odd)
    send[(second, first, deep) + tail] = jnp.where(mine, odd, even)


def pick(place, parts, z, y, x, tail=()):
    mine0, mine1, other0, other1 = parts
    first, second, deep = slots(place, z, y, x)
    mine = jnp.where(first == 0, mine0[(second, deep) + tail], mine1[(second, deep) + tail])
    other = jnp.where(second == 0, other0[(first, deep) + tail], other1[(first, deep) + tail])
    even = place[3] == 0
    return jnp.where(even, mine, other), jnp.where(even, other, mine)


def spread(small, cut, row, stride, start, length):
    lane = lax.broadcasted_iota(jnp.int32, (8, 128), 1)
    tiles = [jnp.zeros((8, 128), F32) for _ in range(length // 128)]
    for i in range(PIECES):
        at = start + i * stride
        tile, shift = at // 128, at % 128
        block = small[i * cut + row : i * cut + row + 8]
        if shift:
            block = pltpu.roll(block, shift, 1)
        if shift + cut <= 128:
            tiles[tile] = tiles[tile] + block
        else:
            tiles[tile] = tiles[tile] + jnp.where(lane >= shift, block, 0.0)
            tiles[tile + 1] = tiles[tile + 1] + jnp.where(lane < shift, block, 0.0)
    return jnp.concatenate(tiles, axis=1)


def attn_forward_body(
    place, tok, time, seg, mine0, mine1, other0, other1, n1, qkv, probs, att, hid, n2, weights, vec, bfc, *, rows
):
    size = tok.shape[0] // rows
    width = tok.shape[1]

    @pl.when(pl.program_id(0) == 0)
    def _():
        for z in range(Z):
            for y in range(Y):
                for x in range(X):
                    both = pick(place, (mine0, mine1, other0, other1), z, y, x)
                    both = jnp.concatenate([b.astype(F32) for b in both], axis=0)
                    step = both.shape[0]
                    at = ((z * Y + y) * X + x) * step
                    weights[at : at + step, :] = both.astype(BF16)
        small = weights[:, 4 * width :].astype(F32)
        cut = width // PIECES
        vec[...] = spread(small, cut, 0, cut, 0, width)
        early = spread(small, cut, 8, 2 * cut, 0, bfc.shape[1])
        late = spread(small, cut, 8, 2 * cut, cut, bfc.shape[1])
        bfc[...] = early[0:2] + late[2:4]

    x = tok[...].astype(F32)
    x = jnp.concatenate(
        [x[r * size : (r + 1) * size] + time[r].astype(F32) for r in range(rows)], axis=0
    )
    nhat, _ = normalise(x)
    normed = (nhat * vec[0:1, :] + vec[1:2, :]).astype(BF16)
    n1[...] = normed
    for part in range(3):
        cols = slice(part * width, (part + 1) * width)
        block = dot(normed, weights[:, cols], 1, 0)
        if part == 0:
            block = block + vec[2:3, :]
        if part == 2:
            block = block + vec[3:4, :]
        qkv[:, cols] = block.astype(BF16)
    pairs = width // (2 * HD)
    for r in range(rows):
        sl = slice(r * size, (r + 1) * size)
        mask = row_mask(seg[r])
        for p in range(pairs):
            c = 2 * HD * p
            q = qkv[sl, c : c + 2 * HD] * jnp.asarray(HD**-0.5, BF16)
            k = head_pair(qkv[sl, width + c : width + c + 2 * HD])
            v = head_pair(qkv[sl, 2 * width + c : 2 * width + c + 2 * HD])
            s = dot(k, q, 1, 1)
            halves = []
            for h in range(2):
                sh = s[h * size : (h + 1) * size] + mask
                e = jnp.exp(sh - jnp.max(sh, axis=0, keepdims=True))
                halves.append((e * (1.0 / jnp.sum(e, axis=0, keepdims=True))).astype(BF16))
            pr = jnp.concatenate(halves, axis=0)
            probs[r, p] = pr
            att[sl, c : c + 2 * HD] = dot(pr, v, 0, 0).astype(BF16)
    hidden = x + dot(att[...], weights[:, 3 * width : 4 * width], 1, 0) + vec[4:5, :]
    hid[...] = hidden
    nhat2, _ = normalise(hidden)
    n2[...] = (nhat2 * vec[5:6, :] + vec[6:7, :]).astype(BF16)


def attn_forward(place, tok, time, seg, gathered, rows=2):
    row_count = seg.shape[0]
    toks, width = tok.shape
    size = toks // row_count
    tm = rows * size
    pairs = width // (2 * HD)
    wide = gathered[0].shape[-1]
    full = lambda s: pl.BlockSpec(s, lambda i: (0,) * len(s))
    tile = lambda cols: pl.BlockSpec((tm, cols), lambda i: (i, 0))
    return pl.pallas_call(
        functools.partial(attn_forward_body, rows=rows),
        grid=(row_count // rows,),
        in_specs=[
            pl.BlockSpec(memory_space=pltpu.SMEM),
            tile(width),
            pl.BlockSpec((rows, 1, width), lambda i: (i, 0, 0)),
            pl.BlockSpec((rows, 1, size), lambda i: (i, 0, 0)),
        ]
        + [full(g.shape) for g in gathered],
        out_specs=[
            tile(width),
            tile(3 * width),
            pl.BlockSpec((rows, pairs, 2 * size, size), lambda i: (i, 0, 0, 0)),
            tile(width),
            tile(width),
            tile(width),
            full((width, wide)),
            full((8, width)),
            full((2, 2 * width)),
        ],
        out_shape=[
            jax.ShapeDtypeStruct((toks, width), BF16),
            jax.ShapeDtypeStruct((toks, 3 * width), BF16),
            jax.ShapeDtypeStruct((row_count, pairs, 2 * size, size), BF16),
            jax.ShapeDtypeStruct((toks, width), BF16),
            jax.ShapeDtypeStruct((toks, width), F32),
            jax.ShapeDtypeStruct((toks, width), BF16),
            jax.ShapeDtypeStruct((width, wide), BF16),
            jax.ShapeDtypeStruct((8, width), F32),
            jax.ShapeDtypeStruct((2, 2 * width), F32),
        ],
        compiler_params=pltpu.CompilerParams(vmem_limit_bytes=VMEM_LIMIT),
        cost_estimate=pl.CostEstimate(flops=16 * 10**9, bytes_accessed=20 * 10**6, transcendentals=2 * 10**6),
        name="attn_forward",
    )(place, tok, time, seg, *gathered)


def ffn_body(
    place, n2, cot, mine0, mine1, other0, other1, bfc, sum_out, sum_dn2, dbfc, keep, send, acc_out, acc_dn2, fc_s, out_s, act_s, dpre_s, *, tm, sub, half
):
    step = pl.program_id(0)

    @pl.when(step == 0)
    def _():
        acc_out[...] = jnp.zeros_like(acc_out)
        acc_dn2[...] = jnp.zeros_like(acc_dn2)

    gathered = (mine0, mine1, other0, other1)
    blocks, rows = 2, mine0.shape[-2]
    for z in range(Z):
        for y in range(Y):
            for x in range(X):
                both = pick(place, gathered, z, y, x, (step,))
                at = ((z * Y + y) * X + x) * CORES * rows
                fc_s[at : at + CORES * rows, :] = merge_rows(jnp.stack(both))
    for z in range(Z // blocks):
        for y in range(Y):
            for x in range(X):
                both = pick(place, gathered, step * (Z // blocks) + z, y, x, (slice(blocks, 2 * blocks),))
                at = ((z * Y + y) * X + x) * CORES * blocks * rows
                out_s[at : at + CORES * blocks * rows, :] = merge_rows(jnp.concatenate(both, axis=0))
    chunk = fc_s.shape[1]
    for part in range(chunk // sub):
        cols = slice(part * sub, (part + 1) * sub)
        bias = bfc[half : half + 1, cols]
        db = jnp.zeros_like(bias)
        for m in range(n2.shape[0] // tm):
            sl = slice(m * tm, (m + 1) * tm)
            pre = dot(n2[sl, :], fc_s[:, cols], 1, 0) + bias
            d_act = dot(cot[sl, :], out_s[cols, :], 1, 1)
            cdf = 0.5 * lax.erf(pre * math.sqrt(0.5)) + 0.5
            density = jnp.exp(pre * pre * -0.5) * (1.0 / math.sqrt(2.0 * math.pi))
            act = (pre * cdf).astype(BF16)
            d_pre = (d_act * (cdf + pre * density)).astype(BF16)
            act_s[sl, cols] = act
            dpre_s[sl, cols] = d_pre
            db = db + jnp.sum(d_pre.astype(F32), axis=0, keepdims=True)
            acc_out[sl, :] += dot(act, out_s[cols, :], 1, 0)
            acc_dn2[sl, :] += dot(d_pre, fc_s[:, cols], 1, 1)
        dbfc[:, cols] = db

    @pl.when(step == pl.num_programs(0) - 1)
    def _():
        sum_out[...] = acc_out[...].astype(BF16)
        sum_dn2[...] = acc_dn2[...].astype(BF16)

    grad = dot(act_s[...], cot[...], 0, 0)
    planes = Z // blocks
    for z in range(planes):
        for y in range(Y):
            for x in range(X):
                for b in range(blocks):
                    at = (((z * Y + y) * X + x) * CORES * blocks + b) * rows
                    even = grad[at : at + rows].astype(BF16)
                    odd = grad[at + blocks * rows : at + (blocks + 1) * rows].astype(BF16)
                    put_blocks(place, step * planes + z, y, x, even, odd, keep, send, (blocks + b,))
    grad = dot(n2[...], dpre_s[...], 0, 0)
    for z in range(Z):
        for y in range(Y):
            for x in range(X):
                at = ((z * Y + y) * X + x) * CORES * rows
                even = grad[at : at + rows].astype(BF16)
                odd = grad[at + rows : at + 2 * rows].astype(BF16)
                put_blocks(place, z, y, x, even, odd, keep, send, (step,))


def ffn(place, n2, cot, gathered, bfc, half, tm=512, sub=768):
    toks, width = n2.shape
    rows = width // PIECES
    blocks = 2
    count = 2 * blocks
    once = pl.Buffered(buffer_count=1)
    full = lambda s: pl.BlockSpec(s, lambda j: (0,) * len(s), pipeline_mode=once)
    whole = lambda s: pl.BlockSpec(s, lambda j: (0,) * len(s))
    parted = (Y, X, Z, count, rows, width)
    return pl.pallas_call(
        functools.partial(ffn_body, tm=tm, sub=sub, half=half),
        grid=(blocks,),
        in_specs=[
            pl.BlockSpec(memory_space=pltpu.SMEM),
            full((toks, width)),
            full((toks, width)),
        ]
        + [full(g.shape) for g in gathered]
        + [
            pl.BlockSpec((2, width), lambda j: (0, j)),
        ],
        out_specs=[
            whole((toks, width)),
            whole((toks, width)),
            pl.BlockSpec((1, width), lambda j: (0, j)),
            whole(parted),
            whole(parted),
        ],
        out_shape=[
            pltpu.HBM((toks, width), BF16),
            pltpu.HBM((toks, width), BF16),
            jax.ShapeDtypeStruct((1, blocks * width), F32),
            jax.ShapeDtypeStruct(parted, BF16),
            jax.ShapeDtypeStruct(parted, BF16),
        ],
        scratch_shapes=[
            pltpu.VMEM((toks, width), F32),
            pltpu.VMEM((toks, width), F32),
            pltpu.VMEM((width, width), BF16),
            pltpu.VMEM((width, width), BF16),
            pltpu.VMEM((toks, width), BF16),
            pltpu.VMEM((toks, width), BF16),
        ],
        compiler_params=pltpu.CompilerParams(vmem_limit_bytes=FFN_VMEM_LIMIT),
        cost_estimate=pl.CostEstimate(flops=15 * 10**9, bytes_accessed=20 * 10**6, transcendentals=3 * 10**6),
        name="ffn",
    )(place, n2, cot, *gathered, bfc)


def attn_backward_body(
    tok, time, hid, out0, out1, dn20, dn21, cot, qkv, probs, weights, vec, layer_out, dtok, dtime, dbr, dqkv, sums, *, rows
):
    width = hid.shape[1]
    size = hid.shape[0] // rows

    @pl.when(pl.program_id(0) == 0)
    def _():
        sums[...] = jnp.zeros_like(sums)

    hidden = hid[...]
    layer_out[...] = (hidden + (out0[...].astype(F32) + out1[...].astype(F32)) + vec[7:8, :]).astype(BF16)
    nhat, inv = normalise(hidden)
    dn2 = dn20[...].astype(F32) + dn21[...].astype(F32)
    cotangent = cot[...].astype(F32)
    q = dn2 * vec[5:6, :]
    mean_q = jnp.mean(q, axis=-1, keepdims=True)
    mean_qn = jnp.mean(q * nhat, axis=-1, keepdims=True)
    d_hidden = cotangent + (q - mean_q - nhat * mean_qn) * inv
    dtok[...] = d_hidden
    branch = d_hidden.astype(BF16)
    dbr[...] = branch
    sums[0:1, :] += colsum(dn2 * nhat)
    sums[1:2, :] += colsum(dn2)
    sums[2:3, :] += colsum(branch.astype(F32))
    sums[3:4, :] += colsum(cotangent)
    d_mixed = dot(branch, weights[:, 3 * width : 4 * width], 1, 1).astype(BF16)
    pairs = width // (2 * HD)
    for r in range(rows):
        sl = slice(r * size, (r + 1) * size)
        for p in range(pairs):
            c = 2 * HD * p
            qb = qkv[sl, c : c + 2 * HD] * jnp.asarray(HD**-0.5, BF16)
            k = head_pair(qkv[sl, width + c : width + c + 2 * HD])
            v = head_pair(qkv[sl, 2 * width + c : 2 * width + c + 2 * HD])
            dm = d_mixed[sl, c : c + 2 * HD]
            pr = probs[r, p]
            dp = dot(v, dm, 1, 1)
            halves = []
            for h in range(2):
                pf = pr[h * size : (h + 1) * size].astype(F32)
                dph = dp[h * size : (h + 1) * size]
                halves.append((pf * (dph - jnp.sum(dph * pf, axis=0, keepdims=True))).astype(BF16))
            ds = jnp.concatenate(halves, axis=0)
            dv = own_lanes(dot(pr, dm, 1, 0))
            dk = own_lanes(dot(ds, qb, 1, 0))
            dq = dot(ds, k, 0, 0) * HD**-0.5
            dqkv[sl, c : c + 2 * HD] = dq.astype(BF16)
            dqkv[sl, width + c : width + c + 2 * HD] = dk.astype(BF16)
            dqkv[sl, 2 * width + c : 2 * width + c + 2 * HD] = dv.astype(BF16)
    sums[4:5, :] += colsum(dqkv[:, :width].astype(F32))
    sums[5:6, :] += colsum(dqkv[:, 2 * width :].astype(F32))

    x = tok[...].astype(F32)
    x = jnp.concatenate(
        [x[r * size : (r + 1) * size] + time[r].astype(F32) for r in range(rows)], axis=0
    )
    nhat, inv = normalise(x)
    dn1 = dot(dqkv[...], weights[:, : 3 * width], 1, 1)
    sums[6:7, :] += colsum(dn1 * nhat)
    sums[7:8, :] += colsum(dn1)
    q = dn1 * vec[0:1, :]
    mean_q = jnp.mean(q, axis=-1, keepdims=True)
    mean_qn = jnp.mean(q * nhat, axis=-1, keepdims=True)
    d_tok = dtok[...] + (q - mean_q - nhat * mean_qn) * inv
    dtok[...] = d_tok
    for r in range(rows):
        dtime[r] = colsum(d_tok[r * size : (r + 1) * size])


def attn_backward(tok, time, hid, outs, dn2s, cot, qkv, probs, weights, vec, rows=2):
    row_count, pairs, _, size = probs.shape
    width = hid.shape[1]
    tm = rows * size
    toks = row_count * size
    steps = row_count // rows
    once = pl.Buffered(buffer_count=1)
    full = lambda s: pl.BlockSpec(s, lambda i: (0,) * len(s), pipeline_mode=once)
    tile = lambda cols: pl.BlockSpec((tm, cols), lambda i: (i, 0))
    per_row = pl.BlockSpec((rows, 1, width), lambda i: (i, 0, 0))
    return pl.pallas_call(
        functools.partial(attn_backward_body, rows=rows),
        grid=(steps,),
        in_specs=[tile(width), per_row]
        + [tile(width)] * 6
        + [
            tile(3 * width),
            pl.BlockSpec((rows, pairs, 2 * size, size), lambda i: (i, 0, 0, 0)),
            full(weights.shape),
            full(vec.shape),
        ],
        out_specs=[
            tile(width),
            tile(width),
            per_row,
            tile(width),
            tile(3 * width),
            pl.BlockSpec((8, width), lambda i: (0, 0)),
        ],
        out_shape=[
            jax.ShapeDtypeStruct((toks, width), BF16),
            jax.ShapeDtypeStruct((toks, width), F32),
            jax.ShapeDtypeStruct((row_count, 1, width), F32),
            jax.ShapeDtypeStruct((toks, width), BF16),
            jax.ShapeDtypeStruct((toks, 3 * width), BF16),
            jax.ShapeDtypeStruct((8, width), F32),
        ],
        compiler_params=pltpu.CompilerParams(vmem_limit_bytes=VMEM_LIMIT),
        cost_estimate=pl.CostEstimate(flops=6 * 10**9 * steps, bytes_accessed=10 * 10**6 * steps, transcendentals=0),
        name="attn_backward",
    )(tok, time, hid, *outs, *dn2s, cot, qkv, probs, weights, vec)


def collect(vectors, cut, stride, start, piece):
    at = start + piece * stride
    tile, shift = at // 128, at % 128
    lane = lax.broadcasted_iota(jnp.int32, (vectors.shape[0], 128), 1)
    block = vectors[:, tile * 128 : (tile + 1) * 128]
    if shift + cut > 128:
        block = jnp.where(lane >= shift, block, vectors[:, (tile + 1) * 128 : (tile + 2) * 128])
    if shift:
        block = pltpu.roll(block, 128 - shift, 1)
    return jnp.where(lane < cut, block, 0.0)


def weight_grad_body(place, n1, dqkv, att, dbr, sums, dbfc0, dbfc1, keep0, send0, keep1, send1):
    rows = keep0.shape[3]
    width = n1.shape[1]
    step = pl.program_id(0)

    def emit(grad, keep, send, at_column):
        tail = (slice(None), slice(at_column, at_column + grad.shape[1]))
        for z in range(Z):
            for y in range(Y):
                for x in range(X):
                    at = ((z * Y + y) * X + x) * CORES * rows
                    even = grad[at : at + rows].astype(BF16)
                    odd = grad[at + rows : at + 2 * rows].astype(BF16)
                    put_blocks(place, z, y, x, even, odd, keep, send, tail)

    for k in range(2):

        @pl.when(step == k)
        def _(k=k):
            emit(dot(n1[...], dqkv[...], 0, 0), keep0, send0, k * width)

    @pl.when(step == 2)
    def _():
        emit(dot(n1[...], dqkv[...], 0, 0), keep1, send1, 0)

    @pl.when(step == 3)
    def _():
        emit(dot(att[...], dbr[...], 0, 0), keep1, send1, width)
        vectors = sums[...]
        pad = jnp.zeros((6, dbfc0.shape[1]), F32)
        hidden = jnp.concatenate([dbfc0[...], dbfc1[...], pad], axis=0)

        def block(piece):
            early = collect(hidden, rows, 2 * rows, 0, piece)
            late = collect(hidden, rows, 2 * rows, rows, piece)
            top = collect(vectors, rows, rows, 0, piece)
            rest = [early[:2], late[:2], jnp.zeros((rows - 12, 128), F32)]
            return jnp.concatenate([top] + rest, axis=0).astype(BF16)

        tail = (slice(None), slice(2 * width, 2 * width + 128))
        for z in range(Z):
            for y in range(Y):
                for x in range(X):
                    piece = ((z * Y + y) * X + x) * CORES
                    put_blocks(place, z, y, x, block(piece), block(piece + 1), keep1, send1, tail)


def weight_grad(place, n1, dqkv, att, dbr, sums, dbfc0, dbfc1):
    toks, width = n1.shape
    rows = width // PIECES
    once = pl.Buffered(buffer_count=1)
    full = lambda a: pl.BlockSpec(a.shape, lambda j: (0, 0), pipeline_mode=once)
    shapes = [(Y, X, Z, rows, columns) for columns in (2 * width, 2 * width + 128) for _ in range(2)]
    return pl.pallas_call(
        weight_grad_body,
        grid=(4,),
        in_specs=[
            pl.BlockSpec(memory_space=pltpu.SMEM),
            full(n1),
            pl.BlockSpec((toks, width), lambda j: (0, jnp.minimum(j, 2))),
        ]
        + [full(e) for e in (att, dbr, sums, dbfc0, dbfc1)],
        out_specs=[pl.BlockSpec(shape, lambda j: (0,) * 5) for shape in shapes],
        out_shape=[jax.ShapeDtypeStruct(shape, BF16) for shape in shapes],
        compiler_params=pltpu.CompilerParams(vmem_limit_bytes=VMEM_LIMIT),
        cost_estimate=pl.CostEstimate(flops=5 * 10**9, bytes_accessed=16 * 10**6, transcendentals=0),
        name="weight_grad",
    )(place, n1, dqkv, att, dbr, sums, dbfc0, dbfc1)


def flip(position):
    return lambda i: i ^ position


def exchange(array, partner):
    return lax.ppermute(array, "dp", [(i, partner(i)) for i in range(PIECES)])


def plane_partner(stage):
    def partner(i):
        along_y = (i % 2 == 0) == (stage == "first")
        return i ^ (4 if along_y else 2)

    return partner


class CubeGather:
    def __init__(self, block):
        self.ready, self.came, self.parts = block, None, None

    def over_z(self, *steps):
        self.came = tuple(exchange(self.ready, flip(8 * k)) for k in steps)

    def over_plane(self, stage):
        self.came = (exchange(self.ready, plane_partner(stage)),)

    def take(self, axis=0):
        self.ready = jnp.stack((self.ready,) + tuple(self.came), axis=axis)

    def share(self):
        self.shared = exchange(self.ready, flip(1))

    def finish(self):
        self.parts = (self.ready, self.came[0], self.shared, exchange(self.came[0], flip(1)))


def meet(*things):
    return lax.optimization_barrier(things)


def total_body(*refs, scale, counts):
    outs = refs[7 * counts :]
    totals = []
    for k in range(counts):
        parts = [r[...].astype(F32) for r in refs[7 * k : 7 * k + 7]]
        totals.append(sum(parts[1:], parts[0]).reshape(parts[-1].shape) * scale)
    return totals, outs


def ffn_total_body(*refs, scale):
    totals, (d_fc, d_out) = total_body(*refs, scale=scale, counts=2)
    _, rows, width = totals[0].shape
    lane = lax.broadcasted_iota(jnp.int32, (rows, 128), 1)
    columns = [jnp.concatenate([t[0], t[1]], axis=1) for t in totals]
    for half, total in enumerate(totals):
        for b in range(2):
            at = (half * 2 + b) * rows
            d_out[at : at + rows, :] = total[2 + b]
    step = 2 * rows
    for t in range(4 * width // 128):
        tile = jnp.zeros((rows, 128), F32)
        for q in range(t * 128 // step, (t * 128 + 127) // step + 1):
            at, source = q * step - t * 128, (q // 2) * step
            first, shift = source // 128, source % 128
            block = columns[q % 2][:, first * 128 : (first + 1) * 128]
            if shift + step > 128:
                following = columns[q % 2][:, (first + 1) * 128 : (first + 2) * 128]
                block = jnp.where(lane >= shift, block, following)
            if (at - shift) % 128:
                block = pltpu.roll(block, (at - shift) % 128, 1)
            tile = jnp.where((lane >= at) & (lane < at + step), block, tile)
        d_fc[:, t * 128 : (t + 1) * 128] = tile


def attn_total_body(*refs, scale):
    (left, right), (d_qkv, d_proj, *vectors, hidden) = total_body(*refs, scale=scale, counts=2)
    width = d_proj.shape[1]
    d_qkv[:, : 2 * width] = left
    d_qkv[:, 2 * width :] = right[:, :width]
    d_proj[...] = right[:, width : 2 * width]
    own = vectors[0].shape[1]
    for v, out in enumerate(vectors):
        out[...] = right[v : v + 1, 2 * width : 2 * width + own]
    block = right[8:16, 2 * width : 2 * width + 128]
    block = jnp.where(lax.broadcasted_iota(jnp.int32, block.shape, 1) < own, block, 0.0)
    row = block[0:1]
    for k, v in enumerate((2, 1, 3), 1):
        row = row + pltpu.roll(block, k * own, 1)[v : v + 1]
    hidden[...] = row[:, : hidden.shape[1]]


def totals(body, sums, scale, shapes, name):
    pieces = [a for s in sums for a in (s.keep, s.came, s.first, s.second) + tuple(s.rest)]
    arrays = [a[0] if isinstance(a, tuple) else a for a in pieces]
    blocks = [s.rest[0].shape for s in sums for _ in range(7)]

    def spec(piece, block):
        array, index = piece if isinstance(piece, tuple) else (piece, 0)
        lead = len(array.shape) - len(block)
        at = (index,) + (0,) * (len(array.shape) - 1)
        return pl.BlockSpec((1,) * lead + tuple(block), lambda i: at)

    return pl.pallas_call(
        functools.partial(body, scale=scale),
        grid=(1,),
        in_specs=[spec(p, b) for p, b in zip(pieces, blocks)],
        out_shape=[jax.ShapeDtypeStruct(shape, F32) for shape in shapes],
        compiler_params=pltpu.CompilerParams(vmem_limit_bytes=VMEM_LIMIT),
        cost_estimate=pl.CostEstimate(flops=10**6, bytes_accessed=5 * 10**6, transcendentals=0),
        name=name,
    )(*arrays)


def over_z(block, k):
    return exchange(block, flip(8 * k))


class CubeSum:
    def __init__(self, keep, send):
        self.grads, self.keep, self.ahead = (keep, send), keep, send
        self.came, self.first, self.second, self.rest = None, None, None, None

    def part(self, *at):
        total = self.keep[at].astype(F32) + self.came[at].astype(F32)
        if self.first is not None:
            total = total + self.first[at[1:]].astype(F32)
        if self.second is not None:
            total = total + self.second[at[2:]].astype(F32)
        return total

    def send(self):
        if self.came is None:
            self.came = exchange(self.ahead, flip(1))
        elif self.first is None:
            self.ahead = self.part(1).astype(BF16)
            self.first = exchange(self.ahead, plane_partner("first"))
        elif self.second is None:
            self.ahead = self.part(0, 1).astype(BF16)
            self.second = exchange(self.ahead, plane_partner("second"))
        else:
            self.ahead = [self.part(0, 0, k).astype(BF16) for k in range(1, Z)]
            self.rest = [over_z(block, k) for k, block in enumerate(self.ahead, 1)]


def hold(first, *then):
    return tuple(lax.optimization_barrier((first, one))[1] for one in then)


def sum_over(values, *bits):
    for bit in bits:
        values = values + exchange(values, flip(bit))
    return values


def cut_any(blocks):
    every = blocks.reshape((Z, Y, X, CORES) + blocks.shape[1:])
    rest = tuple(range(3, every.ndim - 1))
    even = jnp.transpose(every[:, :, :, 0], (1, 2, 0) + rest)
    odd = jnp.transpose(every[:, :, :, 1], (2, 1, 0) + rest)
    return even[0], even[1], odd[0], odd[1]


def natural_blocks(keep, send):
    rest = tuple(range(3, keep.ndim))
    even = jnp.transpose(keep, (2, 0, 1) + rest)
    odd = jnp.transpose(send, (2, 1, 0) + rest)
    both = jnp.stack([even, odd], axis=3)
    return both.reshape((PIECES,) + both.shape[4:])


def on_device(
    tokens,
    segment_ids,
    time_embed,
    norm1_gain,
    norm1_shift,
    w_qkv,
    b_query,
    b_value,
    w_proj,
    b_proj,
    norm2_gain,
    norm2_shift,
    w_fc,
    b_fc,
    w_out,
    b_out,
    cotangent,
):
    row_count, row_len, width = tokens.shape
    toks = row_count * row_len
    devices = lax.axis_size("dp")
    cube = devices == PIECES
    rank = lax.axis_index("dp")
    grad_scale = 1.0 / math.sqrt(toks * devices)
    own = w_proj.shape[0]
    ratio = b_fc.shape[0] // own
    if cube:
        place = jnp.stack([rank // 8, (rank // 4) % 2, (rank // 2) % 2, rank % 2]).astype(jnp.int32)
    else:
        place = jnp.zeros((4,), jnp.int32)

    small = jnp.concatenate(
        [norm1_gain, norm1_shift, b_query, b_value, b_proj, norm2_gain, norm2_shift, b_out, b_fc]
    ).reshape(8 + ratio, own)
    order = list(range(8)) + [8 + 2 * h + k for k in range(ratio // 2) for h in range(2)]
    small = jnp.concatenate([small[v : v + 1] for v in order], axis=0)
    cut = width // PIECES
    halves = 2
    blocks = ratio // halves
    ffn_fc = lambda w: w.reshape(-1, PIECES, halves, blocks * cut).transpose(2, 0, 1, 3).reshape(halves, -1, blocks, width)
    if cube:
        ffn_block = jnp.concatenate(
            [ffn_fc(w_fc).transpose(0, 2, 1, 3), w_out.reshape(halves, blocks, own, width)], axis=1
        )
        small = jnp.pad(small, ((0, own - small.shape[0]), (0, 128 - own)))
        attn_gather = CubeGather(jnp.concatenate([w_qkv, w_proj, small], axis=1))
        early, late = CubeGather(ffn_block[0]), CubeGather(ffn_block[1])
        attn_gather.over_z(1, 2, 3)
        early.over_plane("second")
        late.over_plane("second")
        attn_gather.came, early.came, late.came = meet(attn_gather.came, early.came, late.came)
        attn_gather.take()
        early.take()
        late.take()
        attn_gather.over_plane("second")
        early.over_z(1, 3)
        attn_gather.came, early.came, late.ready = meet(attn_gather.came, early.came, late.ready)
        near = early.came
        attn_gather.take()
        attn_gather.over_plane("first")
        attn_gather.share()
        early.over_z(2)
        late.over_z(1, 2, 3)
        attn_gather.came, early.came = meet(attn_gather.came, early.came)
        attn_gather.finish()
        early.came = (near[0], early.came[0], near[1])
        early.take(axis=1)
        early.over_plane("first")
        early.share()
        attn_full = attn_gather.parts
    else:
        whole = lambda w: lax.all_gather(w, "dp", axis=0, tiled=True)
        natural = whole(small.T.reshape(own, -1))
        vectors = natural[:, :8].T
        hidden_bias = whole(b_fc).reshape(PIECES, ratio, cut)
        small = jnp.concatenate(
            [vectors.reshape(8, PIECES, cut).transpose(1, 0, 2), hidden_bias[:, jnp.array([0, 2, 1, 3])]], axis=1
        )
        small = jnp.pad(small, ((0, 0), (0, cut - small.shape[1]), (0, 128 - cut))).reshape(width, 128)
        attn_full = jnp.concatenate([whole(w_qkv), whole(w_proj), small], axis=1)
        attn_full = cut_any(attn_full.reshape(PIECES, cut, -1))
        fc_full = ffn_fc(whole(w_fc)).reshape(halves, PIECES, cut, blocks, width).transpose(1, 0, 3, 2, 4)
        out_full = whole(w_out).reshape(PIECES, halves, blocks, cut, width)
        ffn_full = jnp.concatenate([fc_full, out_full], axis=2)
        early, late = [cut_any(ffn_full[:, h].reshape(PIECES, -1, cut, width)) for h in range(halves)]

    flat = tokens.reshape(toks, width)
    times = time_embed.reshape(row_count, 1, width)
    segments = segment_ids.reshape(row_count, 1, row_len)
    cot = cotangent.reshape(toks, width)
    if cube:
        (segments,) = hold(early.ready, segments)
    n1, qkv, probs, att, hid, n2, attn_w, vec, bfc = attn_forward(place, flat, times, segments, attn_full)
    if cube:
        n2, early.came, early.shared, late.came = meet(n2, early.came, early.shared, late.came)
        early.finish()
        late.take(axis=1)
        late.over_plane("first")
        late.share()
        (n2,) = hold(late.ready, n2)
        early = early.parts
    out0, dn20, dbfc0, *grads0 = ffn(place, n2, cot, early, bfc, 0)
    sum0 = CubeSum(*grads0)
    if cube:
        out0, late.came, late.shared, sum0.ahead = meet(out0, late.came, late.shared, sum0.ahead)
        late.finish()
        sum0.send()
        sum0.send()
        (n2,) = hold(sum0.ahead, n2)
        late = late.parts
    out1, dn21, dbfc1, *grads1 = ffn(place, n2, cot, late, bfc, 1)
    sum1 = CubeSum(*grads1)
    if cube:
        out1, sum1.ahead, sum0.first = meet(out1, sum1.ahead, sum0.first)
        sum1.send()
        sum0.send()
        sum1.send()
        (hid,) = hold(sum1.ahead, *hold(sum0.ahead, hid))
    layer_out, d_tokens, d_time, dbr, dqkv, sums = attn_backward(
        flat, times, hid, (out0, out1), (dn20, dn21), cot, qkv, probs, attn_w, vec
    )
    if cube:
        dqkv, sum0.second, sum1.first = meet(dqkv, sum0.second, sum1.first)
        sum1.send()
        deep0 = [sum0.part(0, 0, k).astype(BF16) for k in (1, 3)]
        near0, wrap0 = over_z(deep0[0], 1), over_z(deep0[1], 3)
        (dqkv,) = hold(sum1.ahead, *hold(deep0[0], *hold(deep0[1], dqkv)))
    grads = weight_grad(place, n1, dqkv, att, dbr, sums, dbfc0, dbfc1)
    attn0, attn1 = CubeSum(*grads[:2]), CubeSum(*grads[2:])
    if cube:
        attn0.ahead, attn1.ahead, sum1.second, near0, wrap0 = meet(
            attn0.ahead, attn1.ahead, sum1.second, near0, wrap0
        )
        attn0.send()
        attn1.send()
        attn0.send()
        attn1.send()
        (sum1.second,) = hold(attn1.ahead, sum1.second)
        near1, wrap1 = [over_z(sum1.part(0, 0, k).astype(BF16), k) for k in (1, 3)]
        far = over_z(jnp.stack([s.part(0, 0, 2).astype(BF16) for s in (sum0, sum1)]), 2)
        sum0.rest = [near0, (far, 0), wrap0]
        sum1.rest = [near1, (far, 1), wrap1]
        attn0.send()
        for there in (attn0.second, near1, wrap1):
            (attn1.first,) = hold(there, attn1.first)
        attn1.send()
        attn0.send()
        own_fc, own_out = totals(
            ffn_total_body, (sum0, sum1), grad_scale, [(own, ratio * width), (ratio * own, width)], "ffn_total"
        )
        for there in (own_fc, attn0.rest[0], attn0.rest[2]):
            (attn1.second,) = hold(there, attn1.second)
        attn1.send()
        attn0.rest = hold(attn1.ahead[0], *attn0.rest)
        own_qkv, own_proj, *mine, own_bfc = totals(
            attn_total_body,
            (attn0, attn1),
            grad_scale,
            [(own, 3 * width), (own, width)] + [(1, own)] * 8 + [(1, ratio * own)],
            "attn_total",
        )
        mine, own_bfc = [v.reshape(own) for v in mine], own_bfc.reshape(ratio * own)
    else:
        scatter = lambda g: lax.psum_scatter(g, "dp", scatter_dimension=0, tiled=True)
        grads = jnp.concatenate([natural_blocks(*a.grads) for a in (attn0, attn1)], axis=-1).astype(F32)
        own_qkv = scatter(grads[:, :, : 3 * width].reshape(width, -1))
        own_proj = scatter(grads[:, :, 3 * width : 4 * width].reshape(width, -1))
        vectors = lax.psum(grads[:, :, 4 * width : 4 * width + cut], "dp")
        mine = lax.dynamic_slice(
            vectors[:, :8].transpose(1, 0, 2).reshape(8, width), (0, rank * own), (8, own)
        )
        hidden_grad = vectors[:, jnp.array([8, 10, 9, 11])].reshape(-1)
        own_bfc = lax.dynamic_slice(hidden_grad, (rank * own * ratio,), (own * ratio,))
        grads = jnp.stack([natural_blocks(*s.grads) for s in (sum0, sum1)], axis=1).astype(F32)
        out_grad = grads[:, :, blocks:].reshape(ratio * width, width)
        own_out = scatter(out_grad)
        fc_grad = grads[:, :, :blocks].transpose(0, 3, 1, 2, 4).reshape(width, halves, PIECES, blocks * cut)
        own_fc = scatter(fc_grad.transpose(0, 2, 1, 3).reshape(width, ratio * width))
        mine, own_bfc, own_qkv, own_proj, own_fc, own_out = [
            member * grad_scale for member in (mine, own_bfc, own_qkv, own_proj, own_fc, own_out)
        ]
    return (
        layer_out.reshape(tokens.shape),
        d_tokens.reshape(tokens.shape),
        d_time.reshape(time_embed.shape),
        mine[6],
        mine[7],
        own_qkv,
        mine[4],
        mine[5],
        own_proj,
        mine[2],
        mine[0],
        mine[1],
        own_fc,
        own_bfc,
        own_out,
        mine[3],
    )


def solution(mesh):
    in_specs = (
        P("dp", None, None),
        P("dp", None),
        P("dp", None),
        P("dp"),
        P("dp"),
        P("dp", None),
        P("dp"),
        P("dp"),
        P("dp", None),
        P("dp"),
        P("dp"),
        P("dp"),
        P("dp", None),
        P("dp"),
        P("dp", None),
        P("dp"),
        P("dp", None, None),
    )
    out_specs = (
        P("dp", None, None),
        P("dp", None, None),
        P("dp", None),
        P("dp"),
        P("dp"),
        P("dp", None),
        P("dp"),
        P("dp"),
        P("dp", None),
        P("dp"),
        P("dp"),
        P("dp"),
        P("dp", None),
        P("dp"),
        P("dp", None),
        P("dp"),
    )
    return jax.shard_map(
        on_device, mesh=mesh, in_specs=in_specs, out_specs=out_specs, check_vma=False
    )
```
